128 devices in a mesh: lo: 8 (over y, z_hi), hi: 16 (over x, z_lo, core).
Axes of the slice: x: 4, y: 4, z: 4 (z_hi: 2, z_lo: 2; z = z_hi * 2 + z_lo), core: 2. Of those that a mesh axis runs over, the one named last changes fastest.
Arguments:
- coefficients: float32 [2, 32, 8, 131072], P(None, None, None, ('lo', 'hi')), may hold values from -6 to 6
- angle_in: float32 [7, 64, 131072], P(None, None, ('lo', 'hi')), may hold values from -3.140625 to 3.140625
- angle_out: float32 [7, 32, 131072], P(None, None, ('lo', 'hi')), may hold values from -3.140625 to 3.140625
- interp: float32 [7, 32, 64], replicated, may hold values from -0.75 to 0.75
- destination: int32 [128, 1024], P(('lo', 'hi')), may hold values from 0 to 1023, each once within a row
Outputs:
- relaid: float32 [2, 32, 8, 131072], P(None, None, None, ('lo', 'hi'))
The draws below stay inside these ranges and needn't reach their ends.
All inputs are finite; a program needn't handle non-finite values.
Results may differ from the reference program's by a relative error of at most 0.0001.
Values sent between devices are 32-bit elements; how exact they have to be, the bound alone decides.
No kernel may reach another device: no remote copies, remote signals or barrier semaphores. Data moves between devices by JAX's collectives and lax.ppermute only.
A program may use at most 128 MiB of HBM per device.

```python
import jax
import jax.numpy as jnp
from jax import lax

R = 32
V = 8
K = 1024
LB_LO = 3
LB_HI = 4
LEVELS = 7
NDEV = 128
BOXES = 131072


def levels(rng, extent, pieces, least, top_value):
    level, own = 1.0, jax.random.fold_in(rng, 6)
    for axis_at, parts in pieces:
        steps = jnp.exp(jax.random.uniform(jax.random.fold_in(own, axis_at), (parts,), jnp.float32, least / len(pieces), top_value / len(pieces)))
        level = level * jnp.repeat(steps, extent[axis_at] // parts).reshape([-1 if axis == axis_at else 1 for axis in range(len(extent))])
    return level


def bell_draw(rng, dims, scale, reach, pieces=(), dtype=jnp.bfloat16):
    entries = jax.random.normal(rng, dims, jnp.float32) * scale
    if len(pieces) > 0:
        entries = levels(rng, dims, pieces, -0.22, 0.18) * entries
    return jnp.clip(entries, min=-reach, max=reach).astype(dtype)


def setup_inputs(seed: int = 0) -> dict:
    keys = jax.random.split(jax.random.key(seed), 6)
    coefficients = bell_draw(keys[0], (2, R, V, BOXES), 1.0, 6.0, ((3, 128),), jnp.float32)
    angle_in = jnp.clip(jax.random.uniform(keys[1], (LEVELS, 2 * R, BOXES), jnp.float32, -3.140625, 3.140625), -3.140625, 3.140625)
    angle_out = jnp.clip(jax.random.uniform(keys[2], (LEVELS, R, BOXES), jnp.float32, -3.140625, 3.140625), -3.140625, 3.140625)
    interp = bell_draw(keys[3], (LEVELS, R, 2 * R), (2 * R) ** -0.5, 0.75, (), jnp.float32)
    destination = jax.vmap(lambda own: jax.random.permutation(own, K))(jax.random.split(keys[4], NDEV)).reshape((NDEV, K)).astype(jnp.int32)
    return dict(coefficients=coefficients, angle_in=angle_in, angle_out=angle_out, interp=interp, destination=destination)


def rotate(real, imag, angle):
    cosine = jnp.cos(angle)
    sine = jnp.sin(angle)
    return real * cosine - imag * sine, real * sine + imag * cosine


def level_step(state, angle_in, angle_out, interp, position):
    ndev = state.shape[3]
    width = state.shape[4]
    half = width // 2
    stride = 2 ** position
    groups = ndev // (2 * stride)
    shaped = state.reshape(2, R, V, groups, 2, stride, width)
    low = shaped[:, :, :, :, 0]
    high = shaped[:, :, :, :, 1]
    phase_in = angle_in.reshape(2 * R, groups, 2, stride, width)
    phase_out = angle_out.reshape(R, groups, 2, stride, width)
    results = []
    for side in range(2):
        joined = jnp.concatenate([low[..., side * half:(side + 1) * half], high[..., side * half:(side + 1) * half]], axis=1)
        wide = jnp.repeat(joined, 2, axis=-1)
        angle = phase_in[:, :, side][:, None]
        yre, yim = rotate(wide[0], wide[1], angle)
        mapped = jnp.einsum("or,crvgsk->covgsk", interp, jnp.stack([yre, yim]), precision=lax.Precision.HIGHEST)
        zre, zim = rotate(mapped[0], mapped[1], phase_out[:, :, side][:, None])
        results.append(jnp.stack([zre, zim]))
    new_state = jnp.stack(results, axis=4)
    return new_state.reshape(2, R, V, ndev, width)


def reference(coefficients, angle_in, angle_out, interp, destination):
    state = coefficients.reshape(2, R, V, NDEV, K)
    step = 0
    for bit in range(LB_LO):
        state = level_step(state, angle_in[step].reshape(2 * R, NDEV, K), angle_out[step].reshape(R, NDEV, K), interp[step], LB_HI + bit)
        step = step + 1
    for bit in range(LB_HI):
        state = level_step(state, angle_in[step].reshape(2 * R, NDEV, K), angle_out[step].reshape(R, NDEV, K), interp[step], bit)
        step = step + 1
    index = jnp.broadcast_to(destination.astype(jnp.int32)[None, None, None], state.shape)
    taken = jnp.take_along_axis(state, index, axis=4)
    piece = K // NDEV
    moved = taken.reshape(2, R, V, NDEV, NDEV, piece)
    moved = jnp.swapaxes(moved, 3, 4)
    return moved.reshape(2, R, V, NDEV * K)
```

```python
import functools

import jax
import jax.numpy as jnp
from jax import lax
from jax.experimental import pallas as pl
from jax.experimental.pallas import tpu as pltpu
from jax.sharding import PartitionSpec as P

F32 = jnp.float32
BF16 = jnp.bfloat16
VMEM = pl.BlockSpec(memory_space=pltpu.VMEM)
SMEM = pl.BlockSpec(memory_space=pltpu.SMEM)

SIN = (
    0.9999996039252741,
    -0.1666655344642713,
    0.008332407591595805,
    -0.00019808739967677424,
    2.699822692004479e-06,
    -2.036622659870151e-08,
)
COS = (
    0.999999989116818,
    -0.49999989185961996,
    0.04166649020175043,
    -0.0013887807832168462,
    2.476996623505445e-05,
    -2.70797756302502e-07,
    1.724760753325688e-09,
)
MIB = 1024 * 1024


def params(mib):
    return pltpu.CompilerParams(vmem_limit_bytes=mib * MIB)


def rev(value, bits):
    out = 0
    for i in range(bits):
        out = out | ((value >> i & 1) << (bits - 1 - i))
    return out


def horner(coefs, u):
    acc = jnp.full_like(u, coefs[-1])
    for c in reversed(coefs[:-1]):
        acc = acc * u + c
    return acc


def sincos(x):
    u = x * x
    return x * horner(SIN, u), horner(COS, u)


def dot(a, b, dims=((1,), (0,))):
    return lax.dot_general(a, b, (dims, ((), ())), preferred_element_type=F32)


def split(x):
    hi = x.astype(BF16)
    return hi, (x - hi.astype(F32)).astype(BF16)


def send_kernel(nv, half, x_ref, out_ref, columns):
    for kt in range(8):
        columns[kt] = x_ref[:, kt * 128 : kt * 128 + 128]
        for c in range(2):
            for v in range(nv):
                start = c * 256 + half + v
                part = columns[kt, pl.ds(start, 128, stride=2), :]
                at = (c * nv + v) * 128
                out_ref[rev(kt, 3), :, at : at + 128] = part.T


def final_kernel(nv, *refs):
    out_ref, columns = refs[-2:]
    ncv = 2 * nv
    for kt in range(8):
        for half, x_ref in enumerate(refs[:-2]):
            for c in range(2):
                for v in range(nv):
                    cv = c * nv + v
                    part = x_ref[pl.ds(kt * 128 * ncv + cv, 128, stride=ncv), :]
                    start = c * 256 + half + v
                    columns[kt, pl.ds(start, 128, stride=2), :] = part.T
        out_ref[:, kt * 128 : kt * 128 + 128] = columns[kt]


def pack_kernel(pos_ref, ain, aout, y1, y2, y3, x01, x02, x03, z0, z1, z2, z3):
    y = pos_ref[0]
    x = pos_ref[1]
    z = pos_ref[2]

    def put(dst, at, level, chunk, width):
        start = pl.multiple_of(chunk * width, width)
        dst[0:64, at : at + width] = ain[level, :, pl.ds(start, width)]
        dst[64:96, at : at + width] = aout[level, :, pl.ds(start, width)]

    ry = rev(y, 2)
    rx = rev(x, 2)
    for m, dst in ((1, y1), (2, y2), (3, y3)):
        put(dst, 0, 0, ry ^ rev(m, 2), 256)
    put(y2, 256, 1, (y >> 1) ^ 1, 512)
    for m, dst in ((1, x01), (2, x02), (3, x03)):
        put(dst, 0, 3, z * 4 + (rx ^ rev(m, 2)), 128)
        put(dst, 128, 4, rx ^ rev(m, 2), 256)
    put(x02, 384, 5, (x >> 1) ^ 1, 512)
    for m, dst in enumerate((z0, z1, z2, z3)):
        put(dst, 0, 3, (1 - z) * 4 + (rx ^ rev(m, 2)), 128)


def turned(parts, scratch, width):
    a, b = parts
    for t in range(width // 128):
        s = slice(t * 128, t * 128 + 128)
        full = jnp.concatenate([a(s), b(s), jnp.zeros((32, 128), F32)], axis=0)
        scratch[s, :] = full.T


def own(ain, aout, level, chunk, width):
    def read(ref, rows):
        def go(s):
            start = chunk * width + s.start
            return ref[level, 0:rows, pl.ds(pl.multiple_of(start, 128), 128)]

        return go

    return read(ain, 64), read(aout, 32)


def got(ref, at):
    return (
        lambda s: ref[0:64, at + s.start : at + s.stop],
        lambda s: ref[64:96, at + s.start : at + s.stop],
    )


def weights(interp_ref, w_ref, count):
    row = lax.broadcasted_iota(jnp.int32, (256, 64), 0)
    col = lax.broadcasted_iota(jnp.int32, (256, 64), 1)
    left = ((row >> 2) == col).astype(F32).astype(BF16)
    row = lax.broadcasted_iota(jnp.int32, (32, 128), 0)
    col = lax.broadcasted_iota(jnp.int32, (32, 128), 1)
    right = (row == (col >> 2)).astype(F32).astype(BF16)
    row = lax.broadcasted_iota(jnp.int32, (256, 128), 0)
    col = lax.broadcasted_iota(jnp.int32, (256, 128), 1)
    keep = (row & 3) == (col & 3)
    for level in range(count):
        for i, part in enumerate(split(interp_ref[level])):
            mid = dot(left, part, ((1,), (1,))).astype(BF16)
            full = jnp.where(keep, dot(mid, right), 0.0)
            w_ref[level, :, i * 128 : i * 128 + 128] = full.astype(BF16)


def table_lo_kernel(pos_ref, ain, aout, interp, y1, y2, y3, cos_ref, sin_ref, w_ref, scratch):
    y = pos_ref[0]
    ry = rev(y, 2)
    weights(interp, w_ref, 3)

    def emit(level, base, rows, ts):
        for t in range(ts):
            s, c = sincos(scratch[pl.ds(t, 128, stride=ts), :])
            at = pl.multiple_of((base + t) * 128, 128)
            cos_ref[level, pl.ds(at, 128), :] = c
            sin_ref[level, pl.ds(at, 128), :] = s

    for m, src in ((0, None), (1, y1), (2, y2), (3, y3)):
        parts = own(ain, aout, 0, ry, 256) if src is None else got(src, 0)
        turned(parts, scratch, 256)
        emit(0, (ry ^ rev(m, 2)) * 2, 256, 2)
    turned(own(ain, aout, 1, y >> 1, 512), scratch, 512)
    emit(1, (y >> 1) * 4, 512, 4)
    turned(got(y2, 256), scratch, 512)
    emit(1, (1 - (y >> 1)) * 4, 512, 4)
    turned(own(ain, aout, 2, 0, 1024), scratch, 1024)
    emit(2, 0, 1024, 8)


def table_hi_kernel(
    pos_ref, ain, aout, interp, x01, x02, x03, z0, z1, z2, z3, cos_ref, sin_ref, w_ref, scratch
):
    x = pos_ref[1]
    z = pos_ref[2]
    rx = rev(x, 2)
    weights(interp, w_ref, 4)

    def emit(level, base, ts):
        for t in range(ts):
            rows = [scratch[pl.ds(T * ts + t, 8, stride=8 * ts), :] for T in range(8)]
            s, c = sincos(jnp.concatenate(rows, axis=0))
            at = pl.multiple_of((base + t) * 64, 64)
            cos_ref[level, pl.ds(at, 64), :] = c
            sin_ref[level, pl.ds(at, 64), :] = s

    zs = (z0, z1, z2, z3)
    xs = (None, x01, x02, x03)
    for mz in range(2):
        for m in range(4):
            if mz == 0 and m == 0:
                parts = own(ain, aout, 0, z * 4 + rx, 128)
            else:
                parts = got(zs[m], 0) if mz else got(xs[m], 0)
            turned(parts, scratch, 128)
            emit(0, ((z ^ mz) * 4 + (rx ^ rev(m, 2))) * 2, 2)
    for m in range(4):
        parts = own(ain, aout, 1, rx, 256) if m == 0 else got(xs[m], 128)
        turned(parts, scratch, 256)
        emit(1, (rx ^ rev(m, 2)) * 4, 4)
    turned(own(ain, aout, 2, x >> 1, 512), scratch, 512)
    emit(2, (x >> 1) * 8, 8)
    turned(got(x02, 384), scratch, 512)
    emit(2, (1 - (x >> 1)) * 8, 8)
    turned(own(ain, aout, 3, 0, 1024), scratch, 1024)
    emit(3, 0, 16)


def spread(table, kind):
    lane = lax.broadcasted_iota(jnp.int32, table.shape, 1)
    return jnp.take_along_axis(table, kind * 32 + (lane >> 2), axis=1)


def step(nv, low, high, cos, sin, w):
    n = cos.shape[0]
    reals, imags = [], []
    sides = []
    for kind, src in enumerate((low, high)):
        c = spread(cos, kind)
        s = spread(sin, kind)
        re, im = [], []
        for v in range(nv):
            xr = src(v)
            xi = src(nv + v)
            re.append(xr * c - xi * s)
            im.append(xr * s + xi * c)
        sides.append(jnp.concatenate(re + im, axis=0))
    hi, lo = split(jnp.concatenate(sides, axis=1))
    first = dot(hi, w)
    out = first[:, :128] + first[:, 128:] + dot(lo, w[:, :128])
    c = spread(cos, 2)
    s = spread(sin, 2)
    re, im = [], []
    for v in range(nv):
        mr = out[v * n : v * n + n]
        mi = out[(nv + v) * n : (nv + v) * n + n]
        re.append(mr * c - mi * s)
        im.append(mr * s + mi * c)
    return re + im


def run_level(nv, level, count, rows, load_low, load_high, store, cos_ref, sin_ref, w_ref):
    group = 128 // rows
    w = w_ref[level]

    def body(i, _):
        for t in range(2):
            at = [
                pl.multiple_of((2 * (i * group + g) + t) * rows, rows) for g in range(group)
            ]
            c = jnp.concatenate([cos_ref[level, pl.ds(a, rows), :] for a in at], axis=0)
            s = jnp.concatenate([sin_ref[level, pl.ds(a, rows), :] for a in at], axis=0)
            low = lambda q: jnp.concatenate(
                [load_low(i * group + g, q) for g in range(group)], axis=0
            )
            high = lambda q: jnp.concatenate(
                [load_high(i * group + g, q) for g in range(group)], axis=0
            )
            for q, tile in enumerate(step(nv, low, high, c, s, w)):
                for g in range(group):
                    store(2 * (i * group + g) + t, q, tile[g * rows : g * rows + rows])
        return 0

    lax.fori_loop(0, count // group, body, 0)


def levels_lo_kernel(nv, x_ref, cos_ref, sin_ref, w_ref, out_ref, one, two):
    lanes = lambda q: slice(q * 128, q * 128 + 128)

    def keep(ref):
        def store(slab, q, tile):
            ref[slab, :, lanes(q)] = tile

        return store

    def last(slab, q, tile):
        for kp in range(16):
            out_ref[rev(kp, 4), pl.ds(pl.multiple_of(slab * 8, 8), 8), lanes(q)] = tile[
                kp * 8 : kp * 8 + 8
            ]

    run = functools.partial(run_level, nv)
    run(
        0, 4, 128,
        lambda m, q: x_ref[rev(m, 2) * 2, :, lanes(q)],
        lambda m, q: x_ref[rev(m, 2) * 2 + 1, :, lanes(q)],
        keep(one), cos_ref, sin_ref, w_ref,
    )
    run(
        1, 4, 128,
        lambda m, q: one[m, :, lanes(q)],
        lambda m, q: one[m + 4, :, lanes(q)],
        keep(two), cos_ref, sin_ref, w_ref,
    )
    run(
        2, 4, 128,
        lambda m, q: two[m, :, lanes(q)],
        lambda m, q: two[m + 4, :, lanes(q)],
        last, cos_ref, sin_ref, w_ref,
    )


def levels_hi_kernel(nv, where_ref, x_ref, cos_ref, sin_ref, w_ref, out_ref, one, two, last):
    lanes = lambda q: slice(q * 128, q * 128 + 128)
    ncv = 2 * nv

    def keep(ref):
        def store(slab, q, tile):
            ref[slab, :, lanes(q)] = tile

        return store

    def put(slab, q, tile):
        last[pl.ds(pl.multiple_of(slab * 64, 64), 64), q, :] = tile

    run = functools.partial(run_level, nv)
    run(
        0, 8, 64,
        lambda m, q: x_ref[rev(m, 3) * 2, :, lanes(q)],
        lambda m, q: x_ref[rev(m, 3) * 2 + 1, :, lanes(q)],
        keep(one), cos_ref, sin_ref, w_ref,
    )
    for level, src, store in ((1, one, keep(two)), (2, two, keep(one)), (3, one, put)):
        run(
            level, 8, 64,
            lambda m, q, src=src: src[m, :, lanes(q)],
            lambda m, q, src=src: src[m + 8, :, lanes(q)],
            store, cos_ref, sin_ref, w_ref,
        )

    def gather(e, _):
        for r in range(8):
            out_ref[e, r * ncv : r * ncv + ncv, :] = last[where_ref[e * 8 + r]]
        return 0

    lax.fori_loop(0, 128, gather, 0)


def shards(coefficients, angle_in, angle_out, interp, destination):
    nv = 2
    ncv = 2 * nv
    a = lax.axis_index("lo")
    c = lax.axis_index("hi")
    pos = jnp.stack([a >> 1, c >> 2, c >> 1 & 1]).astype(jnp.int32)
    shape = jax.ShapeDtypeStruct

    sends = pl.pallas_call(
        pack_kernel,
        out_shape=[shape((96, w), F32) for w in (256, 768, 256, 384, 896, 384, 128, 128, 128, 128)],
        in_specs=[SMEM, VMEM, VMEM],
        out_specs=[VMEM] * 10,
        compiler_params=params(24),
    )(pos, angle_in, angle_out)
    moved = []
    for m, s in zip((1, 2, 3), sends[:3]):
        moved.append(lax.ppermute(s, "lo", [(i, i ^ (2 * m)) for i in range(8)]))
    for m, s in zip((1, 2, 3), sends[3:6]):
        moved.append(lax.ppermute(s, "hi", [(i, i ^ (4 * m)) for i in range(16)]))
    for m, s in enumerate(sends[6:]):
        moved.append(lax.ppermute(s, "hi", [(i, i ^ (4 * m + 2)) for i in range(16)]))

    state = pl.pallas_call(
        functools.partial(send_kernel, nv, 0),
        out_shape=shape((8, 128, ncv * 128), F32),
        in_specs=[VMEM],
        out_specs=VMEM,
        scratch_shapes=[pltpu.VMEM((8, 512, 128), F32)],
        compiler_params=params(16),
    )(coefficients.reshape(512, 1024))
    state = lax.all_to_all(state, "lo", 0, 0, tiled=True)

    cos_lo, sin_lo, w_lo = pl.pallas_call(
        table_lo_kernel,
        out_shape=[shape((3, 1024, 128), F32)] * 2 + [shape((3, 256, 256), BF16)],
        in_specs=[SMEM] + [VMEM] * 6,
        out_specs=[VMEM] * 3,
        scratch_shapes=[pltpu.VMEM((1024, 128), F32)],
        compiler_params=params(24),
    )(pos, angle_in[:3], angle_out[:3], interp[:3], *moved[:3])
    cos_hi, sin_hi, w_hi = pl.pallas_call(
        table_hi_kernel,
        out_shape=[shape((4, 1024, 128), F32)] * 2 + [shape((4, 256, 256), BF16)],
        in_specs=[SMEM] + [VMEM] * 10,
        out_specs=[VMEM] * 3,
        scratch_shapes=[pltpu.VMEM((1024, 128), F32)],
        compiler_params=params(24),
    )(pos, angle_in[3:], angle_out[3:], interp[3:], *moved[3:])

    state = pl.pallas_call(
        functools.partial(levels_lo_kernel, nv),
        out_shape=shape((16, 64, ncv * 128), F32),
        in_specs=[VMEM] * 4,
        out_specs=VMEM,
        scratch_shapes=[pltpu.VMEM((8, 128, ncv * 128), F32)] * 2,
        compiler_params=params(32),
    )(state, cos_lo, sin_lo, w_lo)
    state = lax.all_to_all(state, "hi", 0, 0, tiled=True)

    wanted = destination[0]
    where = (wanted & 15) * 64 + (wanted >> 4 & 7) * 8 + (wanted >> 7)
    state = pl.pallas_call(
        functools.partial(levels_hi_kernel, nv),
        out_shape=shape((128, 8 * ncv, 128), F32),
        in_specs=[SMEM] + [VMEM] * 4,
        out_specs=VMEM,
        scratch_shapes=[pltpu.VMEM((16, 64, ncv * 128), F32)] * 2
        + [pltpu.VMEM((1024, ncv, 128), F32)],
        compiler_params=params(32),
    )(where, state, cos_hi, sin_hi, w_hi)
    state = lax.all_to_all(state, ("lo", "hi"), 0, 0, tiled=True)

    out = pl.pallas_call(
        functools.partial(final_kernel, nv),
        out_shape=shape((512, 1024), F32),
        in_specs=[VMEM],
        out_specs=VMEM,
        scratch_shapes=[pltpu.VMEM((8, 512, 128), F32)],
        compiler_params=params(16),
    )(state.reshape(1024 * ncv, 128))
    return out.reshape(2, 32, 8, 1024)


def solution(mesh):
    placed = (
        P(None, None, None, ("lo", "hi")),
        P(None, None, ("lo", "hi")),
        P(None, None, ("lo", "hi")),
        P(),
        P(("lo", "hi"), None),
    )
    return jax.shard_map(
        shards,
        mesh=mesh,
        in_specs=placed,
        out_specs=P(None, None, None, ("lo", "hi")),
        check_vma=False,
    )
```

```python
import functools

import jax
import jax.numpy as jnp
from jax import lax
from jax.experimental import pallas as pl
from jax.experimental.pallas import tpu as pltpu
from jax.sharding import PartitionSpec as P

F32 = jnp.float32
BF16 = jnp.bfloat16
VMEM = pl.BlockSpec(memory_space=pltpu.VMEM)
SMEM = pl.BlockSpec(memory_space=pltpu.SMEM)

SIN = (
    0.9999996039252741,
    -0.1666655344642713,
    0.008332407591595805,
    -0.00019808739967677424,
    2.699822692004479e-06,
    -2.036622659870151e-08,
)
COS = (
    0.999999989116818,
    -0.49999989185961996,
    0.04166649020175043,
    -0.0013887807832168462,
    2.476996623505445e-05,
    -2.70797756302502e-07,
    1.724760753325688e-09,
)
MIB = 1024 * 1024


def params(mib):
    return pltpu.CompilerParams(vmem_limit_bytes=mib * MIB)


def rev(value, bits):
    out = 0
    for i in range(bits):
        out = out | ((value >> i & 1) << (bits - 1 - i))
    return out


def horner(coefs, u):
    acc = jnp.full_like(u, coefs[-1])
    for c in reversed(coefs[:-1]):
        acc = acc * u + c
    return acc


def sincos(x):
    u = x * x
    return x * horner(SIN, u), horner(COS, u)


def dot(a, b, dims=((1,), (0,))):
    return lax.dot_general(a, b, (dims, ((), ())), preferred_element_type=F32)


def split(x):
    hi = x.astype(BF16)
    return hi, (x - hi.astype(F32)).astype(BF16)


def send_kernel(nv, half, x_ref, out_ref, columns):
    for kt in range(8):
        columns[kt] = x_ref[:, kt * 128 : kt * 128 + 128]
        for c in range(2):
            for v in range(nv):
                start = c * 256 + half + v
                part = columns[kt, pl.ds(start, 128, stride=2), :]
                at = (c * nv + v) * 128
                out_ref[rev(kt, 3), :, at : at + 128] = part.T


def final_kernel(nv, *refs):
    out_ref, columns = refs[-2:]
    ncv = 2 * nv
    for kt in range(8):
        for half, x_ref in enumerate(refs[:-2]):
            for c in range(2):
                for v in range(nv):
                    cv = c * nv + v
                    part = x_ref[pl.ds(kt * 128 * ncv + cv, 128, stride=ncv), :]
                    start = c * 256 + half + v
                    columns[kt, pl.ds(start, 128, stride=2), :] = part.T
        out_ref[:, kt * 128 : kt * 128 + 128] = columns[kt]


def pack_kernel(pos_ref, ain, aout, y1, y2, y3, x01, x02, x03, z0, z1, z2, z3):
    y = pos_ref[0]
    x = pos_ref[1]
    z = pos_ref[2]

    def put(dst, at, level, chunk, width):
        start = pl.multiple_of(chunk * width, width)
        dst[0:64, at : at + width] = ain[level, :, pl.ds(start, width)]
        dst[64:96, at : at + width] = aout[level, :, pl.ds(start, width)]

    ry = rev(y, 2)
    rx = rev(x, 2)
    for m, dst in ((1, y1), (2, y2), (3, y3)):
        put(dst, 0, 0, ry ^ rev(m, 2), 256)
    put(y2, 256, 1, (y >> 1) ^ 1, 512)
    for m, dst in ((1, x01), (2, x02), (3, x03)):
        put(dst, 0, 3, z * 4 + (rx ^ rev(m, 2)), 128)
        put(dst, 128, 4, rx ^ rev(m, 2), 256)
    put(x02, 384, 5, (x >> 1) ^ 1, 512)
    for m, dst in enumerate((z0, z1, z2, z3)):
        put(dst, 0, 3, (1 - z) * 4 + (rx ^ rev(m, 2)), 128)


def turned(parts, scratch, width):
    a, b = parts
    for t in range(width // 128):
        s = slice(t * 128, t * 128 + 128)
        full = jnp.concatenate([a(s), b(s), jnp.zeros((32, 128), F32)], axis=0)
        scratch[s, :] = full.T


def own(ain, aout, level, chunk, width):
    def read(ref, rows):
        def go(s):
            start = chunk * width + s.start
            return ref[level, 0:rows, pl.ds(pl.multiple_of(start, 128), 128)]

        return go

    return read(ain, 64), read(aout, 32)


def got(ref, at):
    return (
        lambda s: ref[0:64, at + s.start : at + s.stop],
        lambda s: ref[64:96, at + s.start : at + s.stop],
    )


def weights(interp_ref, w_ref, count):
    row = lax.broadcasted_iota(jnp.int32, (256, 64), 0)
    col = lax.broadcasted_iota(jnp.int32, (256, 64), 1)
    left = ((row >> 2) == col).astype(F32).astype(BF16)
    row = lax.broadcasted_iota(jnp.int32, (32, 128), 0)
    col = lax.broadcasted_iota(jnp.int32, (32, 128), 1)
    right = (row == (col >> 2)).astype(F32).astype(BF16)
    row = lax.broadcasted_iota(jnp.int32, (256, 128), 0)
    col = lax.broadcasted_iota(jnp.int32, (256, 128), 1)
    keep = (row & 3) == (col & 3)
    for level in range(count):
        for i, part in enumerate(split(interp_ref[level])):
            mid = dot(left, part, ((1,), (1,))).astype(BF16)
            full = jnp.where(keep, dot(mid, right), 0.0)
            w_ref[level, :, i * 128 : i * 128 + 128] = full.astype(BF16)


def table_lo_kernel(pos_ref, ain, aout, interp, y1, y2, y3, cos_ref, sin_ref, w_ref, scratch):
    y = pos_ref[0]
    ry = rev(y, 2)
    weights(interp, w_ref, 3)

    def emit(level, base, rows, ts):
        for t in range(ts):
            s, c = sincos(scratch[pl.ds(t, 128, stride=ts), :])
            at = pl.multiple_of((base + t) * 128, 128)
            cos_ref[level, pl.ds(at, 128), :] = c
            sin_ref[level, pl.ds(at, 128), :] = s

    for m, src in ((0, None), (1, y1), (2, y2), (3, y3)):
        parts = own(ain, aout, 0, ry, 256) if src is None else got(src, 0)
        turned(parts, scratch, 256)
        emit(0, (ry ^ rev(m, 2)) * 2, 256, 2)
    turned(own(ain, aout, 1, y >> 1, 512), scratch, 512)
    emit(1, (y >> 1) * 4, 512, 4)
    turned(got(y2, 256), scratch, 512)
    emit(1, (1 - (y >> 1)) * 4, 512, 4)
    turned(own(ain, aout, 2, 0, 1024), scratch, 1024)
    emit(2, 0, 1024, 8)


def table_hi_kernel(
    pos_ref, ain, aout, interp, x01, x02, x03, z0, z1, z2, z3, cos_ref, sin_ref, w_ref, scratch
):
    x = pos_ref[1]
    z = pos_ref[2]
    rx = rev(x, 2)
    weights(interp, w_ref, 4)

    def emit(level, base, ts):
        for t in range(ts):
            rows = [scratch[pl.ds(T * ts + t, 8, stride=8 * ts), :] for T in range(8)]
            s, c = sincos(jnp.concatenate(rows, axis=0))
            at = pl.multiple_of((base + t) * 64, 64)
            cos_ref[level, pl.ds(at, 64), :] = c
            sin_ref[level, pl.ds(at, 64), :] = s

    zs = (z0, z1, z2, z3)
    xs = (None, x01, x02, x03)
    for mz in range(2):
        for m in range(4):
            if mz == 0 and m == 0:
                parts = own(ain, aout, 0, z * 4 + rx, 128)
            else:
                parts = got(zs[m], 0) if mz else got(xs[m], 0)
            turned(parts, scratch, 128)
            emit(0, ((z ^ mz) * 4 + (rx ^ rev(m, 2))) * 2, 2)
    for m in range(4):
        parts = own(ain, aout, 1, rx, 256) if m == 0 else got(xs[m], 128)
        turned(parts, scratch, 256)
        emit(1, (rx ^ rev(m, 2)) * 4, 4)
    turned(own(ain, aout, 2, x >> 1, 512), scratch, 512)
    emit(2, (x >> 1) * 8, 8)
    turned(got(x02, 384), scratch, 512)
    emit(2, (1 - (x >> 1)) * 8, 8)
    turned(own(ain, aout, 3, 0, 1024), scratch, 1024)
    emit(3, 0, 16)


def spread(table, kind):
    lane = lax.broadcasted_iota(jnp.int32, table.shape, 1)
    return jnp.take_along_axis(table, kind * 32 + (lane >> 2), axis=1)


def step(nv, low, high, cos, sin, w):
    n = cos.shape[0]
    reals, imags = [], []
    sides = []
    for kind, src in enumerate((low, high)):
        c = spread(cos, kind)
        s = spread(sin, kind)
        re, im = [], []
        for v in range(nv):
            xr = src(v)
            xi = src(nv + v)
            re.append(xr * c - xi * s)
            im.append(xr * s + xi * c)
        sides.append(jnp.concatenate(re + im, axis=0))
    hi, lo = split(jnp.concatenate(sides, axis=1))
    first = dot(hi, w)
    out = first[:, :128] + first[:, 128:] + dot(lo, w[:, :128])
    c = spread(cos, 2)
    s = spread(sin, 2)
    re, im = [], []
    for v in range(nv):
        mr = out[v * n : v * n + n]
        mi = out[(nv + v) * n : (nv + v) * n + n]
        re.append(mr * c - mi * s)
        im.append(mr * s + mi * c)
    return re + im


def run_level(nv, level, count, rows, load_low, load_high, store, cos_ref, sin_ref, w_ref):
    group = 128 // rows
    w = w_ref[level]

    def body(i, _):
        for t in range(2):
            at = [
                pl.multiple_of((2 * (i * group + g) + t) * rows, rows) for g in range(group)
            ]
            c = jnp.concatenate([cos_ref[level, pl.ds(a, rows), :] for a in at], axis=0)
            s = jnp.concatenate([sin_ref[level, pl.ds(a, rows), :] for a in at], axis=0)
            low = lambda q: jnp.concatenate(
                [load_low(i * group + g, q) for g in range(group)], axis=0
            )
            high = lambda q: jnp.concatenate(
                [load_high(i * group + g, q) for g in range(group)], axis=0
            )
            for q, tile in enumerate(step(nv, low, high, c, s, w)):
                for g in range(group):
                    store(2 * (i * group + g) + t, q, tile[g * rows : g * rows + rows])
        return 0

    lax.fori_loop(0, count // group, body, 0)


def levels_lo_kernel(nv, x_ref, cos_ref, sin_ref, w_ref, out_ref, one, two):
    lanes = lambda q: slice(q * 128, q * 128 + 128)

    def keep(ref):
        def store(slab, q, tile):
            ref[slab, :, lanes(q)] = tile

        return store

    def last(slab, q, tile):
        for kp in range(16):
            out_ref[rev(kp, 4), pl.ds(pl.multiple_of(slab * 8, 8), 8), lanes(q)] = tile[
                kp * 8 : kp * 8 + 8
            ]

    run = functools.partial(run_level, nv)
    run(
        0, 4, 128,
        lambda m, q: x_ref[rev(m, 2) * 2, :, lanes(q)],
        lambda m, q: x_ref[rev(m, 2) * 2 + 1, :, lanes(q)],
        keep(one), cos_ref, sin_ref, w_ref,
    )
    run(
        1, 4, 128,
        lambda m, q: one[m, :, lanes(q)],
        lambda m, q: one[m + 4, :, lanes(q)],
        keep(two), cos_ref, sin_ref, w_ref,
    )
    run(
        2, 4, 128,
        lambda m, q: two[m, :, lanes(q)],
        lambda m, q: two[m + 4, :, lanes(q)],
        last, cos_ref, sin_ref, w_ref,
    )


def levels_hi_kernel(nv, where_ref, x_ref, cos_ref, sin_ref, w_ref, out_ref, one, two, last):
    lanes = lambda q: slice(q * 128, q * 128 + 128)
    ncv = 2 * nv

    def keep(ref):
        def store(slab, q, tile):
            ref[slab, :, lanes(q)] = tile

        return store

    def put(slab, q, tile):
        last[pl.ds(pl.multiple_of(slab * 64, 64), 64), q, :] = tile

    run = functools.partial(run_level, nv)
    run(
        0, 8, 64,
        lambda m, q: x_ref[rev(m, 3) * 2, :, lanes(q)],
        lambda m, q: x_ref[rev(m, 3) * 2 + 1, :, lanes(q)],
        keep(one), cos_ref, sin_ref, w_ref,
    )
    for level, src, store in ((1, one, keep(two)), (2, two, keep(one)), (3, one, put)):
        run(
            level, 8, 64,
            lambda m, q, src=src: src[m, :, lanes(q)],
            lambda m, q, src=src: src[m + 8, :, lanes(q)],
            store, cos_ref, sin_ref, w_ref,
        )

    def gather(e, _):
        for r in range(8):
            out_ref[e, r * ncv : r * ncv + ncv, :] = last[where_ref[e * 8 + r]]
        return 0

    lax.fori_loop(0, 128, gather, 0)


def shards(coefficients, angle_in, angle_out, interp, destination):
    nv = 2
    ncv = 2 * nv
    a = lax.axis_index("lo")
    c = lax.axis_index("hi")
    pos = jnp.stack([a >> 1, c >> 2, c >> 1 & 1]).astype(jnp.int32)
    shape = jax.ShapeDtypeStruct

    sends = pl.pallas_call(
        pack_kernel,
        out_shape=[shape((96, w), F32) for w in (256, 768, 256, 384, 896, 384, 128, 128, 128, 128)],
        in_specs=[SMEM, VMEM, VMEM],
        out_specs=[VMEM] * 10,
        compiler_params=params(4),
    )(pos, angle_in, angle_out)
    moved = []
    for m, s in zip((1, 2, 3), sends[:3]):
        moved.append(lax.ppermute(s, "lo", [(i, i ^ (2 * m)) for i in range(8)]))
    for m, s in zip((1, 2, 3), sends[3:6]):
        moved.append(lax.ppermute(s, "hi", [(i, i ^ (4 * m)) for i in range(16)]))
    for m, s in enumerate(sends[6:]):
        moved.append(lax.ppermute(s, "hi", [(i, i ^ (4 * m + 2)) for i in range(16)]))

    state = pl.pallas_call(
        functools.partial(send_kernel, nv, 0),
        out_shape=shape((8, 128, ncv * 128), F32),
        in_specs=[VMEM],
        out_specs=VMEM,
        scratch_shapes=[pltpu.VMEM((8, 512, 128), F32)],
        compiler_params=params(6),
    )(coefficients.reshape(512, 1024))
    state, *moved[:3] = lax.optimization_barrier((state, *moved[:3]))
    state = lax.all_to_all(state, "lo", 0, 0, tiled=True)

    cos_lo, sin_lo, w_lo = pl.pallas_call(
        table_lo_kernel,
        out_shape=[shape((3, 1024, 128), F32)] * 2 + [shape((3, 256, 256), BF16)],
        in_specs=[SMEM] + [VMEM] * 6,
        out_specs=[VMEM] * 3,
        scratch_shapes=[pltpu.VMEM((1024, 128), F32)],
        compiler_params=params(8),
    )(pos, angle_in[:3], angle_out[:3], interp[:3], *moved[:3])
    cos_hi, sin_hi, w_hi = pl.pallas_call(
        table_hi_kernel,
        out_shape=[shape((4, 1024, 128), F32)] * 2 + [shape((4, 256, 256), BF16)],
        in_specs=[SMEM] + [VMEM] * 10,
        out_specs=[VMEM] * 3,
        scratch_shapes=[pltpu.VMEM((1024, 128), F32)],
        compiler_params=params(8),
    )(pos, angle_in[3:], angle_out[3:], interp[3:], *moved[3:])

    state = pl.pallas_call(
        functools.partial(levels_lo_kernel, nv),
        out_shape=shape((16, 64, ncv * 128), F32),
        in_specs=[VMEM] * 4,
        out_specs=VMEM,
        scratch_shapes=[pltpu.VMEM((8, 128, ncv * 128), F32)] * 2,
        compiler_params=params(12),
    )(state, cos_lo, sin_lo, w_lo)
    state, cos_hi, sin_hi, w_hi = lax.optimization_barrier((state, cos_hi, sin_hi, w_hi))
    state = lax.all_to_all(state, "hi", 0, 0, tiled=True)

    wanted = destination[0]
    where = (wanted & 15) * 64 + (wanted >> 4 & 7) * 8 + (wanted >> 7)
    state = pl.pallas_call(
        functools.partial(levels_hi_kernel, nv),
        out_shape=shape((128, 8 * ncv, 128), F32),
        in_specs=[SMEM] + [VMEM] * 4,
        out_specs=VMEM,
        scratch_shapes=[pltpu.VMEM((16, 64, ncv * 128), F32)] * 2
        + [pltpu.VMEM((1024, ncv, 128), F32)],
        compiler_params=params(14),
    )(where, state, cos_hi, sin_hi, w_hi)
    state = lax.all_to_all(state, ("lo", "hi"), 0, 0, tiled=True)

    out = pl.pallas_call(
        functools.partial(final_kernel, nv),
        out_shape=shape((512, 1024), F32),
        in_specs=[VMEM],
        out_specs=VMEM,
        scratch_shapes=[pltpu.VMEM((8, 512, 128), F32)],
        compiler_params=params(6),
    )(state.reshape(1024 * ncv, 128))
    return out.reshape(2, 32, 8, 1024)


def solution(mesh):
    placed = (
        P(None, None, None, ("lo", "hi")),
        P(None, None, ("lo", "hi")),
        P(None, None, ("lo", "hi")),
        P(),
        P(("lo", "hi"), None),
    )
    return jax.shard_map(
        shards,
        mesh=mesh,
        in_specs=placed,
        out_specs=P(None, None, None, ("lo", "hi")),
        check_vma=False,
    )
```

```python
import functools

import jax
import jax.numpy as jnp
from jax import lax
from jax.experimental import pallas as pl
from jax.experimental.pallas import tpu as pltpu
from jax.sharding import PartitionSpec as P

F32 = jnp.float32
BF16 = jnp.bfloat16
VMEM = pl.BlockSpec(memory_space=pltpu.VMEM)
SMEM = pl.BlockSpec(memory_space=pltpu.SMEM)
ANY = pl.BlockSpec(memory_space=pl.ANY)
HBM = pl.BlockSpec(memory_space=pltpu.HBM)
AXES = ("y", "zh", "x", "zl", "c")
PI = 3.141592653589793
TAU = 6.283185307179586

SIN = (
    0.9999996039252741,
    -0.1666655344642713,
    0.008332407591595805,
    -0.00019808739967677424,
    2.699822692004479e-06,
    -2.036622659870151e-08,
)
COS = (
    0.999999989116818,
    -0.49999989185961996,
    0.04166649020175043,
    -0.0013887807832168462,
    2.476996623505445e-05,
    -2.70797756302502e-07,
    1.724760753325688e-09,
)
MIB = 1024 * 1024


def params(mib):
    return pltpu.CompilerParams(vmem_limit_bytes=mib * MIB)


def rev(value, bits):
    out = 0
    for i in range(bits):
        out = out | ((value >> i & 1) << (bits - 1 - i))
    return out


def horner(coefs, u):
    acc = jnp.full_like(u, coefs[-1])
    for c in reversed(coefs[:-1]):
        acc = acc * u + c
    return acc


def sincos(x):
    u = x * x
    return x * horner(SIN, u), horner(COS, u)


def dot(a, b, dims=((1,), (0,))):
    return lax.dot_general(a, b, (dims, ((), ())), preferred_element_type=F32)


def split(x):
    hi = x.astype(BF16)
    return hi, (x - hi.astype(F32)).astype(BF16)


def send_kernel(nv, x_ref, out_ref, columns):
    for kt in range(8):
        columns[kt] = x_ref[:, kt * 128 : kt * 128 + 128]
        for c in range(2):
            for v in range(nv):
                part = columns[kt, pl.ds(c * 256 + v, 128, stride=2), :].T
                lanes = slice((c * nv + v) * 128, (c * nv + v) * 128 + 128)
                for core in range(2):
                    out_ref[rev(kt, 3) * 2 + core, :, lanes] = part[core * 64 : core * 64 + 64]


def final_kernel(nv, x_ref, out_ref, columns):
    ncv = 2 * nv
    for kt in range(8):
        for c in range(2):
            for v in range(nv):
                cv = c * nv + v
                part = x_ref[pl.ds(kt * 128 * ncv + cv, 128, stride=ncv), :]
                columns[kt, pl.ds(c * 256 + v, 128, stride=2), :] = part.T
        out_ref[:, kt * 128 : kt * 128 + 128] = columns[kt]


def fetch(jobs, sems):
    copies = []
    for i, (ain, aout, level, start, width, dst, at) in enumerate(jobs):
        cols = pl.ds(pl.multiple_of(start, 128), width)
        copies.append(
            pltpu.make_async_copy(
                ain.at[level, :, cols], dst.at[0:64, at : at + width], sems.at[0, i]
            )
        )
        copies.append(
            pltpu.make_async_copy(
                aout.at[level, :, cols], dst.at[64:96, at : at + width], sems.at[1, i]
            )
        )
    for copy in copies:
        copy.start()
    for copy in copies:
        copy.wait()


def pack_kernel(pos_ref, ain, aout, y1, y2, y3, x1, x2, x3, sems):
    y = pos_ref[0]
    x = pos_ref[1]
    ry = rev(y, 2)
    rx = rev(x, 2)
    jobs = []
    for m, dst in ((1, y1), (2, y2), (3, y3)):
        jobs.append((ain, aout, 0, (ry ^ rev(m, 2)) * 256, 256, dst, 0))
    jobs.append((ain, aout, 1, ((y >> 1) ^ 1) * 512, 512, y2, 256))
    for m, dst in ((1, x1), (2, x2), (3, x3)):
        jobs.append((ain, aout, 4, (rx ^ rev(m, 2)) * 256, 256, dst, 0))
    jobs.append((ain, aout, 5, ((x >> 1) ^ 1) * 512, 512, x2, 256))
    fetch(jobs, sems)


def core_kernel(pos_ref, ain, aout, y1, y2, y3, kept, sent, sems):
    y = pos_ref[0]
    core = pos_ref[2]
    ry = rev(y, 2)
    jobs = []
    for dst, side in ((kept, core), (sent, 1 - core)):
        jobs.append((ain, aout, 0, ry * 256 + side * 128, 128, dst, 0))
        jobs.append((ain, aout, 1, (y >> 1) * 512 + side * 256, 256, dst, 512))
        jobs.append((ain, aout, 2, side * 512, 512, dst, 1024))
    fetch(jobs, sems)
    for dst, side in ((kept, core), (sent, 1 - core)):
        for m, src in ((1, y1), (2, y2), (3, y3)):
            cols = pl.ds(pl.multiple_of(side * 128, 128), 128)
            dst[:, m * 128 : m * 128 + 128] = src[:, cols]
        cols = pl.ds(pl.multiple_of(256 + side * 256, 128), 256)
        dst[:, 768:1024] = y2[:, cols]


def turned(read, scratch, width):
    for t in range(width // 128):
        part = read(slice(t * 128, t * 128 + 128))
        full = jnp.concatenate([part, jnp.zeros((32, 128), F32)], axis=0)
        scratch[t * 128 : t * 128 + 128, :] = full.T


def got(ref, at):
    return lambda s: ref[:, at + s.start : at + s.stop]


def weights(interp_ref, w_ref, first, count):
    row = lax.broadcasted_iota(jnp.int32, (256, 64), 0)
    col = lax.broadcasted_iota(jnp.int32, (256, 64), 1)
    left = ((row >> 2) == col).astype(F32).astype(BF16)
    row = lax.broadcasted_iota(jnp.int32, (32, 128), 0)
    col = lax.broadcasted_iota(jnp.int32, (32, 128), 1)
    right = (row == (col >> 2)).astype(F32).astype(BF16)
    row = lax.broadcasted_iota(jnp.int32, (256, 128), 0)
    col = lax.broadcasted_iota(jnp.int32, (256, 128), 1)
    keep = (row & 3) == (col & 3)
    for level in range(count):
        for i, part in enumerate(split(interp_ref[first + level])):
            mid = dot(left, part, ((1,), (1,))).astype(BF16)
            full = jnp.where(keep, dot(mid, right), 0.0)
            w_ref[level, :, i * 128 : i * 128 + 128] = full.astype(BF16)


def tables(count, slabs, raw, cos_ref, sin_ref):
    rows = 1024 // slabs
    lane = lax.broadcasted_iota(jnp.int32, (rows, 128), 1)

    def body(m, _):
        low = pl.ds(pl.multiple_of(m * rows, rows), rows)
        high = pl.ds(pl.multiple_of((m + slabs // 2) * rows, rows), rows)
        for level in range(count):
            if level:
                before = jnp.where(
                    lane < 32,
                    pltpu.roll(raw[level - 1, low, :], 64, 1),
                    pltpu.roll(raw[level - 1, high, :], 96, 1),
                )
                before = jnp.where(lane < 64, before, 0.0)
            for t in range(2):
                at = pl.ds(pl.multiple_of((2 * m + t) * rows, rows), rows)
                angle = raw[level, at, :]
                if level:
                    angle = angle + before
                    turn = jnp.where(angle > PI, TAU, jnp.where(angle < -PI, -TAU, 0.0))
                    angle = angle - turn
                s, c = sincos(angle)
                cos_ref[level, at, :] = c
                sin_ref[level, at, :] = s
        return 0

    lax.fori_loop(0, slabs // 2, body, 0)


def table_lo_kernel(
    pos_ref, ain, aout, interp, kept, other, cos_ref, sin_ref, w_ref, raw, scratch, mine, sems
):
    y = pos_ref[0]
    core = pos_ref[2]
    ry = rev(y, 2)
    fetch([(ain, aout, 3, 0, 1024, mine, 0)], sems)
    weights(interp, w_ref, 0, 4)

    def emit(level, base, ts):
        for t in range(ts):
            at = pl.multiple_of((base + t) * 64, 64)
            raw[level, pl.ds(at, 64), :] = scratch[pl.ds(t, 64, stride=ts), :]

    for src, side in ((kept, core), (other, 1 - core)):
        for m in range(4):
            turned(got(src, m * 128), scratch, 128)
            emit(0, ((ry ^ rev(m, 2)) * 2 + side) * 2, 2)
        for m in range(2):
            turned(got(src, 512 + m * 256), scratch, 256)
            emit(1, (((y >> 1) ^ m) * 2 + side) * 4, 4)
        turned(got(src, 1024), scratch, 512)
        emit(2, side * 8, 8)
    turned(got(mine, 0), scratch, 1024)
    emit(3, 0, 16)
    tables(4, 16, raw, cos_ref, sin_ref)


def table_hi_kernel(
    pos_ref, ain, aout, interp, x1, x2, x3, cos_ref, sin_ref, w_ref, raw, scratch, mine, sems
):
    x = pos_ref[1]
    rx = rev(x, 2)
    fetch(
        [
            (ain, aout, 4, rx * 256, 256, mine, 0),
            (ain, aout, 5, (x >> 1) * 512, 512, mine, 256),
            (ain, aout, 6, 0, 1024, mine, 768),
        ],
        sems,
    )
    weights(interp, w_ref, 4, 3)

    def emit(level, base, ts):
        for t in range(ts):
            for T in range(16):
                at = pl.multiple_of((base + t) * 128 + T * 8, 8)
                raw[level, pl.ds(at, 8), :] = scratch[pl.ds(T * ts + t, 8, stride=16 * ts), :]

    for m, src in enumerate((None, x1, x2, x3)):
        read = got(mine, 0) if m == 0 else got(src, 0)
        turned(read, scratch, 256)
        emit(0, (rx ^ rev(m, 2)) * 2, 2)
    turned(got(mine, 256), scratch, 512)
    emit(1, (x >> 1) * 4, 4)
    turned(got(x2, 256), scratch, 512)
    emit(1, (1 - (x >> 1)) * 4, 4)
    turned(got(mine, 768), scratch, 1024)
    emit(2, 0, 8)
    tables(3, 8, raw, cos_ref, sin_ref)


def spread(table, kind):
    lane = lax.broadcasted_iota(jnp.int32, table.shape, 1)
    return jnp.take_along_axis(table, kind * 32 + (lane >> 2), axis=1)


def step(nv, low, high, cos, sin, w, last):
    n = cos.shape[0]
    sides = []
    for kind, src in enumerate((low, high)):
        c = spread(cos, kind)
        s = spread(sin, kind)
        re, im = [], []
        for v in range(nv):
            xr = src(v)
            xi = src(nv + v)
            re.append(xr * c - xi * s)
            im.append(xr * s + xi * c)
        sides.append(jnp.concatenate(re + im, axis=0))
    hi, lo = split(jnp.concatenate(sides, axis=1))
    first = dot(hi, w)
    out = first[:, :128] + first[:, 128:] + dot(lo, w[:, :128])
    out = [out[q * n : q * n + n] for q in range(2 * nv)]
    if not last:
        return out
    c = spread(cos, 2)
    s = spread(sin, 2)
    re = [out[v] * c - out[nv + v] * s for v in range(nv)]
    im = [out[v] * s + out[nv + v] * c for v in range(nv)]
    return re + im


def run_level(nv, level, last, count, rows, load_low, load_high, store, cos_ref, sin_ref, w_ref):
    group = 128 // rows
    w = w_ref[level]

    def body(i, _):
        for t in range(2):
            at = [
                pl.multiple_of((2 * (i * group + g) + t) * rows, rows) for g in range(group)
            ]
            c = jnp.concatenate([cos_ref[level, pl.ds(a, rows), :] for a in at], axis=0)
            s = jnp.concatenate([sin_ref[level, pl.ds(a, rows), :] for a in at], axis=0)
            low = lambda q: jnp.concatenate(
                [load_low(i * group + g, q) for g in range(group)], axis=0
            )
            high = lambda q: jnp.concatenate(
                [load_high(i * group + g, q) for g in range(group)], axis=0
            )
            for q, tile in enumerate(step(nv, low, high, c, s, w, last)):
                for g in range(group):
                    store(2 * (i * group + g) + t, q, tile[g * rows : g * rows + rows])
        return 0

    lax.fori_loop(0, count // group, body, 0)


def levels_kernel(nv, count, slabs, load_first, store_last, sources, held, sems, one, two):
    rows = 1024 // slabs
    lanes = lambda q: slice(q * 128, q * 128 + 128)
    copies = []
    for level in range(count):
        copies.append(
            [
                pltpu.make_async_copy(src.at[level], dst.at[level], sems.at[i, level])
                for i, (src, dst) in enumerate(zip(sources, held))
            ]
        )
        for copy in copies[-1]:
            copy.start()
    bufs = (one, two)
    for level in range(count):
        for copy in copies[level]:
            copy.wait()
        src = bufs[(level + 1) % 2]
        dst = bufs[level % 2]
        if level == 0:
            low, high = load_first
        else:
            low = lambda m, q, src=src: src[m, :, lanes(q)]
            high = lambda m, q, src=src: src[m + slabs // 2, :, lanes(q)]
        last = level == count - 1

        def store(slab, q, tile, dst=dst):
            dst[slab, :, lanes(q)] = tile

        run_level(
            nv, level, last, slabs // 2, rows, low, high,
            store_last if last else store, *held,
        )


def levels_lo_kernel(nv, x_ref, cos, sin, w, out_ref, one, two, cos_v, sin_v, w_v, sems):
    lanes = lambda q: slice(q * 128, q * 128 + 128)

    def at(m):
        return (m >> 1 & 1) * 8 + (m >> 2 & 1) * 4 + (m & 1)

    def put(slab, q, tile):
        for kp in range(8):
            rows = pl.ds(pl.multiple_of(slab * 8, 8), 8)
            out_ref[rev(kp, 3), rows, lanes(q)] = tile[kp * 8 : kp * 8 + 8]

    levels_kernel(
        nv, 4, 16,
        (lambda m, q: x_ref[at(m), :, lanes(q)], lambda m, q: x_ref[at(m) + 2, :, lanes(q)]),
        put, (cos, sin, w), (cos_v, sin_v, w_v), sems, one, two,
    )


def levels_hi_kernel(
    nv, where_ref, x_ref, cos, sin, w, out_ref, one, two, cos_v, sin_v, w_v, sems, done
):
    lanes = lambda q: slice(q * 128, q * 128 + 128)
    ncv = 2 * nv

    def put(slab, q, tile):
        done[pl.ds(pl.multiple_of(slab * 128, 128), 128), q, :] = tile

    levels_kernel(
        nv, 3, 8,
        (
            lambda m, q: x_ref[rev(m, 2) * 2, :, lanes(q)],
            lambda m, q: x_ref[rev(m, 2) * 2 + 1, :, lanes(q)],
        ),
        put, (cos, sin, w), (cos_v, sin_v, w_v), sems, one, two,
    )

    def gather(e, _):
        for r in range(8):
            out_ref[e, r * ncv : r * ncv + ncv, :] = done[where_ref[e * 8 + r]]
        return 0

    lax.fori_loop(0, 128, gather, 0)


def held(count):
    return [
        pltpu.VMEM((count, 1024, 128), F32),
        pltpu.VMEM((count, 1024, 128), F32),
        pltpu.VMEM((count, 256, 256), BF16),
        pltpu.SemaphoreType.DMA((3, count)),
    ]


def table_shapes(count):
    shape = jax.ShapeDtypeStruct
    return [shape((count, 1024, 128), F32)] * 2 + [shape((count, 256, 256), BF16)]


def shards(coefficients, angle_in, angle_out, interp, destination):
    nv = 2
    ncv = 2 * nv
    shape = jax.ShapeDtypeStruct
    pos = jnp.stack([lax.axis_index("y"), lax.axis_index("x"), lax.axis_index("c")])
    pos = pos.astype(jnp.int32)

    sends = pl.pallas_call(
        pack_kernel,
        out_shape=[shape((96, w), F32) for w in (256, 768, 256) * 2],
        in_specs=[SMEM, HBM, HBM],
        out_specs=[VMEM] * 6,
        scratch_shapes=[pltpu.SemaphoreType.DMA((2, 8))],
        compiler_params=params(56),
    )(pos, angle_in, angle_out)
    from_y = [
        lax.ppermute(s, "y", [(i, i ^ m) for i in range(4)]) for m, s in zip((1, 2, 3), sends[:3])
    ]

    state = pl.pallas_call(
        functools.partial(send_kernel, nv),
        out_shape=shape((16, 64, ncv * 128), F32),
        in_specs=[VMEM],
        out_specs=VMEM,
        scratch_shapes=[pltpu.VMEM((8, 512, 128), F32)],
        compiler_params=params(6),
    )(coefficients.reshape(512, 1024))
    state, *from_y = lax.optimization_barrier((state, *from_y))
    state = lax.all_to_all(state, ("y", "zh", "c"), 0, 0, tiled=True)

    from_x = [
        lax.ppermute(s, "x", [(i, i ^ m) for i in range(4)]) for m, s in zip((1, 2, 3), sends[3:])
    ]
    kept, sent = pl.pallas_call(
        core_kernel,
        out_shape=[shape((96, 1536), F32)] * 2,
        in_specs=[SMEM, HBM, HBM] + [VMEM] * 3,
        out_specs=[VMEM] * 2,
        scratch_shapes=[pltpu.SemaphoreType.DMA((2, 6))],
        compiler_params=params(6),
    )(pos, angle_in, angle_out, *from_y)
    other = lax.ppermute(sent, "c", [(0, 1), (1, 0)])

    tables_lo = pl.pallas_call(
        table_lo_kernel,
        out_shape=table_shapes(4),
        in_specs=[SMEM, HBM, HBM] + [VMEM] * 3,
        out_specs=[VMEM] * 3,
        scratch_shapes=[
            pltpu.VMEM((4, 1024, 128), F32),
            pltpu.VMEM((1024, 128), F32),
            pltpu.VMEM((96, 1024), F32),
            pltpu.SemaphoreType.DMA((2, 1)),
        ],
        compiler_params=params(12),
    )(pos, angle_in, angle_out, interp, kept, other)
    tables_hi = pl.pallas_call(
        table_hi_kernel,
        out_shape=table_shapes(3),
        in_specs=[SMEM, HBM, HBM] + [VMEM] * 4,
        out_specs=[VMEM] * 3,
        scratch_shapes=[
            pltpu.VMEM((3, 1024, 128), F32),
            pltpu.VMEM((1024, 128), F32),
            pltpu.VMEM((96, 1792), F32),
            pltpu.SemaphoreType.DMA((2, 3)),
        ],
        compiler_params=params(12),
    )(pos, angle_in, angle_out, interp, *from_x)

    state = pl.pallas_call(
        functools.partial(levels_lo_kernel, nv),
        out_shape=shape((8, 128, ncv * 128), F32),
        in_specs=[VMEM] + [ANY] * 3,
        out_specs=VMEM,
        scratch_shapes=[pltpu.VMEM((16, 64, ncv * 128), F32)] * 2 + held(4),
        compiler_params=params(24),
    )(state, *tables_lo)
    state, *tables_hi = lax.optimization_barrier((state, *tables_hi))
    state = lax.all_to_all(state, ("x", "zl"), 0, 0, tiled=True)

    wanted = destination[0]
    where = (wanted & 7) * 128 + (wanted >> 3 & 15) * 8 + (wanted >> 7)
    state = pl.pallas_call(
        functools.partial(levels_hi_kernel, nv),
        out_shape=shape((128, 8 * ncv, 128), F32),
        in_specs=[SMEM, VMEM] + [ANY] * 3,
        out_specs=VMEM,
        scratch_shapes=[pltpu.VMEM((8, 128, ncv * 128), F32)] * 2
        + held(3)
        + [pltpu.VMEM((1024, ncv, 128), F32)],
        compiler_params=params(24),
    )(where, state, *tables_hi)
    state = lax.all_to_all(state, AXES, 0, 0, tiled=True)

    out = pl.pallas_call(
        functools.partial(final_kernel, nv),
        out_shape=shape((512, 1024), F32),
        in_specs=[VMEM],
        out_specs=VMEM,
        scratch_shapes=[pltpu.VMEM((8, 512, 128), F32)],
        compiler_params=params(6),
    )(state.reshape(1024 * ncv, 128))
    return out.reshape(2, 32, 8, 1024)


def solution(mesh):
    mesh = jax.sharding.Mesh(mesh.devices.reshape(4, 2, 4, 2, 2), AXES)
    placed = (
        P(None, None, None, AXES),
        P(None, None, AXES),
        P(None, None, AXES),
        P(),
        P(AXES, None),
    )
    return jax.shard_map(
        shards,
        mesh=mesh,
        in_specs=placed,
        out_specs=P(None, None, None, AXES),
        check_vma=False,
    )
```

```python
import functools

import jax
import jax.numpy as jnp
from jax import lax
from jax.experimental import pallas as pl
from jax.experimental.pallas import tpu as pltpu
from jax.sharding import PartitionSpec as P

F32 = jnp.float32
BF16 = jnp.bfloat16
VMEM = pl.BlockSpec(memory_space=pltpu.VMEM)
SMEM = pl.BlockSpec(memory_space=pltpu.SMEM)
ANY = pl.BlockSpec(memory_space=pl.ANY)
HBM = pl.BlockSpec(memory_space=pltpu.HBM)
AXES = ("y", "zh", "x", "zl", "c")
PI = 3.141592653589793
TAU = 6.283185307179586

SIN = (
    0.9999996039252741,
    -0.1666655344642713,
    0.008332407591595805,
    -0.00019808739967677424,
    2.699822692004479e-06,
    -2.036622659870151e-08,
)
COS = (
    0.999999989116818,
    -0.49999989185961996,
    0.04166649020175043,
    -0.0013887807832168462,
    2.476996623505445e-05,
    -2.70797756302502e-07,
    1.724760753325688e-09,
)
MIB = 1024 * 1024
BIG = 56


def params(mib):
    return pltpu.CompilerParams(vmem_limit_bytes=mib * MIB)


def rev(value, bits):
    out = 0
    for i in range(bits):
        out = out | ((value >> i & 1) << (bits - 1 - i))
    return out


def horner(coefs, u):
    acc = jnp.full_like(u, coefs[-1])
    for c in reversed(coefs[:-1]):
        acc = acc * u + c
    return acc


def sincos(x):
    u = x * x
    return x * horner(SIN, u), horner(COS, u)


def dot(a, b, dims=((1,), (0,))):
    return lax.dot_general(a, b, (dims, ((), ())), preferred_element_type=F32)


def split(x):
    hi = x.astype(BF16)
    return hi, (x - hi.astype(F32)).astype(BF16)


def send_kernel(nv, x_ref, out_ref, columns):
    for kt in range(8):
        columns[kt] = x_ref[:, kt * 128 : kt * 128 + 128]
        for c in range(2):
            for v in range(nv):
                part = columns[kt, pl.ds(c * 256 + v, 128, stride=2), :].T
                lanes = slice((c * nv + v) * 128, (c * nv + v) * 128 + 128)
                for core in range(2):
                    out_ref[rev(kt, 3) * 2 + core, :, lanes] = part[core * 64 : core * 64 + 64]


def final_kernel(nv, x_ref, out_ref, columns):
    ncv = 2 * nv
    for kt in range(8):
        for c in range(2):
            for v in range(nv):
                cv = c * nv + v
                part = x_ref[pl.ds(kt * 128 * ncv + cv, 128, stride=ncv), :]
                columns[kt, pl.ds(c * 256 + v, 128, stride=2), :] = part.T
        out_ref[:, kt * 128 : kt * 128 + 128] = columns[kt]


def fetch(jobs, sems):
    copies = []
    for i, (ain, aout, level, start, width, dst, at) in enumerate(jobs):
        cols = pl.ds(pl.multiple_of(start, 128), width)
        copies.append(
            pltpu.make_async_copy(
                ain.at[level, :, cols], dst.at[0:64, at : at + width], sems.at[0, i]
            )
        )
        copies.append(
            pltpu.make_async_copy(
                aout.at[level, :, cols], dst.at[64:96, at : at + width], sems.at[1, i]
            )
        )
    for copy in copies:
        copy.start()
    for copy in copies:
        copy.wait()


def pack_y_kernel(ain, aout, y1, y2, y3, sems):
    y = lax.axis_index("y")
    ry = rev(y, 2)
    jobs = [(ain, aout, 1, ((y >> 1) ^ 1) * 512, 512, y2, 256)]
    for m, dst in ((2, y2), (1, y1), (3, y3)):
        jobs.append((ain, aout, 0, (ry ^ rev(m, 2)) * 256, 256, dst, 0))
    fetch(jobs, sems)


def pack_x_kernel(ain, aout, x1, x2, x3, sems):
    x = lax.axis_index("x")
    rx = rev(x, 2)
    jobs = [(ain, aout, 5, ((x >> 1) ^ 1) * 512, 512, x2, 256)]
    for m, dst in ((2, x2), (1, x1), (3, x3)):
        jobs.append((ain, aout, 4, (rx ^ rev(m, 2)) * 256, 256, dst, 0))
    fetch(jobs, sems)


def core_kernel(ain, aout, y1, y2, y3, kept, sent, sems):
    y = lax.axis_index("y")
    core = lax.axis_index("c")
    ry = rev(y, 2)
    jobs = []
    for dst, side in ((kept, core), (sent, 1 - core)):
        jobs.append((ain, aout, 0, ry * 256 + side * 128, 128, dst, 0))
        jobs.append((ain, aout, 1, (y >> 1) * 512 + side * 256, 256, dst, 512))
        jobs.append((ain, aout, 2, side * 512, 512, dst, 1024))
    fetch(jobs, sems)
    for dst, side in ((kept, core), (sent, 1 - core)):
        for m, src in ((1, y1), (2, y2), (3, y3)):
            cols = pl.ds(pl.multiple_of(side * 128, 128), 128)
            dst[:, m * 128 : m * 128 + 128] = src[:, cols]
        cols = pl.ds(pl.multiple_of(256 + side * 256, 128), 256)
        dst[:, 768:1024] = y2[:, cols]


def turned(read, scratch, width):
    for t in range(width // 128):
        part = read(slice(t * 128, t * 128 + 128))
        full = jnp.concatenate([part, jnp.zeros((32, 128), F32)], axis=0)
        scratch[t * 128 : t * 128 + 128, :] = full.T


def got(ref, at):
    return lambda s: ref[:, at + s.start : at + s.stop]


def weights(interp_ref, w_ref, first, count):
    row = lax.broadcasted_iota(jnp.int32, (256, 64), 0)
    col = lax.broadcasted_iota(jnp.int32, (256, 64), 1)
    left = ((row >> 2) == col).astype(F32).astype(BF16)
    row = lax.broadcasted_iota(jnp.int32, (32, 128), 0)
    col = lax.broadcasted_iota(jnp.int32, (32, 128), 1)
    right = (row == (col >> 2)).astype(F32).astype(BF16)
    row = lax.broadcasted_iota(jnp.int32, (256, 128), 0)
    col = lax.broadcasted_iota(jnp.int32, (256, 128), 1)
    keep = (row & 3) == (col & 3)
    for level in range(count):
        for i, part in enumerate(split(interp_ref[first + level])):
            mid = dot(left, part, ((1,), (1,))).astype(BF16)
            full = jnp.where(keep, dot(mid, right), 0.0)
            w_ref[level, :, i * 128 : i * 128 + 128] = full.astype(BF16)


def tables(count, slabs, raw, cos_ref, sin_ref):
    rows = 1024 // slabs
    lane = lax.broadcasted_iota(jnp.int32, (rows, 128), 1)

    def body(m, _):
        low = pl.ds(pl.multiple_of(m * rows, rows), rows)
        high = pl.ds(pl.multiple_of((m + slabs // 2) * rows, rows), rows)
        for level in range(count):
            if level:
                before = jnp.where(
                    lane < 32,
                    pltpu.roll(raw[level - 1, low, :], 64, 1),
                    pltpu.roll(raw[level - 1, high, :], 96, 1),
                )
                before = jnp.where(lane < 64, before, 0.0)
            for t in range(2):
                at = pl.ds(pl.multiple_of((2 * m + t) * rows, rows), rows)
                angle = raw[level, at, :]
                if level:
                    angle = angle + before
                    turn = jnp.where(angle > PI, TAU, jnp.where(angle < -PI, -TAU, 0.0))
                    angle = angle - turn
                s, c = sincos(angle)
                cos_ref[level, at, :] = c
                sin_ref[level, at, :] = s
        return 0

    lax.fori_loop(0, slabs // 2, body, 0)


def table_lo_kernel(
    ain, aout, interp, kept, other, cos_ref, sin_ref, w_ref, raw, scratch, mine, sems
):
    y = lax.axis_index("y")
    core = lax.axis_index("c")
    ry = rev(y, 2)
    fetch([(ain, aout, 3, 0, 1024, mine, 0)], sems)
    weights(interp, w_ref, 0, 4)

    def emit(level, base, ts):
        for t in range(ts):
            at = pl.multiple_of((base + t) * 64, 64)
            raw[level, pl.ds(at, 64), :] = scratch[pl.ds(t, 64, stride=ts), :]

    for src, side in ((kept, core), (other, 1 - core)):
        for m in range(4):
            turned(got(src, m * 128), scratch, 128)
            emit(0, ((ry ^ rev(m, 2)) * 2 + side) * 2, 2)
        for m in range(2):
            turned(got(src, 512 + m * 256), scratch, 256)
            emit(1, (((y >> 1) ^ m) * 2 + side) * 4, 4)
        turned(got(src, 1024), scratch, 512)
        emit(2, side * 8, 8)
    turned(got(mine, 0), scratch, 1024)
    emit(3, 0, 16)
    tables(4, 16, raw, cos_ref, sin_ref)


def table_hi_kernel(
    ain, aout, interp, x1, x2, x3, cos_ref, sin_ref, w_ref, raw, scratch, mine, sems
):
    x = lax.axis_index("x")
    rx = rev(x, 2)
    fetch(
        [
            (ain, aout, 4, rx * 256, 256, mine, 0),
            (ain, aout, 5, (x >> 1) * 512, 512, mine, 256),
            (ain, aout, 6, 0, 1024, mine, 768),
        ],
        sems,
    )
    weights(interp, w_ref, 4, 3)

    def emit(level, base, ts):
        for t in range(ts):
            for T in range(16):
                at = pl.multiple_of((base + t) * 128 + T * 8, 8)
                raw[level, pl.ds(at, 8), :] = scratch[pl.ds(T * ts + t, 8, stride=16 * ts), :]

    for m, src in enumerate((None, x1, x2, x3)):
        read = got(mine, 0) if m == 0 else got(src, 0)
        turned(read, scratch, 256)
        emit(0, (rx ^ rev(m, 2)) * 2, 2)
    turned(got(mine, 256), scratch, 512)
    emit(1, (x >> 1) * 4, 4)
    turned(got(x2, 256), scratch, 512)
    emit(1, (1 - (x >> 1)) * 4, 4)
    turned(got(mine, 768), scratch, 1024)
    emit(2, 0, 8)
    tables(3, 8, raw, cos_ref, sin_ref)


def spread(table, kind):
    lane = lax.broadcasted_iota(jnp.int32, table.shape, 1)
    return jnp.take_along_axis(table, kind * 32 + (lane >> 2), axis=1)


def step(nv, low, high, cos, sin, w, last):
    n = cos.shape[0]
    sides = []
    for kind, src in enumerate((low, high)):
        c = spread(cos, kind)
        s = spread(sin, kind)
        re, im = [], []
        for v in range(nv):
            xr = src(v)
            xi = src(nv + v)
            re.append(xr * c - xi * s)
            im.append(xr * s + xi * c)
        sides.append(jnp.concatenate(re + im, axis=0))
    hi, lo = split(jnp.concatenate(sides, axis=1))
    first = dot(hi, w)
    out = first[:, :128] + first[:, 128:] + dot(lo, w[:, :128])
    out = [out[q * n : q * n + n] for q in range(2 * nv)]
    if not last:
        return out
    c = spread(cos, 2)
    s = spread(sin, 2)
    re = [out[v] * c - out[nv + v] * s for v in range(nv)]
    im = [out[v] * s + out[nv + v] * c for v in range(nv)]
    return re + im


def run_level(nv, level, last, count, rows, load_low, load_high, store, cos_ref, sin_ref, w_ref):
    group = 128 // rows
    w = w_ref[level]

    for i in range(count // group):
        for t in range(2):
            at = [(2 * (i * group + g) + t) * rows for g in range(group)]
            c = jnp.concatenate([cos_ref[level, pl.ds(a, rows), :] for a in at], axis=0)
            s = jnp.concatenate([sin_ref[level, pl.ds(a, rows), :] for a in at], axis=0)
            low = lambda q: jnp.concatenate(
                [load_low(i * group + g, q) for g in range(group)], axis=0
            )
            high = lambda q: jnp.concatenate(
                [load_high(i * group + g, q) for g in range(group)], axis=0
            )
            for q, tile in enumerate(step(nv, low, high, c, s, w, last)):
                for g in range(group):
                    store(2 * (i * group + g) + t, q, tile[g * rows : g * rows + rows])


def levels_kernel(nv, count, slabs, load_first, store_last, sources, held, sems, one, two):
    rows = 1024 // slabs
    lanes = lambda q: slice(q * 128, q * 128 + 128)
    copies = []
    for level in range(count):
        copies.append(
            [
                pltpu.make_async_copy(src.at[level], dst.at[level], sems.at[i, level])
                for i, (src, dst) in enumerate(zip(sources, held))
            ]
        )
        for copy in copies[-1]:
            copy.start()
    bufs = (one, two)
    for level in range(count):
        for copy in copies[level]:
            copy.wait()
        src = bufs[(level + 1) % 2]
        dst = bufs[level % 2]
        if level == 0:
            low, high = load_first
        else:
            low = lambda m, q, src=src: src[m, :, lanes(q)]
            high = lambda m, q, src=src: src[m + slabs // 2, :, lanes(q)]
        last = level == count - 1

        def store(slab, q, tile, dst=dst):
            dst[slab, :, lanes(q)] = tile

        run_level(
            nv, level, last, slabs // 2, rows, low, high,
            store_last if last else store, *held,
        )


def levels_lo_kernel(nv, x_ref, cos, sin, w, out_ref, one, two, cos_v, sin_v, w_v, sems):
    lanes = lambda q: slice(q * 128, q * 128 + 128)

    def at(m):
        return (m >> 1 & 1) * 8 + (m >> 2 & 1) * 4 + (m & 1)

    def put(slab, q, tile):
        for kp in range(8):
            rows = slice(slab * 8, slab * 8 + 8)
            out_ref[rev(kp, 3), rows, lanes(q)] = tile[kp * 8 : kp * 8 + 8]

    levels_kernel(
        nv, 4, 16,
        (lambda m, q: x_ref[at(m), :, lanes(q)], lambda m, q: x_ref[at(m) + 2, :, lanes(q)]),
        put, (cos, sin, w), (cos_v, sin_v, w_v), sems, one, two,
    )


def levels_hi_kernel(
    nv, where_ref, x_ref, cos, sin, w, out_ref, one, two, cos_v, sin_v, w_v, sems, done
):
    lanes = lambda q: slice(q * 128, q * 128 + 128)
    ncv = 2 * nv

    def put(slab, q, tile):
        done[slab * 128 : slab * 128 + 128, q, :] = tile

    levels_kernel(
        nv, 3, 8,
        (
            lambda m, q: x_ref[rev(m, 2) * 2, :, lanes(q)],
            lambda m, q: x_ref[rev(m, 2) * 2 + 1, :, lanes(q)],
        ),
        put, (cos, sin, w), (cos_v, sin_v, w_v), sems, one, two,
    )

    def gather(e, _):
        for r in range(8):
            out_ref[e, r * ncv : r * ncv + ncv, :] = done[where_ref[e * 8 + r]]
        return 0

    lax.fori_loop(0, 128, gather, 0)


def held(count):
    return [
        pltpu.VMEM((count, 1024, 128), F32),
        pltpu.VMEM((count, 1024, 128), F32),
        pltpu.VMEM((count, 256, 256), BF16),
        pltpu.SemaphoreType.DMA((3, count)),
    ]


def table_shapes(count):
    shape = jax.ShapeDtypeStruct
    return [shape((count, 1024, 128), F32)] * 2 + [shape((count, 256, 256), BF16)]


def shards(coefficients, angle_in, angle_out, interp, destination):
    nv = 2
    ncv = 2 * nv
    shape = jax.ShapeDtypeStruct
    sends = pl.pallas_call(
        pack_y_kernel,
        out_shape=[shape((96, w), F32) for w in (256, 768, 256)],
        in_specs=[HBM, HBM],
        out_specs=[VMEM] * 3,
        scratch_shapes=[pltpu.SemaphoreType.DMA((2, 4))],
        compiler_params=params(BIG),
    )(angle_in, angle_out)
    from_y = [
        lax.ppermute(s, "y", [(i, i ^ m) for i in range(4)]) for m, s in zip((1, 2, 3), sends)
    ]

    state = pl.pallas_call(
        functools.partial(send_kernel, nv),
        out_shape=shape((16, 64, ncv * 128), F32),
        in_specs=[VMEM],
        out_specs=VMEM,
        scratch_shapes=[pltpu.VMEM((8, 512, 128), F32)],
        compiler_params=params(6),
    )(coefficients.reshape(512, 1024))
    state, *from_y = lax.optimization_barrier((state, *from_y))
    state = lax.all_to_all(state, ("y", "zh", "c"), 0, 0, tiled=True)

    sends = pl.pallas_call(
        pack_x_kernel,
        out_shape=[shape((96, w), F32) for w in (256, 768, 256)],
        in_specs=[HBM, HBM],
        out_specs=[VMEM] * 3,
        scratch_shapes=[pltpu.SemaphoreType.DMA((2, 4))],
        compiler_params=params(BIG),
    )(angle_in, angle_out)
    from_x = [
        lax.ppermute(s, "x", [(i, i ^ m) for i in range(4)]) for m, s in zip((1, 2, 3), sends)
    ]
    kept, sent = pl.pallas_call(
        core_kernel,
        out_shape=[shape((96, 1536), F32)] * 2,
        in_specs=[HBM, HBM] + [VMEM] * 3,
        out_specs=[VMEM] * 2,
        scratch_shapes=[pltpu.SemaphoreType.DMA((2, 6))],
        compiler_params=params(BIG),
    )(angle_in, angle_out, *from_y)
    other = lax.ppermute(sent, "c", [(0, 1), (1, 0)])

    tables_lo = pl.pallas_call(
        table_lo_kernel,
        out_shape=table_shapes(4),
        in_specs=[HBM, HBM] + [VMEM] * 3,
        out_specs=[VMEM] * 3,
        scratch_shapes=[
            pltpu.VMEM((4, 1024, 128), F32),
            pltpu.VMEM((1024, 128), F32),
            pltpu.VMEM((96, 1024), F32),
            pltpu.SemaphoreType.DMA((2, 1)),
        ],
        compiler_params=params(BIG),
    )(angle_in, angle_out, interp, kept, other)
    tables_hi = pl.pallas_call(
        table_hi_kernel,
        out_shape=table_shapes(3),
        in_specs=[HBM, HBM] + [VMEM] * 4,
        out_specs=[VMEM] * 3,
        scratch_shapes=[
            pltpu.VMEM((3, 1024, 128), F32),
            pltpu.VMEM((1024, 128), F32),
            pltpu.VMEM((96, 1792), F32),
            pltpu.SemaphoreType.DMA((2, 3)),
        ],
        compiler_params=params(BIG),
    )(angle_in, angle_out, interp, *from_x)

    state = pl.pallas_call(
        functools.partial(levels_lo_kernel, nv),
        out_shape=shape((8, 128, ncv * 128), F32),
        in_specs=[VMEM] + [ANY] * 3,
        out_specs=VMEM,
        scratch_shapes=[pltpu.VMEM((16, 64, ncv * 128), F32)] * 2 + held(4),
        compiler_params=params(BIG),
    )(state, *tables_lo)
    wanted = destination[0]
    where = (wanted & 7) * 128 + (wanted >> 3 & 15) * 8 + (wanted >> 7)
    state, where, *tables_hi = lax.optimization_barrier((state, where, *tables_hi))
    state = lax.all_to_all(state, ("x", "zl"), 0, 0, tiled=True)

    state = pl.pallas_call(
        functools.partial(levels_hi_kernel, nv),
        out_shape=shape((128, 8 * ncv, 128), F32),
        in_specs=[SMEM, VMEM] + [ANY] * 3,
        out_specs=VMEM,
        scratch_shapes=[pltpu.VMEM((8, 128, ncv * 128), F32)] * 2
        + held(3)
        + [pltpu.VMEM((1024, ncv, 128), F32)],
        compiler_params=params(BIG),
    )(where, state, *tables_hi)
    state = lax.all_to_all(state, AXES, 0, 0, tiled=True)

    out = pl.pallas_call(
        functools.partial(final_kernel, nv),
        out_shape=shape((512, 1024), F32),
        in_specs=[VMEM],
        out_specs=VMEM,
        scratch_shapes=[pltpu.VMEM((8, 512, 128), F32)],
        compiler_params=params(6),
    )(state.reshape(1024 * ncv, 128))
    return out.reshape(2, 32, 8, 1024)


def solution(mesh):
    mesh = jax.sharding.Mesh(mesh.devices.reshape(4, 2, 4, 2, 2), AXES)
    placed = (
        P(None, None, None, AXES),
        P(None, None, AXES),
        P(None, None, AXES),
        P(),
        P(AXES, None),
    )
    return jax.shard_map(
        shards,
        mesh=mesh,
        in_specs=placed,
        out_specs=P(None, None, None, AXES),
        check_vma=False,
    )
```

```python
import functools

import jax
import jax.numpy as jnp
from jax import lax
from jax.experimental import pallas as pl
from jax.experimental.pallas import tpu as pltpu
from jax.sharding import PartitionSpec as P

F32 = jnp.float32
BF16 = jnp.bfloat16
VMEM = pl.BlockSpec(memory_space=pltpu.VMEM)
SMEM = pl.BlockSpec(memory_space=pltpu.SMEM)
ANY = pl.BlockSpec(memory_space=pl.ANY)
HBM = pl.BlockSpec(memory_space=pltpu.HBM)
AXES = ("y", "zh", "x", "zl", "c")
PI = 3.141592653589793
TAU = 6.283185307179586

SIN = (
    0.9999996039252741,
    -0.1666655344642713,
    0.008332407591595805,
    -0.00019808739967677424,
    2.699822692004479e-06,
    -2.036622659870151e-08,
)
COS = (
    0.999999989116818,
    -0.49999989185961996,
    0.04166649020175043,
    -0.0013887807832168462,
    2.476996623505445e-05,
    -2.70797756302502e-07,
    1.724760753325688e-09,
)
MIB = 1024 * 1024
BIG = 56


def params(mib):
    return pltpu.CompilerParams(vmem_limit_bytes=mib * MIB)


def rev(value, bits):
    out = 0
    for i in range(bits):
        out = out | ((value >> i & 1) << (bits - 1 - i))
    return out


def horner(coefs, u):
    acc = jnp.full_like(u, coefs[-1])
    for c in reversed(coefs[:-1]):
        acc = acc * u + c
    return acc


def sincos(x):
    u = x * x
    return x * horner(SIN, u), horner(COS, u)


def dot(a, b, dims=((1,), (0,))):
    return lax.dot_general(a, b, (dims, ((), ())), preferred_element_type=F32)


def split(x):
    hi = x.astype(BF16)
    return hi, (x - hi.astype(F32)).astype(BF16)


def send_kernel(nv, x_ref, out_ref, columns):
    for kt in range(8):
        columns[kt] = x_ref[:, kt * 128 : kt * 128 + 128]
        for c in range(2):
            for v in range(nv):
                part = columns[kt, pl.ds(c * 256 + v, 128, stride=2), :].T
                lanes = slice((c * nv + v) * 128, (c * nv + v) * 128 + 128)
                for core in range(2):
                    out_ref[rev(kt, 3) * 2 + core, :, lanes] = part[core * 64 : core * 64 + 64]


def final_kernel(nv, x_ref, out_ref, columns, sems):
    ncv = 2 * nv

    def leave(kt):
        lanes = slice(kt * 128, kt * 128 + 128)
        return pltpu.make_async_copy(columns.at[kt], out_ref.at[:, lanes], sems.at[kt])

    for kt in range(8):
        for c in range(2):
            for v in range(nv):
                cv = c * nv + v
                part = x_ref[pl.ds(kt * 128 * ncv + cv, 128, stride=ncv), :]
                columns[kt, pl.ds(c * 256 + v, 128, stride=2), :] = part.T
        leave(kt).start()
    for kt in range(8):
        leave(kt).wait()


def fetch(jobs, sems):
    copies = []
    for i, (ain, aout, level, start, width, dst, at) in enumerate(jobs):
        cols = pl.ds(pl.multiple_of(start, 128), width)
        copies.append(
            pltpu.make_async_copy(
                ain.at[level, :, cols], dst.at[0:64, at : at + width], sems.at[0, i]
            )
        )
        copies.append(
            pltpu.make_async_copy(
                aout.at[level, :, cols], dst.at[64:96, at : at + width], sems.at[1, i]
            )
        )
    for copy in copies:
        copy.start()
    for copy in copies:
        copy.wait()


def pack_y_kernel(ain, aout, y1, y2, y3, sems):
    y = lax.axis_index("y")
    ry = rev(y, 2)
    jobs = [(ain, aout, 1, ((y >> 1) ^ 1) * 512, 512, y2, 256)]
    for m, dst in ((2, y2), (1, y1), (3, y3)):
        jobs.append((ain, aout, 0, (ry ^ rev(m, 2)) * 256, 256, dst, 0))
    fetch(jobs, sems)


def pack_x_kernel(ain, aout, x1, x2, x3, sems):
    x = lax.axis_index("x")
    rx = rev(x, 2)
    jobs = [(ain, aout, 5, ((x >> 1) ^ 1) * 512, 512, x2, 256)]
    for m, dst in ((2, x2), (1, x1), (3, x3)):
        jobs.append((ain, aout, 4, (rx ^ rev(m, 2)) * 256, 256, dst, 0))
    fetch(jobs, sems)


def core_kernel(ain, aout, y1, y2, y3, kept, sent, sems):
    y = lax.axis_index("y")
    core = lax.axis_index("c")
    ry = rev(y, 2)
    jobs = []
    for dst, side in ((kept, core), (sent, 1 - core)):
        jobs.append((ain, aout, 0, ry * 256 + side * 128, 128, dst, 0))
        jobs.append((ain, aout, 1, (y >> 1) * 512 + side * 256, 256, dst, 512))
        jobs.append((ain, aout, 2, side * 512, 512, dst, 1024))
    fetch(jobs, sems)
    for dst, side in ((kept, core), (sent, 1 - core)):
        for m, src in ((1, y1), (2, y2), (3, y3)):
            cols = pl.ds(pl.multiple_of(side * 128, 128), 128)
            dst[:, m * 128 : m * 128 + 128] = src[:, cols]
        cols = pl.ds(pl.multiple_of(256 + side * 256, 128), 256)
        dst[:, 768:1024] = y2[:, cols]


def turned(read, scratch, width):
    for t in range(width // 128):
        part = read(slice(t * 128, t * 128 + 128))
        full = jnp.concatenate([part, jnp.zeros((32, 128), F32)], axis=0)
        scratch[t * 128 : t * 128 + 128, :] = full.T


def got(ref, at):
    return lambda s: ref[:, at + s.start : at + s.stop]


def weights(interp_ref, w_ref, first, count):
    row = lax.broadcasted_iota(jnp.int32, (256, 64), 0)
    col = lax.broadcasted_iota(jnp.int32, (256, 64), 1)
    left = ((row >> 2) == col).astype(F32).astype(BF16)
    row = lax.broadcasted_iota(jnp.int32, (32, 128), 0)
    col = lax.broadcasted_iota(jnp.int32, (32, 128), 1)
    right = (row == (col >> 2)).astype(F32).astype(BF16)
    row = lax.broadcasted_iota(jnp.int32, (256, 128), 0)
    col = lax.broadcasted_iota(jnp.int32, (256, 128), 1)
    keep = (row & 3) == (col & 3)
    for level in range(count):
        for i, part in enumerate(split(interp_ref[first + level])):
            mid = dot(left, part, ((1,), (1,))).astype(BF16)
            full = jnp.where(keep, dot(mid, right), 0.0)
            w_ref[level, :, i * 128 : i * 128 + 128] = full.astype(BF16)


def tables(count, slabs, raw, cos_ref, sin_ref, cos_v, sin_v, sems):
    rows = 1024 // slabs
    lane = lax.broadcasted_iota(jnp.int32, (rows, 128), 1)

    def leave(level):
        return [
            pltpu.make_async_copy(src.at[level], dst.at[level], sems.at[i, level])
            for i, (src, dst) in enumerate(((cos_v, cos_ref), (sin_v, sin_ref)))
        ]

    for level in range(count):

        def body(m, _):
            low = pl.ds(pl.multiple_of(m * rows, rows), rows)
            high = pl.ds(pl.multiple_of((m + slabs // 2) * rows, rows), rows)
            if level:
                before = jnp.where(
                    lane < 32,
                    pltpu.roll(raw[level - 1, low, :], 64, 1),
                    pltpu.roll(raw[level - 1, high, :], 96, 1),
                )
                before = jnp.where(lane < 64, before, 0.0)
            for t in range(2):
                at = pl.ds(pl.multiple_of((2 * m + t) * rows, rows), rows)
                angle = raw[level, at, :]
                if level:
                    angle = angle + before
                    turn = jnp.where(angle > PI, TAU, jnp.where(angle < -PI, -TAU, 0.0))
                    angle = angle - turn
                s, c = sincos(angle)
                cos_v[level, at, :] = c
                sin_v[level, at, :] = s
            return 0

        lax.fori_loop(0, slabs // 2, body, 0, unroll=2)
        for copy in leave(level):
            copy.start()
    for level in range(count):
        for copy in leave(level):
            copy.wait()


def table_lo_kernel(
    ain, aout, interp, kept, other, cos_ref, sin_ref, w_ref, raw, scratch, mine, sems,
    cos_v, sin_v, out_sems,
):
    y = lax.axis_index("y")
    core = lax.axis_index("c")
    ry = rev(y, 2)
    fetch([(ain, aout, 3, 0, 1024, mine, 0)], sems)
    weights(interp, w_ref, 0, 4)

    def emit(level, base, ts):
        for t in range(ts):
            at = pl.multiple_of((base + t) * 64, 64)
            raw[level, pl.ds(at, 64), :] = scratch[pl.ds(t, 64, stride=ts), :]

    for src, side in ((kept, core), (other, 1 - core)):
        for m in range(4):
            turned(got(src, m * 128), scratch, 128)
            emit(0, ((ry ^ rev(m, 2)) * 2 + side) * 2, 2)
        for m in range(2):
            turned(got(src, 512 + m * 256), scratch, 256)
            emit(1, (((y >> 1) ^ m) * 2 + side) * 4, 4)
        turned(got(src, 1024), scratch, 512)
        emit(2, side * 8, 8)
    turned(got(mine, 0), scratch, 1024)
    emit(3, 0, 16)
    tables(4, 16, raw, cos_ref, sin_ref, cos_v, sin_v, out_sems)


def table_hi_kernel(
    ain, aout, interp, x1, x2, x3, cos_ref, sin_ref, w_ref, raw, scratch, mine, sems,
    cos_v, sin_v, out_sems,
):
    x = lax.axis_index("x")
    rx = rev(x, 2)
    fetch(
        [
            (ain, aout, 4, rx * 256, 256, mine, 0),
            (ain, aout, 5, (x >> 1) * 512, 512, mine, 256),
            (ain, aout, 6, 0, 1024, mine, 768),
        ],
        sems,
    )
    weights(interp, w_ref, 4, 3)

    def emit(level, base, ts):
        for t in range(ts):
            for T in range(16):
                at = pl.multiple_of((base + t) * 128 + T * 8, 8)
                raw[level, pl.ds(at, 8), :] = scratch[pl.ds(T * ts + t, 8, stride=16 * ts), :]

    for m, src in enumerate((None, x1, x2, x3)):
        read = got(mine, 0) if m == 0 else got(src, 0)
        turned(read, scratch, 256)
        emit(0, (rx ^ rev(m, 2)) * 2, 2)
    turned(got(mine, 256), scratch, 512)
    emit(1, (x >> 1) * 4, 4)
    turned(got(x2, 256), scratch, 512)
    emit(1, (1 - (x >> 1)) * 4, 4)
    turned(got(mine, 768), scratch, 1024)
    emit(2, 0, 8)
    tables(3, 8, raw, cos_ref, sin_ref, cos_v, sin_v, out_sems)


def spread(table, kind):
    lane = lax.broadcasted_iota(jnp.int32, table.shape, 1)
    return jnp.take_along_axis(table, kind * 32 + (lane >> 2), axis=1)


def step(nv, low, high, cos, sin, w, last):
    n = cos.shape[0]
    sides = []
    for kind, src in enumerate((low, high)):
        c = spread(cos, kind)
        s = spread(sin, kind)
        re, im = [], []
        for v in range(nv):
            xr = src(v)
            xi = src(nv + v)
            re.append(xr * c - xi * s)
            im.append(xr * s + xi * c)
        sides.append(jnp.concatenate(re + im, axis=0))
    hi, lo = split(jnp.concatenate(sides, axis=1))
    first = dot(hi, w)
    out = first[:, :128] + first[:, 128:] + dot(lo, w[:, :128])
    out = [out[q * n : q * n + n] for q in range(2 * nv)]
    if not last:
        return out
    c = spread(cos, 2)
    s = spread(sin, 2)
    re = [out[v] * c - out[nv + v] * s for v in range(nv)]
    im = [out[v] * s + out[nv + v] * c for v in range(nv)]
    return re + im


def levels_kernel(nv, count, slabs, first, put, sources, held, sems, x_ref, bufs, x_sems, sent):
    rows = 1024 // slabs
    group = 128 // rows
    bodies = slabs // 2 // group
    lanes = lambda q: slice(q * 128, q * 128 + 128)
    one, two = bufs

    def copies(level):
        return [
            pltpu.make_async_copy(src.at[level], dst.at[level], sems.at[i, level])
            for i, (src, dst) in enumerate(zip(sources, held))
        ]

    def arrive(i):
        part = first(i)[0]
        return pltpu.make_async_copy(x_ref.at[part], two.at[part], x_sems.at[i])

    arrive(0).start()
    for copy in copies(0):
        copy.start()
    for i in range(1, bodies):
        arrive(i).start()
    for level in range(1, count):
        for copy in copies(level):
            copy.start()
    cos_ref, sin_ref, w_ref = held
    for level in range(count):
        for copy in copies(level):
            copy.wait()
        last = level == count - 1
        src = bufs[(level + 1) % 2]
        dst = bufs[level % 2]
        w = w_ref[level]
        for i in range(bodies):
            if level == 0:
                arrive(i).wait()
                lows, highs = first(i)[1:]
            else:
                lows = [i * group + g for g in range(group)]
                highs = [m + slabs // 2 for m in lows]
            low = lambda q: jnp.concatenate([src[m, :, lanes(q)] for m in lows], axis=0)
            high = lambda q: jnp.concatenate([src[m, :, lanes(q)] for m in highs], axis=0)
            for t in range(2):
                outs = [2 * (i * group + g) + t for g in range(group)]
                at = [slice(m * rows, m * rows + rows) for m in outs]
                c = jnp.concatenate([cos_ref[level, k, :] for k in at], axis=0)
                s = jnp.concatenate([sin_ref[level, k, :] for k in at], axis=0)
                for q, tile in enumerate(step(nv, low, high, c, s, w, last)):
                    for g, m in enumerate(outs):
                        part = tile[g * rows : g * rows + rows]
                        if last:
                            put(m, q, part)
                        else:
                            dst[m, :, lanes(q)] = part
            if last:
                sent(i)


def levels_lo_kernel(
    nv, x_ref, cos, sin, w, out_ref, one, two, cos_v, sin_v, w_v, sems, x_sems, stage, out_sems
):
    lanes = lambda q: slice(q * 128, q * 128 + 128)

    def first(i):
        a = (i & 1) * 8 + (i >> 1) * 4
        return slice(a, a + 4), [a, a + 1], [a + 2, a + 3]

    def put(slab, q, tile):
        for kp in range(8):
            stage[rev(kp, 3), slab * 8 : slab * 8 + 8, lanes(q)] = tile[kp * 8 : kp * 8 + 8]

    def leave(i):
        rows = slice(i * 32, i * 32 + 32)
        return pltpu.make_async_copy(
            stage.at[:, rows, :], out_ref.at[:, rows, :], out_sems.at[i]
        )

    levels_kernel(
        nv, 4, 16, first, put, (cos, sin, w), (cos_v, sin_v, w_v), sems,
        x_ref, (one, two), x_sems, lambda i: leave(i).start(),
    )
    for i in range(4):
        leave(i).wait()


def levels_hi_kernel(
    nv, where_ref, x_ref, cos, sin, w, out_ref, one, two, cos_v, sin_v, w_v, sems, x_sems,
    stage, out_sems, done,
):
    ncv = 2 * nv

    def first(i):
        a = rev(i, 2) * 2
        return slice(a, a + 2), [a], [a + 1]

    def put(slab, q, tile):
        done[slab * 128 : slab * 128 + 128, q, :] = tile

    levels_kernel(
        nv, 3, 8, first, put, (cos, sin, w), (cos_v, sin_v, w_v), sems,
        x_ref, (one, two), x_sems, lambda i: None,
    )

    def leave(i):
        part = slice(i * 32, i * 32 + 32)
        return pltpu.make_async_copy(stage.at[part], out_ref.at[part], out_sems.at[i])

    for i in range(4):

        def gather(e, _):
            for r in range(8):
                stage[e, r * ncv : r * ncv + ncv, :] = done[where_ref[e * 8 + r]]
            return 0

        lax.fori_loop(i * 32, i * 32 + 32, gather, 0)
        leave(i).start()
    for i in range(4):
        leave(i).wait()


def held(count):
    return [
        pltpu.VMEM((count, 1024, 128), F32),
        pltpu.VMEM((count, 1024, 128), F32),
        pltpu.VMEM((count, 256, 256), BF16),
        pltpu.SemaphoreType.DMA((3, count)),
        pltpu.SemaphoreType.DMA((4,)),
    ]


def table_shapes(count):
    shape = jax.ShapeDtypeStruct
    return [shape((count, 1024, 128), F32)] * 2 + [shape((count, 256, 256), BF16)]


def shards(coefficients, angle_in, angle_out, interp, destination):
    nv = 2
    ncv = 2 * nv
    shape = jax.ShapeDtypeStruct
    sends = pl.pallas_call(
        pack_y_kernel,
        out_shape=[shape((96, w), F32) for w in (256, 768, 256)],
        in_specs=[HBM, HBM],
        out_specs=[VMEM] * 3,
        scratch_shapes=[pltpu.SemaphoreType.DMA((2, 4))],
        compiler_params=params(BIG),
    )(angle_in, angle_out)
    from_y = [
        lax.ppermute(s, "y", [(i, i ^ m) for i in range(4)]) for m, s in zip((1, 2, 3), sends)
    ]

    state = pl.pallas_call(
        functools.partial(send_kernel, nv),
        out_shape=shape((16, 64, ncv * 128), F32),
        in_specs=[VMEM],
        out_specs=VMEM,
        scratch_shapes=[pltpu.VMEM((8, 512, 128), F32)],
        compiler_params=params(6),
    )(coefficients.reshape(512, 1024))
    state, *from_y = lax.optimization_barrier((state, *from_y))
    state = lax.all_to_all(state, ("y", "zh", "c"), 0, 0, tiled=True)

    sends = pl.pallas_call(
        pack_x_kernel,
        out_shape=[shape((96, w), F32) for w in (256, 768, 256)],
        in_specs=[HBM, HBM],
        out_specs=[VMEM] * 3,
        scratch_shapes=[pltpu.SemaphoreType.DMA((2, 4))],
        compiler_params=params(BIG),
    )(angle_in, angle_out)
    from_x = [
        lax.ppermute(s, "x", [(i, i ^ m) for i in range(4)]) for m, s in zip((1, 2, 3), sends)
    ]
    kept, sent = pl.pallas_call(
        core_kernel,
        out_shape=[shape((96, 1536), F32)] * 2,
        in_specs=[HBM, HBM] + [VMEM] * 3,
        out_specs=[VMEM] * 2,
        scratch_shapes=[pltpu.SemaphoreType.DMA((2, 6))],
        compiler_params=params(BIG),
    )(angle_in, angle_out, *from_y)
    other = lax.ppermute(sent, "c", [(0, 1), (1, 0)])

    tables_lo = pl.pallas_call(
        table_lo_kernel,
        out_shape=table_shapes(4),
        in_specs=[HBM, HBM] + [VMEM] * 3,
        out_specs=[ANY, ANY, VMEM],
        scratch_shapes=[
            pltpu.VMEM((4, 1024, 128), F32),
            pltpu.VMEM((1024, 128), F32),
            pltpu.VMEM((96, 1024), F32),
            pltpu.SemaphoreType.DMA((2, 1)),
        ]
        + [pltpu.VMEM((4, 1024, 128), F32)] * 2
        + [pltpu.SemaphoreType.DMA((2, 4))],
        compiler_params=params(BIG),
    )(angle_in, angle_out, interp, kept, other)
    first, *from_x = lax.optimization_barrier((tables_lo[0], *from_x))
    tables_lo = [first, *tables_lo[1:]]
    tables_hi = pl.pallas_call(
        table_hi_kernel,
        out_shape=table_shapes(3),
        in_specs=[HBM, HBM] + [VMEM] * 4,
        out_specs=[ANY, ANY, VMEM],
        scratch_shapes=[
            pltpu.VMEM((3, 1024, 128), F32),
            pltpu.VMEM((1024, 128), F32),
            pltpu.VMEM((96, 1792), F32),
            pltpu.SemaphoreType.DMA((2, 3)),
        ]
        + [pltpu.VMEM((3, 1024, 128), F32)] * 2
        + [pltpu.SemaphoreType.DMA((2, 3))],
        compiler_params=params(BIG),
    )(angle_in, angle_out, interp, *from_x)

    state = pl.pallas_call(
        functools.partial(levels_lo_kernel, nv),
        out_shape=shape((8, 128, ncv * 128), F32),
        in_specs=[ANY] * 4,
        out_specs=ANY,
        scratch_shapes=[pltpu.VMEM((16, 64, ncv * 128), F32)] * 2
        + held(4)
        + [pltpu.VMEM((8, 128, ncv * 128), F32), pltpu.SemaphoreType.DMA((4,))],
        compiler_params=params(BIG),
    )(state, *tables_lo)
    wanted = destination[0]
    where = (wanted & 7) * 128 + (wanted >> 3 & 15) * 8 + (wanted >> 7)
    state, where, *tables_hi = lax.optimization_barrier((state, where, *tables_hi))
    state = lax.all_to_all(state, ("x", "zl"), 0, 0, tiled=True)

    state = pl.pallas_call(
        functools.partial(levels_hi_kernel, nv),
        out_shape=shape((128, 8 * ncv, 128), F32),
        in_specs=[SMEM] + [ANY] * 4,
        out_specs=ANY,
        scratch_shapes=[pltpu.VMEM((8, 128, ncv * 128), F32)] * 2
        + held(3)
        + [
            pltpu.VMEM((128, 8 * ncv, 128), F32),
            pltpu.SemaphoreType.DMA((4,)),
            pltpu.VMEM((1024, ncv, 128), F32),
        ],
        compiler_params=params(BIG),
    )(where, state, *tables_hi)
    state = lax.all_to_all(state, AXES, 0, 0, tiled=True)

    out = pl.pallas_call(
        functools.partial(final_kernel, nv),
        out_shape=shape((512, 1024), F32),
        in_specs=[VMEM],
        out_specs=ANY,
        scratch_shapes=[pltpu.VMEM((8, 512, 128), F32), pltpu.SemaphoreType.DMA((8,))],
        compiler_params=params(6),
    )(state.reshape(1024 * ncv, 128))
    return out.reshape(2, 32, 8, 1024)


def solution(mesh):
    mesh = jax.sharding.Mesh(mesh.devices.reshape(4, 2, 4, 2, 2), AXES)
    placed = (
        P(None, None, None, AXES),
        P(None, None, AXES),
        P(None, None, AXES),
        P(),
        P(AXES, None),
    )
    return jax.shard_map(
        shards,
        mesh=mesh,
        in_specs=placed,
        out_specs=P(None, None, None, AXES),
        check_vma=False,
    )
```

```python
import functools

import jax
import jax.numpy as jnp
from jax import lax
from jax.experimental import pallas as pl
from jax.experimental.pallas import tpu as pltpu
from jax.sharding import PartitionSpec as P

F32 = jnp.float32
BF16 = jnp.bfloat16
VMEM = pl.BlockSpec(memory_space=pltpu.VMEM)
SMEM = pl.BlockSpec(memory_space=pltpu.SMEM)
ANY = pl.BlockSpec(memory_space=pl.ANY)
HBM = pl.BlockSpec(memory_space=pltpu.HBM)
AXES = ("y", "zh", "x", "zl", "c")
PI = 3.141592653589793
TAU = 6.283185307179586

SIN = (
    0.9999996039252741,
    -0.1666655344642713,
    0.008332407591595805,
    -0.00019808739967677424,
    2.699822692004479e-06,
    -2.036622659870151e-08,
)
COS = (
    0.999999989116818,
    -0.49999989185961996,
    0.04166649020175043,
    -0.0013887807832168462,
    2.476996623505445e-05,
    -2.70797756302502e-07,
    1.724760753325688e-09,
)
MIB = 1024 * 1024
BIG = 30
PAD = 72


def params(mib):
    return pltpu.CompilerParams(vmem_limit_bytes=mib * MIB)


def rev(value, bits):
    out = 0
    for i in range(bits):
        out = out | ((value >> i & 1) << (bits - 1 - i))
    return out


def horner(coefs, u):
    acc = jnp.full_like(u, coefs[-1])
    for c in reversed(coefs[:-1]):
        acc = acc * u + c
    return acc


def sincos(x):
    u = x * x
    return x * horner(SIN, u), horner(COS, u)


def dot(a, b, dims=((1,), (0,))):
    return lax.dot_general(a, b, (dims, ((), ())), preferred_element_type=F32)


def split(x):
    hi = x.astype(BF16)
    return hi, (x - hi.astype(F32)).astype(BF16)


def send_kernel(nv, x_ref, out_ref, columns):
    for kt in range(8):
        columns[kt] = x_ref[:, kt * 128 : kt * 128 + 128]
        for c in range(2):
            for v in range(nv):
                part = columns[kt, pl.ds(c * 256 + v, 128, stride=2), :].T
                lanes = slice((c * nv + v) * 128, (c * nv + v) * 128 + 128)
                for core in range(2):
                    out_ref[rev(kt, 3) * 2 + core, :, lanes] = part[core * 64 : core * 64 + 64]


def final_kernel(nv, x_ref, out_ref, columns, sems):
    ncv = 2 * nv

    def leave(kt):
        lanes = slice(kt * 128, kt * 128 + 128)
        return pltpu.make_async_copy(columns.at[kt], out_ref.at[:, lanes], sems.at[kt])

    for kt in range(8):
        for c in range(2):
            for v in range(nv):
                cv = c * nv + v
                part = x_ref[pl.ds(kt * 128 * ncv + cv, 128, stride=ncv), :]
                columns[kt, pl.ds(c * 256 + v, 128, stride=2), :] = part.T
        leave(kt).start()
    for kt in range(8):
        leave(kt).wait()


def fetch(jobs, sems):
    copies = []
    for i, (ain, aout, level, start, width, dst, at) in enumerate(jobs):
        cols = pl.ds(pl.multiple_of(start, 128), width)
        copies.append(
            pltpu.make_async_copy(
                ain.at[level, :, cols], dst.at[0:64, at : at + width], sems.at[0, i]
            )
        )
        copies.append(
            pltpu.make_async_copy(
                aout.at[level, :, cols], dst.at[64:96, at : at + width], sems.at[1, i]
            )
        )
    for copy in copies:
        copy.start()
    for copy in copies:
        copy.wait()


def pack_y_kernel(ain, aout, y1, y2, y3, sems):
    y = lax.axis_index("y")
    ry = rev(y, 2)
    jobs = [(ain, aout, 1, ((y >> 1) ^ 1) * 512, 512, y2, 256)]
    for m, dst in ((2, y2), (1, y1), (3, y3)):
        jobs.append((ain, aout, 0, (ry ^ rev(m, 2)) * 256, 256, dst, 0))
    fetch(jobs, sems)


def pack_x_kernel(ain, aout, x1, x2, x3, sems):
    x = lax.axis_index("x")
    rx = rev(x, 2)
    jobs = [(ain, aout, 5, ((x >> 1) ^ 1) * 512, 512, x2, 256)]
    for m, dst in ((2, x2), (1, x1), (3, x3)):
        jobs.append((ain, aout, 4, (rx ^ rev(m, 2)) * 256, 256, dst, 0))
    fetch(jobs, sems)


def core_kernel(ain, aout, y1, y2, y3, kept, sent, sems):
    y = lax.axis_index("y")
    core = lax.axis_index("c")
    ry = rev(y, 2)
    jobs = []
    for dst, side in ((kept, core), (sent, 1 - core)):
        jobs.append((ain, aout, 0, ry * 256 + side * 128, 128, dst, 0))
        jobs.append((ain, aout, 1, (y >> 1) * 512 + side * 256, 256, dst, 512))
        jobs.append((ain, aout, 2, side * 512, 512, dst, 1024))
    fetch(jobs, sems)
    for dst, side in ((kept, core), (sent, 1 - core)):
        for m, src in ((1, y1), (2, y2), (3, y3)):
            cols = pl.ds(pl.multiple_of(side * 128, 128), 128)
            dst[:, m * 128 : m * 128 + 128] = src[:, cols]
        cols = pl.ds(pl.multiple_of(256 + side * 256, 128), 256)
        dst[:, 768:1024] = y2[:, cols]


def turned(read, scratch, width):
    for t in range(width // 128):
        part = read(slice(t * 128, t * 128 + 128))
        full = jnp.concatenate([part, jnp.zeros((32, 128), F32)], axis=0)
        scratch[t * 128 : t * 128 + 128, :] = full.T


def got(ref, at):
    return lambda s: ref[:, at + s.start : at + s.stop]


def weights(interp_ref, w_ref, first, count):
    row = lax.broadcasted_iota(jnp.int32, (256, 64), 0)
    col = lax.broadcasted_iota(jnp.int32, (256, 64), 1)
    left = ((row >> 2) == col).astype(F32).astype(BF16)
    row = lax.broadcasted_iota(jnp.int32, (32, 128), 0)
    col = lax.broadcasted_iota(jnp.int32, (32, 128), 1)
    right = (row == (col >> 2)).astype(F32).astype(BF16)
    row = lax.broadcasted_iota(jnp.int32, (256, 128), 0)
    col = lax.broadcasted_iota(jnp.int32, (256, 128), 1)
    keep = (row & 3) == (col & 3)
    for level in range(count):
        for i, part in enumerate(split(interp_ref[first + level])):
            mid = dot(left, part, ((1,), (1,))).astype(BF16)
            full = jnp.where(keep, dot(mid, right), 0.0)
            w_ref[level, :, i * 128 : i * 128 + 128] = full.astype(BF16)


def tables(count, slabs, raw, tab_ref, tab_v, sems):
    rows = 1024 // slabs
    lane = lax.broadcasted_iota(jnp.int32, (rows, 128), 1)

    def leave(level):
        return pltpu.make_async_copy(tab_v.at[level], tab_ref.at[level], sems.at[level])

    for level in range(count):

        def body(m, _):
            low = pl.ds(pl.multiple_of(m * rows, rows), rows)
            high = pl.ds(pl.multiple_of((m + slabs // 2) * rows, rows), rows)
            if level:
                before = jnp.where(
                    lane < 32,
                    pltpu.roll(raw[level - 1, low, :], 64, 1),
                    pltpu.roll(raw[level - 1, high, :], 96, 1),
                )
                before = jnp.where(lane < 64, before, 0.0)
            for t in range(2):
                at = pl.ds(pl.multiple_of((2 * m + t) * rows, rows), rows)
                angle = raw[level, at, :]
                if level:
                    angle = angle + before
                    turn = jnp.where(angle > PI, TAU, jnp.where(angle < -PI, -TAU, 0.0))
                    angle = angle - turn
                s, c = sincos(angle)
                tab_v[level, at, :] = jnp.where(lane < 64, c, pltpu.roll(s, 64, 1))
                if level == count - 1:
                    out = jnp.where(lane < 32, pltpu.roll(c, 64, 1), pltpu.roll(s, 96, 1))
                    tab_v[count, at, :] = out
            return 0

        lax.fori_loop(0, slabs // 2, body, 0, unroll=2)
        leave(level).start()
    leave(count).start()
    for level in range(count + 1):
        leave(level).wait()


def table_lo_kernel(
    ain, aout, interp, kept, other, tab_ref, w_ref, raw, scratch, mine, sems,
    tab_v, out_sems,
):
    y = lax.axis_index("y")
    core = lax.axis_index("c")
    ry = rev(y, 2)
    fetch([(ain, aout, 3, 0, 1024, mine, 0)], sems)
    weights(interp, w_ref, 0, 4)

    def emit(level, base, ts):
        for t in range(ts):
            at = pl.multiple_of((base + t) * 64, 64)
            raw[level, pl.ds(at, 64), :] = scratch[pl.ds(t, 64, stride=ts), :]

    for src, side in ((kept, core), (other, 1 - core)):
        for m in range(4):
            turned(got(src, m * 128), scratch, 128)
            emit(0, ((ry ^ rev(m, 2)) * 2 + side) * 2, 2)
        for m in range(2):
            turned(got(src, 512 + m * 256), scratch, 256)
            emit(1, (((y >> 1) ^ m) * 2 + side) * 4, 4)
        turned(got(src, 1024), scratch, 512)
        emit(2, side * 8, 8)
    turned(got(mine, 0), scratch, 1024)
    emit(3, 0, 16)
    tables(4, 16, raw, tab_ref, tab_v, out_sems)


def table_hi_kernel(
    ain, aout, interp, x1, x2, x3, tab_ref, w_ref, raw, scratch, mine, sems,
    tab_v, out_sems,
):
    x = lax.axis_index("x")
    rx = rev(x, 2)
    fetch(
        [
            (ain, aout, 4, rx * 256, 256, mine, 0),
            (ain, aout, 5, (x >> 1) * 512, 512, mine, 256),
            (ain, aout, 6, 0, 1024, mine, 768),
        ],
        sems,
    )
    weights(interp, w_ref, 4, 3)

    def emit(level, base, ts):
        for t in range(ts):
            for T in range(16):
                at = pl.multiple_of((base + t) * 128 + T * 8, 8)
                raw[level, pl.ds(at, 8), :] = scratch[pl.ds(T * ts + t, 8, stride=16 * ts), :]

    for m, src in enumerate((None, x1, x2, x3)):
        read = got(mine, 0) if m == 0 else got(src, 0)
        turned(read, scratch, 256)
        emit(0, (rx ^ rev(m, 2)) * 2, 2)
    turned(got(mine, 256), scratch, 512)
    emit(1, (x >> 1) * 4, 4)
    turned(got(x2, 256), scratch, 512)
    emit(1, (1 - (x >> 1)) * 4, 4)
    turned(got(mine, 768), scratch, 1024)
    emit(2, 0, 8)
    tables(3, 8, raw, tab_ref, tab_v, out_sems)


def spread(table, first):
    lane = lax.broadcasted_iota(jnp.int32, table.shape, 1)
    return jnp.take_along_axis(table, first + (lane >> 2), axis=1)


def step(nv, low, high, table, w, after):
    n = table.shape[0]
    sides = []
    for kind, src in enumerate((low, high)):
        c = spread(table, kind * 32)
        s = spread(table, kind * 32 + 64)
        re, im = [], []
        for v in range(nv):
            xr = src(v)
            xi = src(nv + v)
            re.append(xr * c - xi * s)
            im.append(xr * s + xi * c)
        sides.append(jnp.concatenate(re + im, axis=0))
    hi, lo = split(jnp.concatenate(sides, axis=1))
    first = dot(hi, w)
    out = first[:, :128] + first[:, 128:] + dot(lo, w[:, :128])
    out = [out[q * n : q * n + n] for q in range(2 * nv)]
    if after is None:
        return out
    c = spread(after, 0)
    s = spread(after, 32)
    re = [out[v] * c - out[nv + v] * s for v in range(nv)]
    im = [out[v] * s + out[nv + v] * c for v in range(nv)]
    return re + im


def levels_kernel(nv, count, slabs, first, put, sources, held, sems, x_ref, bufs):
    rows = 1024 // slabs
    group = 128 // rows
    bodies = slabs // 2 // group
    lanes = lambda q: slice(q * 128, q * 128 + 128)
    one, two = bufs

    tab_ref, w_ref = held

    def copies(level):
        got = [(0, level), (1, level)] if level < count else [(0, count)]
        return [
            pltpu.make_async_copy(
                sources[i].at[k], held[i].at[k], sems.at[i, k]
            )
            for i, k in got
        ]

    for copy in copies(0):
        copy.start()
    for level in range(count):
        for copy in copies(level):
            copy.wait()
        for copy in copies(level + 1):
            copy.start()
        if level == count - 1:
            for copy in copies(count):
                copy.wait()
        last = level == count - 1
        src = bufs[(level + 1) % 2] if level else x_ref
        dst = bufs[level % 2]
        w = w_ref[level]
        for i in range(bodies):
            if level == 0:
                lows, highs = first(i)
            else:
                lows = [i * group + g for g in range(group)]
                highs = [m + slabs // 2 for m in lows]
            low = lambda q: jnp.concatenate([src[m, :, lanes(q)] for m in lows], axis=0)
            high = lambda q: jnp.concatenate([src[m, :, lanes(q)] for m in highs], axis=0)
            for t in range(2):
                outs = [2 * (i * group + g) + t for g in range(group)]
                at = [slice(m * rows, m * rows + rows) for m in outs]
                read = lambda k: jnp.concatenate([tab_ref[k, r, :] for r in at], axis=0)
                after = read(count) if last else None
                for q, tile in enumerate(step(nv, low, high, read(level), w, after)):
                    for g, m in enumerate(outs):
                        part = tile[g * rows : g * rows + rows]
                        if last:
                            put(m, q, part)
                        else:
                            dst[m, :, lanes(q)] = part


def levels_lo_kernel(nv, x_ref, tab, w, out_ref, one, two, tab_v, w_v, sems):
    def first(i):
        a = (i & 1) * 8 + (i >> 1) * 4
        return [a, a + 1], [a + 2, a + 3]

    def put(slab, q, tile):
        for kp in range(8):
            rows = slice(slab * 8, slab * 8 + 8)
            out_ref[rev(kp, 3), rows, q * 128 : q * 128 + 128] = tile[kp * 8 : kp * 8 + 8]

    levels_kernel(
        nv, 4, 16, first, put, (tab, w), (tab_v, w_v), sems, x_ref, (one, two)
    )


def levels_hi_kernel(nv, where_ref, x_ref, tab, w, out_ref, one, two, tab_v, w_v, sems, done):
    ncv = 2 * nv

    def first(i):
        a = rev(i, 2) * 2
        return [a], [a + 1]

    def put(slab, q, tile):
        done[slab * 128 : slab * 128 + 128, q, :] = tile

    levels_kernel(
        nv, 3, 8, first, put, (tab, w), (tab_v, w_v), sems, x_ref, (one, two)
    )

    def gather(e, _):
        for r in range(8):
            out_ref[e, r * ncv : r * ncv + ncv, :] = done[where_ref[e * 8 + r]]
        return 0

    lax.fori_loop(0, 128, gather, 0, unroll=2)


def held(count):
    return [
        pltpu.VMEM((count + 1, 1024, 128), F32),
        pltpu.VMEM((count, 256, 256), BF16),
        pltpu.SemaphoreType.DMA((2, count + 1)),
    ]


def table_shapes(count):
    shape = jax.ShapeDtypeStruct
    return [shape((PAD, 1024, 128), F32), shape((count, 256, 256), BF16)]


def shards(coefficients, angle_in, angle_out, interp, destination):
    nv = 2
    ncv = 2 * nv
    shape = jax.ShapeDtypeStruct
    sends = pl.pallas_call(
        pack_y_kernel,
        out_shape=[shape((96, w), F32) for w in (256, 768, 256)],
        in_specs=[HBM, HBM],
        out_specs=[VMEM] * 3,
        scratch_shapes=[pltpu.SemaphoreType.DMA((2, 4))],
        compiler_params=params(56),
    )(angle_in, angle_out)
    from_y = [
        lax.ppermute(s, "y", [(i, i ^ m) for i in range(4)]) for m, s in zip((1, 2, 3), sends)
    ]

    state = pl.pallas_call(
        functools.partial(send_kernel, nv),
        out_shape=shape((16, 64, ncv * 128), F32),
        in_specs=[VMEM],
        out_specs=VMEM,
        scratch_shapes=[pltpu.VMEM((8, 512, 128), F32)],
        compiler_params=params(6),
    )(coefficients.reshape(512, 1024))
    state, *from_y = lax.optimization_barrier((state, *from_y))
    state = lax.all_to_all(state, ("y", "zh", "c"), 0, 0, tiled=True)

    sends = pl.pallas_call(
        pack_x_kernel,
        out_shape=[shape((96, w), F32) for w in (256, 768, 256)],
        in_specs=[HBM, HBM],
        out_specs=[VMEM] * 3,
        scratch_shapes=[pltpu.SemaphoreType.DMA((2, 4))],
        compiler_params=params(BIG),
    )(angle_in, angle_out)
    from_x = [
        lax.ppermute(s, "x", [(i, i ^ m) for i in range(4)]) for m, s in zip((1, 2, 3), sends)
    ]
    kept, sent = pl.pallas_call(
        core_kernel,
        out_shape=[shape((96, 1536), F32)] * 2,
        in_specs=[HBM, HBM] + [VMEM] * 3,
        out_specs=[VMEM] * 2,
        scratch_shapes=[pltpu.SemaphoreType.DMA((2, 6))],
        compiler_params=params(BIG),
    )(angle_in, angle_out, *from_y)
    other = lax.ppermute(sent, "c", [(0, 1), (1, 0)])

    tables_lo = pl.pallas_call(
        table_lo_kernel,
        out_shape=table_shapes(4),
        in_specs=[HBM, HBM] + [VMEM] * 3,
        out_specs=[ANY, VMEM],
        scratch_shapes=[
            pltpu.VMEM((4, 1024, 128), F32),
            pltpu.VMEM((1024, 128), F32),
            pltpu.VMEM((96, 1024), F32),
            pltpu.SemaphoreType.DMA((2, 1)),
        ]
        + [pltpu.VMEM((5, 1024, 128), F32), pltpu.SemaphoreType.DMA((5,))],
        compiler_params=params(BIG),
    )(angle_in, angle_out, interp, kept, other)
    first, *from_x = lax.optimization_barrier((tables_lo[0], *from_x))
    tables_lo = [first, *tables_lo[1:]]
    tables_hi = pl.pallas_call(
        table_hi_kernel,
        out_shape=table_shapes(3),
        in_specs=[HBM, HBM] + [VMEM] * 4,
        out_specs=[ANY, VMEM],
        scratch_shapes=[
            pltpu.VMEM((3, 1024, 128), F32),
            pltpu.VMEM((1024, 128), F32),
            pltpu.VMEM((96, 1792), F32),
            pltpu.SemaphoreType.DMA((2, 3)),
        ]
        + [pltpu.VMEM((4, 1024, 128), F32), pltpu.SemaphoreType.DMA((4,))],
        compiler_params=params(BIG),
    )(angle_in, angle_out, interp, *from_x)

    state = pl.pallas_call(
        functools.partial(levels_lo_kernel, nv),
        out_shape=shape((8, 128, ncv * 128), F32),
        in_specs=[VMEM, ANY, ANY],
        out_specs=VMEM,
        scratch_shapes=[pltpu.VMEM((16, 64, ncv * 128), F32)] * 2 + held(4),
        compiler_params=params(BIG),
    )(state, *tables_lo)
    wanted = destination[0]
    where = (wanted & 7) * 128 + (wanted >> 3 & 15) * 8 + (wanted >> 7)
    state, where, *tables_hi = lax.optimization_barrier((state, where, *tables_hi))
    state = lax.all_to_all(state, ("x", "zl"), 0, 0, tiled=True)

    state = pl.pallas_call(
        functools.partial(levels_hi_kernel, nv),
        out_shape=shape((128, 8 * ncv, 128), F32),
        in_specs=[SMEM, VMEM, ANY, ANY],
        out_specs=VMEM,
        scratch_shapes=[pltpu.VMEM((8, 128, ncv * 128), F32)] * 2
        + held(3)
        + [pltpu.VMEM((1024, ncv, 128), F32)],
        compiler_params=params(BIG),
    )(where, state, *tables_hi)
    state = lax.all_to_all(state, AXES, 0, 0, tiled=True)

    out = pl.pallas_call(
        functools.partial(final_kernel, nv),
        out_shape=shape((512, 1024), F32),
        in_specs=[VMEM],
        out_specs=ANY,
        scratch_shapes=[pltpu.VMEM((8, 512, 128), F32), pltpu.SemaphoreType.DMA((8,))],
        compiler_params=params(6),
    )(state.reshape(1024 * ncv, 128))
    return out.reshape(2, 32, 8, 1024)


def solution(mesh):
    mesh = jax.sharding.Mesh(mesh.devices.reshape(4, 2, 4, 2, 2), AXES)
    placed = (
        P(None, None, None, AXES),
        P(None, None, AXES),
        P(None, None, AXES),
        P(),
        P(AXES, None),
    )
    return jax.shard_map(
        shards,
        mesh=mesh,
        in_specs=placed,
        out_specs=P(None, None, None, AXES),
        check_vma=False,
    )
```

```python
import functools

import jax
import jax.numpy as jnp
from jax import lax
from jax.experimental import pallas as pl
from jax.experimental.pallas import tpu as pltpu
from jax.sharding import PartitionSpec as P

F32 = jnp.float32
BF16 = jnp.bfloat16
VMEM = pl.BlockSpec(memory_space=pltpu.VMEM)
SMEM = pl.BlockSpec(memory_space=pltpu.SMEM)
ANY = pl.BlockSpec(memory_space=pl.ANY)
HBM = pl.BlockSpec(memory_space=pltpu.HBM)
AXES = ("y", "zh", "x", "zl", "c")
PI = 3.141592653589793
TAU = 6.283185307179586

SIN = (
    0.9999996039252741,
    -0.1666655344642713,
    0.008332407591595805,
    -0.00019808739967677424,
    2.699822692004479e-06,
    -2.036622659870151e-08,
)
COS = (
    0.999999989116818,
    -0.49999989185961996,
    0.04166649020175043,
    -0.0013887807832168462,
    2.476996623505445e-05,
    -2.70797756302502e-07,
    1.724760753325688e-09,
)
MIB = 1024 * 1024
BIG = 30
PAD = 72


def params(mib):
    return pltpu.CompilerParams(vmem_limit_bytes=mib * MIB)


def rev(value, bits):
    out = 0
    for i in range(bits):
        out = out | ((value >> i & 1) << (bits - 1 - i))
    return out


def horner(coefs, u):
    acc = jnp.full_like(u, coefs[-1])
    for c in reversed(coefs[:-1]):
        acc = acc * u + c
    return acc


def sincos(x):
    u = x * x
    return x * horner(SIN, u), horner(COS, u)


def dot(a, b, dims=((1,), (0,))):
    return lax.dot_general(a, b, (dims, ((), ())), preferred_element_type=F32)


def split(x):
    hi = x.astype(BF16)
    return hi, (x - hi.astype(F32)).astype(BF16)


def send_kernel(nv, x_ref, out_ref, columns):
    for kt in range(8):
        columns[kt] = x_ref[:, kt * 128 : kt * 128 + 128]
        for c in range(2):
            for v in range(nv):
                part = columns[kt, pl.ds(c * 256 + v, 128, stride=2), :].T
                lanes = slice((c * nv + v) * 128, (c * nv + v) * 128 + 128)
                for core in range(2):
                    out_ref[rev(kt, 3) * 2 + core, :, lanes] = part[core * 64 : core * 64 + 64]


def final_kernel(nv, x_ref, out_ref, columns, sems):
    ncv = 2 * nv

    def leave(kt):
        lanes = slice(kt * 128, kt * 128 + 128)
        return pltpu.make_async_copy(columns.at[kt], out_ref.at[:, lanes], sems.at[kt])

    for kt in range(8):
        for c in range(2):
            for v in range(nv):
                cv = c * nv + v
                part = x_ref[pl.ds(kt * 128 * ncv + cv, 128, stride=ncv), :]
                columns[kt, pl.ds(c * 256 + v, 128, stride=2), :] = part.T
        leave(kt).start()
    for kt in range(8):
        leave(kt).wait()


def fetch(jobs, sems):
    copies = []
    for i, (ain, aout, level, start, width, dst, at) in enumerate(jobs):
        cols = pl.ds(pl.multiple_of(start, 128), width)
        copies.append(
            pltpu.make_async_copy(
                ain.at[level, :, cols], dst.at[0:64, at : at + width], sems.at[0, i]
            )
        )
        copies.append(
            pltpu.make_async_copy(
                aout.at[level, :, cols], dst.at[64:96, at : at + width], sems.at[1, i]
            )
        )
    for copy in copies:
        copy.start()
    for copy in copies:
        copy.wait()


def pack_y_kernel(ain, aout, y1, y2, y3, sems):
    y = lax.axis_index("y")
    ry = rev(y, 2)
    jobs = [(ain, aout, 1, ((y >> 1) ^ 1) * 512, 512, y2, 256)]
    for m, dst in ((2, y2), (1, y1), (3, y3)):
        jobs.append((ain, aout, 0, (ry ^ rev(m, 2)) * 256, 256, dst, 0))
    fetch(jobs, sems)


def pack_x_kernel(ain, aout, x1, x2, x3, sems):
    x = lax.axis_index("x")
    rx = rev(x, 2)
    jobs = [(ain, aout, 5, ((x >> 1) ^ 1) * 512, 512, x2, 256)]
    for m, dst in ((2, x2), (1, x1), (3, x3)):
        jobs.append((ain, aout, 4, (rx ^ rev(m, 2)) * 256, 256, dst, 0))
    fetch(jobs, sems)


def core_kernel(ain, aout, y1, y2, y3, kept, sent, sems):
    y = lax.axis_index("y")
    core = lax.axis_index("c")
    ry = rev(y, 2)
    jobs = []
    for dst, side in ((kept, core), (sent, 1 - core)):
        jobs.append((ain, aout, 0, ry * 256 + side * 128, 128, dst, 0))
        jobs.append((ain, aout, 1, (y >> 1) * 512 + side * 256, 256, dst, 512))
        jobs.append((ain, aout, 2, side * 512, 512, dst, 1024))
    fetch(jobs, sems)
    for dst, side in ((kept, core), (sent, 1 - core)):
        for m, src in ((1, y1), (2, y2), (3, y3)):
            cols = pl.ds(pl.multiple_of(side * 128, 128), 128)
            dst[:, m * 128 : m * 128 + 128] = src[:, cols]
        cols = pl.ds(pl.multiple_of(256 + side * 256, 128), 256)
        dst[:, 768:1024] = y2[:, cols]


def turned(read, scratch, width):
    for t in range(width // 128):
        part = read(slice(t * 128, t * 128 + 128))
        full = jnp.concatenate([part, jnp.zeros((32, 128), F32)], axis=0)
        scratch[t * 128 : t * 128 + 128, :] = full.T


def got(ref, at):
    return lambda s: ref[:, at + s.start : at + s.stop]


def weights(interp_ref, w_ref, first, count):
    row = lax.broadcasted_iota(jnp.int32, (256, 64), 0)
    col = lax.broadcasted_iota(jnp.int32, (256, 64), 1)
    left = ((row >> 2) == col).astype(F32).astype(BF16)
    row = lax.broadcasted_iota(jnp.int32, (32, 128), 0)
    col = lax.broadcasted_iota(jnp.int32, (32, 128), 1)
    right = (row == (col >> 2)).astype(F32).astype(BF16)
    row = lax.broadcasted_iota(jnp.int32, (256, 128), 0)
    col = lax.broadcasted_iota(jnp.int32, (256, 128), 1)
    keep = (row & 3) == (col & 3)
    for level in range(count):
        for i, part in enumerate(split(interp_ref[first + level])):
            mid = dot(left, part, ((1,), (1,))).astype(BF16)
            full = jnp.where(keep, dot(mid, right), 0.0)
            w_ref[level, :, i * 128 : i * 128 + 128] = full.astype(BF16)


def tables(count, slabs, raw, tab_ref, tab_v, sems):
    rows = 1024 // slabs
    lane = lax.broadcasted_iota(jnp.int32, (rows, 128), 1)

    def leave(level):
        return pltpu.make_async_copy(tab_v.at[level], tab_ref.at[level], sems.at[level])

    for level in range(count):

        def body(m, _):
            low = pl.ds(pl.multiple_of(m * rows, rows), rows)
            high = pl.ds(pl.multiple_of((m + slabs // 2) * rows, rows), rows)
            if level:
                before = jnp.where(
                    lane < 32,
                    pltpu.roll(raw[level - 1, low, :], 64, 1),
                    pltpu.roll(raw[level - 1, high, :], 96, 1),
                )
                before = jnp.where(lane < 64, before, 0.0)
            for t in range(2):
                at = pl.ds(pl.multiple_of((2 * m + t) * rows, rows), rows)
                angle = raw[level, at, :]
                if level:
                    angle = angle + before
                    turn = jnp.where(angle > PI, TAU, jnp.where(angle < -PI, -TAU, 0.0))
                    angle = angle - turn
                s, c = sincos(angle)
                tab_v[level, at, :] = jnp.where(lane < 64, c, pltpu.roll(s, 64, 1))
                if level == count - 1:
                    out = jnp.where(lane < 32, pltpu.roll(c, 64, 1), pltpu.roll(s, 96, 1))
                    tab_v[count, at, :] = out
            return 0

        lax.fori_loop(0, slabs // 2, body, 0, unroll=2)
        leave(level).start()
    leave(count).start()
    for level in range(count + 1):
        leave(level).wait()


def table_lo_kernel(
    ain, aout, interp, kept, other, tab_ref, w_ref, raw, scratch, mine, sems,
    tab_v, out_sems,
):
    y = lax.axis_index("y")
    core = lax.axis_index("c")
    ry = rev(y, 2)
    fetch([(ain, aout, 3, 0, 1024, mine, 0)], sems)
    weights(interp, w_ref, 0, 4)

    def emit(level, base, ts):
        for t in range(ts):
            at = pl.multiple_of((base + t) * 64, 64)
            raw[level, pl.ds(at, 64), :] = scratch[pl.ds(t, 64, stride=ts), :]

    for src, side in ((kept, core), (other, 1 - core)):
        for m in range(4):
            turned(got(src, m * 128), scratch, 128)
            emit(0, ((ry ^ rev(m, 2)) * 2 + side) * 2, 2)
        for m in range(2):
            turned(got(src, 512 + m * 256), scratch, 256)
            emit(1, (((y >> 1) ^ m) * 2 + side) * 4, 4)
        turned(got(src, 1024), scratch, 512)
        emit(2, side * 8, 8)
    turned(got(mine, 0), scratch, 1024)
    emit(3, 0, 16)
    tables(4, 16, raw, tab_ref, tab_v, out_sems)


def table_hi_kernel(
    ain, aout, interp, x1, x2, x3, tab_ref, w_ref, raw, scratch, mine, sems,
    tab_v, out_sems,
):
    x = lax.axis_index("x")
    rx = rev(x, 2)
    fetch(
        [
            (ain, aout, 4, rx * 256, 256, mine, 0),
            (ain, aout, 5, (x >> 1) * 512, 512, mine, 256),
            (ain, aout, 6, 0, 1024, mine, 768),
        ],
        sems,
    )
    weights(interp, w_ref, 4, 3)

    def emit(level, base, ts):
        for t in range(ts):
            for T in range(16):
                at = pl.multiple_of((base + t) * 128 + T * 8, 8)
                raw[level, pl.ds(at, 8), :] = scratch[pl.ds(T * ts + t, 8, stride=16 * ts), :]

    for m, src in enumerate((None, x1, x2, x3)):
        read = got(mine, 0) if m == 0 else got(src, 0)
        turned(read, scratch, 256)
        emit(0, (rx ^ rev(m, 2)) * 2, 2)
    turned(got(mine, 256), scratch, 512)
    emit(1, (x >> 1) * 4, 4)
    turned(got(x2, 256), scratch, 512)
    emit(1, (1 - (x >> 1)) * 4, 4)
    turned(got(mine, 768), scratch, 1024)
    emit(2, 0, 8)
    tables(3, 8, raw, tab_ref, tab_v, out_sems)


def spread(table, first):
    lane = lax.broadcasted_iota(jnp.int32, table.shape, 1)
    return jnp.take_along_axis(table, first + (lane >> 2), axis=1)


def step(nv, low, high, table, w, after):
    n = table.shape[0]
    sides = []
    for kind, src in enumerate((low, high)):
        c = spread(table, kind * 32)
        s = spread(table, kind * 32 + 64)
        re, im = [], []
        for v in range(nv):
            xr = src(v)
            xi = src(nv + v)
            re.append(xr * c - xi * s)
            im.append(xr * s + xi * c)
        sides.append(jnp.concatenate(re + im, axis=0))
    hi, lo = split(jnp.concatenate(sides, axis=1))
    first = dot(hi, w)
    out = first[:, :128] + first[:, 128:] + dot(lo, w[:, :128])
    out = [out[q * n : q * n + n] for q in range(2 * nv)]
    if after is None:
        return out
    c = spread(after, 0)
    s = spread(after, 32)
    re = [out[v] * c - out[nv + v] * s for v in range(nv)]
    im = [out[v] * s + out[nv + v] * c for v in range(nv)]
    return re + im


def levels_kernel(nv, count, slabs, first, put, x_ref, bufs, tab_ref, w_ref, ready, arrived):
    rows = 1024 // slabs
    group = 128 // rows
    lanes = lambda q: slice(q * 128, q * 128 + 128)
    for level in range(count):
        ready(level)
        last = level == count - 1
        src = bufs[(level + 1) % 2] if level else x_ref
        dst = bufs[level % 2]
        w = w_ref[level]
        for i in range(slabs // 2 // group):
            if level == 0:
                arrived(i)
                lows, highs = first(i)
            else:
                lows = [i * group + g for g in range(group)]
                highs = [m + slabs // 2 for m in lows]
            low = lambda q: jnp.concatenate([src[m, :, lanes(q)] for m in lows], axis=0)
            high = lambda q: jnp.concatenate([src[m, :, lanes(q)] for m in highs], axis=0)
            for t in range(2):
                outs = [2 * (i * group + g) + t for g in range(group)]
                at = [slice(m * rows, m * rows + rows) for m in outs]
                read = lambda k: jnp.concatenate([tab_ref[k, r, :] for r in at], axis=0)
                after = read(count) if last else None
                for q, tile in enumerate(step(nv, low, high, read(level), w, after)):
                    for g, m in enumerate(outs):
                        part = tile[g * rows : g * rows + rows]
                        if last:
                            put(m, q, part)
                        else:
                            dst[m, :, lanes(q)] = part


def levels_lo_kernel(nv, x_ref, tab, w, out_ref, one, two, tab_v, w_v, sems, x_sems):
    def first(i):
        a = (i & 1) * 8 + (i >> 1) * 4
        return [a, a + 1], [a + 2, a + 3]

    def put(slab, q, tile):
        for kp in range(8):
            rows = slice(slab * 8, slab * 8 + 8)
            out_ref[rev(kp, 3), rows, q * 128 : q * 128 + 128] = tile[kp * 8 : kp * 8 + 8]

    def arrive(i):
        at = first(i)[0][0]
        part = slice(at, at + 4)
        return pltpu.make_async_copy(x_ref.at[part], two.at[part], x_sems.at[i])

    def copies(level):
        got = [(tab, tab_v, 0, level)]
        if level < 4:
            got.append((w, w_v, 1, level))
        return [
            pltpu.make_async_copy(src.at[k], dst.at[k], sems.at[i, k]) for src, dst, i, k in got
        ]

    def ready(level):
        for copy in copies(level) + (copies(4) if level == 3 else []):
            copy.wait()

    arrive(0).start()
    for copy in copies(0):
        copy.start()
    for i in range(1, 4):
        arrive(i).start()
    for level in range(1, 5):
        for copy in copies(level):
            copy.start()
    levels_kernel(
        nv, 4, 16, first, put, two, (one, two), tab_v, w_v, ready, lambda i: arrive(i).wait()
    )


def levels_hi_kernel(nv, where_ref, x_ref, tab, w, out_ref, one, two, done):
    ncv = 2 * nv

    def first(i):
        a = rev(i, 2) * 2
        return [a], [a + 1]

    def put(slab, q, tile):
        done[slab * 128 : slab * 128 + 128, q, :] = tile

    nothing = lambda k: None
    levels_kernel(nv, 3, 8, first, put, x_ref, (one, two), tab, w, nothing, nothing)

    def gather(e, _):
        for r in range(8):
            out_ref[e, r * ncv : r * ncv + ncv, :] = done[where_ref[e * 8 + r]]
        return 0

    lax.fori_loop(0, 128, gather, 0, unroll=2)


def table_shapes(count, rows):
    shape = jax.ShapeDtypeStruct
    return [shape((rows, 1024, 128), F32), shape((count, 256, 256), BF16)]


def shards(coefficients, angle_in, angle_out, interp, destination):
    nv = 2
    ncv = 2 * nv
    shape = jax.ShapeDtypeStruct
    sends = pl.pallas_call(
        pack_y_kernel,
        out_shape=[shape((96, w), F32) for w in (256, 768, 256)],
        in_specs=[HBM, HBM],
        out_specs=[VMEM] * 3,
        scratch_shapes=[pltpu.SemaphoreType.DMA((2, 4))],
        compiler_params=params(56),
    )(angle_in, angle_out)
    coefficients, *sends = lax.optimization_barrier((coefficients, *sends))
    from_y = [
        lax.ppermute(s, "y", [(i, i ^ m) for i in range(4)]) for m, s in zip((1, 2, 3), sends)
    ]

    state = pl.pallas_call(
        functools.partial(send_kernel, nv),
        out_shape=shape((16, 64, ncv * 128), F32),
        in_specs=[VMEM],
        out_specs=VMEM,
        scratch_shapes=[pltpu.VMEM((8, 512, 128), F32)],
        compiler_params=params(6),
    )(coefficients.reshape(512, 1024))
    state = lax.all_to_all(state, ("y", "zh", "c"), 0, 0, tiled=True)

    sends = pl.pallas_call(
        pack_x_kernel,
        out_shape=[shape((96, w), F32) for w in (256, 768, 256)],
        in_specs=[HBM, HBM],
        out_specs=[VMEM] * 3,
        scratch_shapes=[pltpu.SemaphoreType.DMA((2, 4))],
        compiler_params=params(BIG),
    )(angle_in, angle_out)
    from_x = [
        lax.ppermute(s, "x", [(i, i ^ m) for i in range(4)]) for m, s in zip((1, 2, 3), sends)
    ]
    kept, sent = pl.pallas_call(
        core_kernel,
        out_shape=[shape((96, 1536), F32)] * 2,
        in_specs=[HBM, HBM] + [VMEM] * 3,
        out_specs=[VMEM] * 2,
        scratch_shapes=[pltpu.SemaphoreType.DMA((2, 6))],
        compiler_params=params(BIG),
    )(angle_in, angle_out, *from_y)
    other = lax.ppermute(sent, "c", [(0, 1), (1, 0)])

    tables_lo = pl.pallas_call(
        table_lo_kernel,
        out_shape=table_shapes(4, PAD),
        in_specs=[HBM, HBM] + [VMEM] * 3,
        out_specs=[ANY, VMEM],
        scratch_shapes=[
            pltpu.VMEM((4, 1024, 128), F32),
            pltpu.VMEM((1024, 128), F32),
            pltpu.VMEM((96, 1024), F32),
            pltpu.SemaphoreType.DMA((2, 1)),
        ]
        + [pltpu.VMEM((5, 1024, 128), F32), pltpu.SemaphoreType.DMA((5,))],
        compiler_params=params(BIG),
    )(angle_in, angle_out, interp, kept, other)
    first, *from_x = lax.optimization_barrier((tables_lo[0], *from_x))
    tables_lo = [first, *tables_lo[1:]]
    tables_hi = pl.pallas_call(
        table_hi_kernel,
        out_shape=table_shapes(3, 4),
        in_specs=[HBM, HBM] + [VMEM] * 4,
        out_specs=[ANY, VMEM],
        scratch_shapes=[
            pltpu.VMEM((3, 1024, 128), F32),
            pltpu.VMEM((1024, 128), F32),
            pltpu.VMEM((96, 1792), F32),
            pltpu.SemaphoreType.DMA((2, 3)),
        ]
        + [pltpu.VMEM((4, 1024, 128), F32), pltpu.SemaphoreType.DMA((4,))],
        compiler_params=params(BIG),
    )(angle_in, angle_out, interp, *from_x)

    state = pl.pallas_call(
        functools.partial(levels_lo_kernel, nv),
        out_shape=shape((8, 128, ncv * 128), F32),
        in_specs=[ANY, ANY, ANY],
        out_specs=VMEM,
        scratch_shapes=[pltpu.VMEM((16, 64, ncv * 128), F32)] * 2
        + [
            pltpu.VMEM((5, 1024, 128), F32),
            pltpu.VMEM((4, 256, 256), BF16),
            pltpu.SemaphoreType.DMA((2, 5)),
            pltpu.SemaphoreType.DMA((4,)),
        ],
        compiler_params=params(BIG),
    )(state, *tables_lo)
    wanted = destination[0]
    where = (wanted & 7) * 128 + (wanted >> 3 & 15) * 8 + (wanted >> 7)
    state, where, *tables_hi = lax.optimization_barrier((state, where, *tables_hi))
    state = lax.all_to_all(state, ("x", "zl"), 0, 0, tiled=True)

    state = pl.pallas_call(
        functools.partial(levels_hi_kernel, nv),
        out_shape=shape((128, 8 * ncv, 128), F32),
        in_specs=[SMEM] + [VMEM] * 3,
        out_specs=VMEM,
        scratch_shapes=[pltpu.VMEM((8, 128, ncv * 128), F32)] * 2
        + [pltpu.VMEM((1024, ncv, 128), F32)],
        compiler_params=params(BIG),
    )(where, state, *tables_hi)
    state = lax.all_to_all(state, AXES, 0, 0, tiled=True)

    out = pl.pallas_call(
        functools.partial(final_kernel, nv),
        out_shape=shape((512, 1024), F32),
        in_specs=[VMEM],
        out_specs=ANY,
        scratch_shapes=[pltpu.VMEM((8, 512, 128), F32), pltpu.SemaphoreType.DMA((8,))],
        compiler_params=params(6),
    )(state.reshape(1024 * ncv, 128))
    return out.reshape(2, 32, 8, 1024)


def solution(mesh):
    mesh = jax.sharding.Mesh(mesh.devices.reshape(4, 2, 4, 2, 2), AXES)
    placed = (
        P(None, None, None, AXES),
        P(None, None, AXES),
        P(None, None, AXES),
        P(),
        P(AXES, None),
    )
    return jax.shard_map(
        shards,
        mesh=mesh,
        in_specs=placed,
        out_specs=P(None, None, None, AXES),
        check_vma=False,
    )
```

```python
import functools

import jax
import jax.numpy as jnp
from jax import lax
from jax.experimental import pallas as pl
from jax.experimental.pallas import tpu as pltpu
from jax.sharding import PartitionSpec as P

F32 = jnp.float32
BF16 = jnp.bfloat16
VMEM = pl.BlockSpec(memory_space=pltpu.VMEM)
SMEM = pl.BlockSpec(memory_space=pltpu.SMEM)
ANY = pl.BlockSpec(memory_space=pl.ANY)
HBM = pl.BlockSpec(memory_space=pltpu.HBM)
AXES = ("y", "zh", "x", "zl", "c")
PI = 3.141592653589793
TAU = 6.283185307179586

SIN = (
    0.9999996039252741,
    -0.1666655344642713,
    0.008332407591595805,
    -0.00019808739967677424,
    2.699822692004479e-06,
    -2.036622659870151e-08,
)
COS = (
    0.999999989116818,
    -0.49999989185961996,
    0.04166649020175043,
    -0.0013887807832168462,
    2.476996623505445e-05,
    -2.70797756302502e-07,
    1.724760753325688e-09,
)
MIB = 1024 * 1024
BIG = 30
PAD = 72


def params(mib):
    return pltpu.CompilerParams(vmem_limit_bytes=mib * MIB)


def rev(value, bits):
    out = 0
    for i in range(bits):
        out = out | ((value >> i & 1) << (bits - 1 - i))
    return out


def horner(coefs, u):
    acc = jnp.full_like(u, coefs[-1])
    for c in reversed(coefs[:-1]):
        acc = acc * u + c
    return acc


def sincos(x):
    u = x * x
    return x * horner(SIN, u), horner(COS, u)


def dot(a, b, dims=((1,), (0,))):
    return lax.dot_general(a, b, (dims, ((), ())), preferred_element_type=F32)


def split(x):
    hi = x.astype(BF16)
    return hi, (x - hi.astype(F32)).astype(BF16)


def send_kernel(nv, x_ref, out_ref, columns):
    for kt in range(8):
        columns[kt] = x_ref[:, kt * 128 : kt * 128 + 128]
        for c in range(2):
            for v in range(nv):
                part = columns[kt, pl.ds(c * 256 + v, 128, stride=2), :].T
                lanes = slice((c * nv + v) * 128, (c * nv + v) * 128 + 128)
                for core in range(2):
                    out_ref[rev(kt, 3) * 2 + core, :, lanes] = part[core * 64 : core * 64 + 64]


def final_kernel(nv, x_ref, out_ref, columns, sems):
    ncv = 2 * nv

    def leave(kt):
        lanes = slice(kt * 128, kt * 128 + 128)
        return pltpu.make_async_copy(columns.at[kt], out_ref.at[:, lanes], sems.at[kt])

    for kt in range(8):
        for c in range(2):
            for v in range(nv):
                cv = c * nv + v
                part = x_ref[pl.ds(kt * 128 * ncv + cv, 128, stride=ncv), :]
                columns[kt, pl.ds(c * 256 + v, 128, stride=2), :] = part.T
        leave(kt).start()
    for kt in range(8):
        leave(kt).wait()


def fetch(jobs, sems):
    copies = []
    for i, (ain, aout, level, start, width, dst, at) in enumerate(jobs):
        cols = pl.ds(pl.multiple_of(start, 128), width)
        copies.append(
            pltpu.make_async_copy(
                ain.at[level, :, cols], dst.at[0:64, at : at + width], sems.at[0, i]
            )
        )
        copies.append(
            pltpu.make_async_copy(
                aout.at[level, :, cols], dst.at[64:96, at : at + width], sems.at[1, i]
            )
        )
    for copy in copies:
        copy.start()
    for copy in copies:
        copy.wait()


def pack_y_kernel(ain, aout, y1, y2, y3, sems):
    y = lax.axis_index("y")
    ry = rev(y, 2)
    jobs = [(ain, aout, 1, ((y >> 1) ^ 1) * 512, 512, y2, 256)]
    for m, dst in ((2, y2), (1, y1), (3, y3)):
        jobs.append((ain, aout, 0, (ry ^ rev(m, 2)) * 256, 256, dst, 0))
    fetch(jobs, sems)


def pack_x_kernel(ain, aout, x1, x2, x3, sems):
    x = lax.axis_index("x")
    rx = rev(x, 2)
    jobs = [(ain, aout, 5, ((x >> 1) ^ 1) * 512, 512, x2, 256)]
    for m, dst in ((2, x2), (1, x1), (3, x3)):
        jobs.append((ain, aout, 4, (rx ^ rev(m, 2)) * 256, 256, dst, 0))
    fetch(jobs, sems)


def core_kernel(ain, aout, y1, y2, y3, kept, sent, sems):
    y = lax.axis_index("y")
    core = lax.axis_index("c")
    ry = rev(y, 2)
    jobs = []
    for dst, side in ((kept, core), (sent, 1 - core)):
        jobs.append((ain, aout, 0, ry * 256 + side * 128, 128, dst, 0))
        jobs.append((ain, aout, 1, (y >> 1) * 512 + side * 256, 256, dst, 512))
        jobs.append((ain, aout, 2, side * 512, 512, dst, 1024))
    fetch(jobs, sems)
    for dst, side in ((kept, core), (sent, 1 - core)):
        for m, src in ((1, y1), (2, y2), (3, y3)):
            cols = pl.ds(pl.multiple_of(side * 128, 128), 128)
            dst[:, m * 128 : m * 128 + 128] = src[:, cols]
        cols = pl.ds(pl.multiple_of(256 + side * 256, 128), 256)
        dst[:, 768:1024] = y2[:, cols]


def turned(read, scratch, width):
    for t in range(width // 128):
        part = read(slice(t * 128, t * 128 + 128))
        full = jnp.concatenate([part, jnp.zeros((32, 128), F32)], axis=0)
        scratch[t * 128 : t * 128 + 128, :] = full.T


def got(ref, at):
    return lambda s: ref[:, at + s.start : at + s.stop]


def weights(interp_ref, w_ref, first, count):
    row = lax.broadcasted_iota(jnp.int32, (256, 64), 0)
    col = lax.broadcasted_iota(jnp.int32, (256, 64), 1)
    left = ((row >> 2) == col).astype(F32).astype(BF16)
    row = lax.broadcasted_iota(jnp.int32, (32, 128), 0)
    col = lax.broadcasted_iota(jnp.int32, (32, 128), 1)
    right = (row == (col >> 2)).astype(F32).astype(BF16)
    row = lax.broadcasted_iota(jnp.int32, (256, 128), 0)
    col = lax.broadcasted_iota(jnp.int32, (256, 128), 1)
    keep = (row & 3) == (col & 3)
    for level in range(count):
        for i, part in enumerate(split(interp_ref[first + level])):
            mid = dot(left, part, ((1,), (1,))).astype(BF16)
            full = jnp.where(keep, dot(mid, right), 0.0)
            w_ref[level, :, i * 128 : i * 128 + 128] = full.astype(BF16)


def tables(count, slabs, raw, tab_ref, tab_v, sems):
    rows = 1024 // slabs
    lane = lax.broadcasted_iota(jnp.int32, (rows, 128), 1)

    def leave(level):
        return pltpu.make_async_copy(tab_v.at[level], tab_ref.at[level], sems.at[level])

    for level in range(count):

        def body(m, _):
            low = pl.ds(pl.multiple_of(m * rows, rows), rows)
            high = pl.ds(pl.multiple_of((m + slabs // 2) * rows, rows), rows)
            if level:
                before = jnp.where(
                    lane < 32,
                    pltpu.roll(raw[level - 1, low, :], 64, 1),
                    pltpu.roll(raw[level - 1, high, :], 96, 1),
                )
                before = jnp.where(lane < 64, before, 0.0)
            for t in range(2):
                at = pl.ds(pl.multiple_of((2 * m + t) * rows, rows), rows)
                angle = raw[level, at, :]
                if level:
                    angle = angle + before
                    turn = jnp.where(angle > PI, TAU, jnp.where(angle < -PI, -TAU, 0.0))
                    angle = angle - turn
                s, c = sincos(angle)
                tab_v[level, at, :] = jnp.where(lane < 64, c, pltpu.roll(s, 64, 1))
                if level == count - 1:
                    out = jnp.where(lane < 32, pltpu.roll(c, 64, 1), pltpu.roll(s, 96, 1))
                    tab_v[count, at, :] = out
            return 0

        lax.fori_loop(0, slabs // 2, body, 0, unroll=2)
        leave(level).start()
    leave(count).start()
    for level in range(count + 1):
        leave(level).wait()


def table_lo_kernel(
    ain, aout, interp, kept, other, tab_ref, w_ref, raw, scratch, mine, sems,
    tab_v, out_sems,
):
    y = lax.axis_index("y")
    core = lax.axis_index("c")
    ry = rev(y, 2)
    fetch([(ain, aout, 3, 0, 1024, mine, 0)], sems)
    weights(interp, w_ref, 0, 4)

    def emit(level, base, ts):
        for t in range(ts):
            at = pl.multiple_of((base + t) * 64, 64)
            raw[level, pl.ds(at, 64), :] = scratch[pl.ds(t, 64, stride=ts), :]

    for src, side in ((kept, core), (other, 1 - core)):
        for m in range(4):
            turned(got(src, m * 128), scratch, 128)
            emit(0, ((ry ^ rev(m, 2)) * 2 + side) * 2, 2)
        for m in range(2):
            turned(got(src, 512 + m * 256), scratch, 256)
            emit(1, (((y >> 1) ^ m) * 2 + side) * 4, 4)
        turned(got(src, 1024), scratch, 512)
        emit(2, side * 8, 8)
    turned(got(mine, 0), scratch, 1024)
    emit(3, 0, 16)
    tables(4, 16, raw, tab_ref, tab_v, out_sems)


def table_hi_kernel(
    ain, aout, interp, x1, x2, x3, tab_ref, w_ref, raw, scratch, mine, sems,
    tab_v, out_sems,
):
    x = lax.axis_index("x")
    rx = rev(x, 2)
    fetch(
        [
            (ain, aout, 4, rx * 256, 256, mine, 0),
            (ain, aout, 5, (x >> 1) * 512, 512, mine, 256),
            (ain, aout, 6, 0, 1024, mine, 768),
        ],
        sems,
    )
    weights(interp, w_ref, 4, 3)

    def emit(level, base, ts):
        for t in range(ts):
            for T in range(16):
                at = pl.multiple_of((base + t) * 128 + T * 8, 8)
                raw[level, pl.ds(at, 8), :] = scratch[pl.ds(T * ts + t, 8, stride=16 * ts), :]

    for m, src in enumerate((None, x1, x2, x3)):
        read = got(mine, 0) if m == 0 else got(src, 0)
        turned(read, scratch, 256)
        emit(0, (rx ^ rev(m, 2)) * 2, 2)
    turned(got(mine, 256), scratch, 512)
    emit(1, (x >> 1) * 4, 4)
    turned(got(x2, 256), scratch, 512)
    emit(1, (1 - (x >> 1)) * 4, 4)
    turned(got(mine, 768), scratch, 1024)
    emit(2, 0, 8)
    tables(3, 8, raw, tab_ref, tab_v, out_sems)


def spread(table, first):
    lane = lax.broadcasted_iota(jnp.int32, table.shape, 1)
    return jnp.take_along_axis(table, first + (lane >> 2), axis=1)


def step(nv, low, high, table, w, after):
    n = table.shape[0]
    sides = []
    for kind, src in enumerate((low, high)):
        c = spread(table, kind * 32)
        s = spread(table, kind * 32 + 64)
        re, im = [], []
        for v in range(nv):
            xr = src(v)
            xi = src(nv + v)
            re.append(xr * c - xi * s)
            im.append(xr * s + xi * c)
        sides.append(jnp.concatenate(re + im, axis=0))
    hi, lo = split(jnp.concatenate(sides, axis=1))
    first = dot(hi, w)
    out = first[:, :128] + first[:, 128:] + dot(lo, w[:, :128])
    out = [out[q * n : q * n + n] for q in range(2 * nv)]
    if after is None:
        return out
    c = spread(after, 0)
    s = spread(after, 32)
    re = [out[v] * c - out[nv + v] * s for v in range(nv)]
    im = [out[v] * s + out[nv + v] * c for v in range(nv)]
    return re + im


def levels_kernel(nv, count, slabs, first, put, x_ref, bufs, tab_ref, w_ref, ready):
    rows = 1024 // slabs
    group = 128 // rows
    lanes = lambda q: slice(q * 128, q * 128 + 128)
    for level in range(count):
        ready(level)
        last = level == count - 1
        src = bufs[(level + 1) % 2] if level else x_ref
        dst = bufs[level % 2]
        w = w_ref[level]
        for i in range(slabs // 2 // group):
            if level == 0:
                lows, highs = first(i)
            else:
                lows = [i * group + g for g in range(group)]
                highs = [m + slabs // 2 for m in lows]
            low = lambda q: jnp.concatenate([src[m, :, lanes(q)] for m in lows], axis=0)
            high = lambda q: jnp.concatenate([src[m, :, lanes(q)] for m in highs], axis=0)
            for t in range(2):
                outs = [2 * (i * group + g) + t for g in range(group)]
                at = [slice(m * rows, m * rows + rows) for m in outs]
                read = lambda k: jnp.concatenate([tab_ref[k, r, :] for r in at], axis=0)
                after = read(count) if last else None
                for q, tile in enumerate(step(nv, low, high, read(level), w, after)):
                    for g, m in enumerate(outs):
                        part = tile[g * rows : g * rows + rows]
                        if last:
                            put(m, q, part)
                        else:
                            dst[m, :, lanes(q)] = part


def levels_lo_kernel(nv, x_ref, tab, w, out_ref, one, two, tab_v, w_v, sems):
    def first(i):
        a = (i & 1) * 8 + (i >> 1) * 4
        return [a, a + 1], [a + 2, a + 3]

    def put(slab, q, tile):
        for kp in range(8):
            rows = slice(slab * 8, slab * 8 + 8)
            out_ref[rev(kp, 3), rows, q * 128 : q * 128 + 128] = tile[kp * 8 : kp * 8 + 8]

    begin = [
        pltpu.make_async_copy(tab.at[0], tab_v.at[0], sems.at[0]),
        pltpu.make_async_copy(w, w_v, sems.at[1]),
        pltpu.make_async_copy(x_ref, two, sems.at[2]),
    ]
    rest = [pltpu.make_async_copy(tab.at[1:5], tab_v.at[1:5], sems.at[3])]

    def ready(level):
        for copy in (begin, rest, [], [])[level]:
            copy.wait()

    for copy in begin + rest:
        copy.start()
    levels_kernel(
        nv, 4, 16, first, put, two, (one, two), tab_v, w_v, ready
    )


def levels_hi_kernel(nv, where_ref, x_ref, tab, w, out_ref, one, two, done):
    ncv = 2 * nv

    def first(i):
        a = rev(i, 2) * 2
        return [a], [a + 1]

    def put(slab, q, tile):
        done[slab * 128 : slab * 128 + 128, q, :] = tile

    levels_kernel(nv, 3, 8, first, put, x_ref, (one, two), tab, w, lambda level: None)

    def gather(e, _):
        for r in range(8):
            out_ref[e, r * ncv : r * ncv + ncv, :] = done[where_ref[e * 8 + r]]
        return 0

    lax.fori_loop(0, 128, gather, 0, unroll=2)


def table_shapes(count, rows):
    shape = jax.ShapeDtypeStruct
    return [shape((rows, 1024, 128), F32), shape((count, 256, 256), BF16)]


def shards(coefficients, angle_in, angle_out, interp, destination):
    nv = 2
    ncv = 2 * nv
    shape = jax.ShapeDtypeStruct
    sends = pl.pallas_call(
        pack_y_kernel,
        out_shape=[shape((96, w), F32) for w in (256, 768, 256)],
        in_specs=[HBM, HBM],
        out_specs=[VMEM] * 3,
        scratch_shapes=[pltpu.SemaphoreType.DMA((2, 4))],
        compiler_params=params(56),
    )(angle_in, angle_out)
    from_y = [
        lax.ppermute(s, "y", [(i, i ^ m) for i in range(4)]) for m, s in zip((1, 2, 3), sends)
    ]

    state = pl.pallas_call(
        functools.partial(send_kernel, nv),
        out_shape=shape((16, 64, ncv * 128), F32),
        in_specs=[VMEM],
        out_specs=VMEM,
        scratch_shapes=[pltpu.VMEM((8, 512, 128), F32)],
        compiler_params=params(6),
    )(coefficients.reshape(512, 1024))
    state, *from_y = lax.optimization_barrier((state, *from_y))
    state = lax.all_to_all(state, ("y", "zh", "c"), 0, 0, tiled=True)

    sends = pl.pallas_call(
        pack_x_kernel,
        out_shape=[shape((96, w), F32) for w in (256, 768, 256)],
        in_specs=[HBM, HBM],
        out_specs=[VMEM] * 3,
        scratch_shapes=[pltpu.SemaphoreType.DMA((2, 4))],
        compiler_params=params(BIG),
    )(angle_in, angle_out)
    from_x = [
        lax.ppermute(s, "x", [(i, i ^ m) for i in range(4)]) for m, s in zip((1, 2, 3), sends)
    ]
    kept, sent = pl.pallas_call(
        core_kernel,
        out_shape=[shape((96, 1536), F32)] * 2,
        in_specs=[HBM, HBM] + [VMEM] * 3,
        out_specs=[VMEM] * 2,
        scratch_shapes=[pltpu.SemaphoreType.DMA((2, 6))],
        compiler_params=params(BIG),
    )(angle_in, angle_out, *from_y)
    other = lax.ppermute(sent, "c", [(0, 1), (1, 0)])

    tables_lo = pl.pallas_call(
        table_lo_kernel,
        out_shape=table_shapes(4, PAD),
        in_specs=[HBM, HBM] + [VMEM] * 3,
        out_specs=[ANY, VMEM],
        scratch_shapes=[
            pltpu.VMEM((4, 1024, 128), F32),
            pltpu.VMEM((1024, 128), F32),
            pltpu.VMEM((96, 1024), F32),
            pltpu.SemaphoreType.DMA((2, 1)),
        ]
        + [pltpu.VMEM((5, 1024, 128), F32), pltpu.SemaphoreType.DMA((5,))],
        compiler_params=params(BIG),
    )(angle_in, angle_out, interp, kept, other)
    first, *from_x = lax.optimization_barrier((tables_lo[0], *from_x))
    tables_lo = [first, *tables_lo[1:]]
    tables_hi = pl.pallas_call(
        table_hi_kernel,
        out_shape=table_shapes(3, 4),
        in_specs=[HBM, HBM] + [VMEM] * 4,
        out_specs=[ANY, VMEM],
        scratch_shapes=[
            pltpu.VMEM((3, 1024, 128), F32),
            pltpu.VMEM((1024, 128), F32),
            pltpu.VMEM((96, 1792), F32),
            pltpu.SemaphoreType.DMA((2, 3)),
        ]
        + [pltpu.VMEM((4, 1024, 128), F32), pltpu.SemaphoreType.DMA((4,))],
        compiler_params=params(BIG),
    )(angle_in, angle_out, interp, *from_x)

    state = pl.pallas_call(
        functools.partial(levels_lo_kernel, nv),
        out_shape=shape((8, 128, ncv * 128), F32),
        in_specs=[ANY, ANY, ANY],
        out_specs=VMEM,
        scratch_shapes=[pltpu.VMEM((16, 64, ncv * 128), F32)] * 2
        + [
            pltpu.VMEM((5, 1024, 128), F32),
            pltpu.VMEM((4, 256, 256), BF16),
            pltpu.SemaphoreType.DMA((4,)),
        ],
        compiler_params=params(BIG),
    )(state, *tables_lo)
    wanted = destination[0]
    where = (wanted & 7) * 128 + (wanted >> 3 & 15) * 8 + (wanted >> 7)
    state, where, *tables_hi = lax.optimization_barrier((state, where, *tables_hi))
    state = lax.all_to_all(state, ("x", "zl"), 0, 0, tiled=True)

    state = pl.pallas_call(
        functools.partial(levels_hi_kernel, nv),
        out_shape=shape((128, 8 * ncv, 128), F32),
        in_specs=[SMEM] + [VMEM] * 3,
        out_specs=VMEM,
        scratch_shapes=[pltpu.VMEM((8, 128, ncv * 128), F32)] * 2
        + [pltpu.VMEM((1024, ncv, 128), F32)],
        compiler_params=params(BIG),
    )(where, state, *tables_hi)
    state = lax.all_to_all(state, AXES, 0, 0, tiled=True)

    out = pl.pallas_call(
        functools.partial(final_kernel, nv),
        out_shape=shape((512, 1024), F32),
        in_specs=[VMEM],
        out_specs=ANY,
        scratch_shapes=[pltpu.VMEM((8, 512, 128), F32), pltpu.SemaphoreType.DMA((8,))],
        compiler_params=params(6),
    )(state.reshape(1024 * ncv, 128))
    return out.reshape(2, 32, 8, 1024)


def solution(mesh):
    mesh = jax.sharding.Mesh(mesh.devices.reshape(4, 2, 4, 2, 2), AXES)
    placed = (
        P(None, None, None, AXES),
        P(None, None, AXES),
        P(None, None, AXES),
        P(),
        P(AXES, None),
    )
    return jax.shard_map(
        shards,
        mesh=mesh,
        in_specs=placed,
        out_specs=P(None, None, None, AXES),
        check_vma=False,
    )
```

```python
import functools

import jax
import jax.numpy as jnp
from jax import lax
from jax.experimental import pallas as pl
from jax.experimental.pallas import tpu as pltpu
from jax.sharding import PartitionSpec as P

F32 = jnp.float32
BF16 = jnp.bfloat16
VMEM = pl.BlockSpec(memory_space=pltpu.VMEM)
SMEM = pl.BlockSpec(memory_space=pltpu.SMEM)
ANY = pl.BlockSpec(memory_space=pl.ANY)
HBM = pl.BlockSpec(memory_space=pltpu.HBM)
AXES = ("y", "zh", "x", "zl", "c")
PI = 3.141592653589793
TAU = 6.283185307179586

SIN = (
    0.9999996039252741,
    -0.1666655344642713,
    0.008332407591595805,
    -0.00019808739967677424,
    2.699822692004479e-06,
    -2.036622659870151e-08,
)
COS = (
    0.999999989116818,
    -0.49999989185961996,
    0.04166649020175043,
    -0.0013887807832168462,
    2.476996623505445e-05,
    -2.70797756302502e-07,
    1.724760753325688e-09,
)
MIB = 1024 * 1024
BIG = 30
PAD = 72


def params(mib):
    return pltpu.CompilerParams(vmem_limit_bytes=mib * MIB)


def rev(value, bits):
    out = 0
    for i in range(bits):
        out = out | ((value >> i & 1) << (bits - 1 - i))
    return out


def horner(coefs, u):
    acc = jnp.full_like(u, coefs[-1])
    for c in reversed(coefs[:-1]):
        acc = acc * u + c
    return acc


def sincos(x):
    u = x * x
    return x * horner(SIN, u), horner(COS, u)


def dot(a, b, dims=((1,), (0,))):
    return lax.dot_general(a, b, (dims, ((), ())), preferred_element_type=F32)


def split(x):
    hi = x.astype(BF16)
    return hi, (x - hi.astype(F32)).astype(BF16)


def send_kernel(nv, x_ref, out_ref, columns):
    for kt in range(8):
        columns[kt] = x_ref[:, kt * 128 : kt * 128 + 128]
        for c in range(2):
            for v in range(nv):
                part = columns[kt, pl.ds(c * 256 + v, 128, stride=2), :].T
                lanes = slice((c * nv + v) * 128, (c * nv + v) * 128 + 128)
                for core in range(2):
                    out_ref[rev(kt, 3) * 2 + core, :, lanes] = part[core * 64 : core * 64 + 64]


def final_kernel(nv, x_ref, out_ref, columns, sems):
    ncv = 2 * nv

    def leave(kt):
        lanes = slice(kt * 128, kt * 128 + 128)
        return pltpu.make_async_copy(columns.at[kt], out_ref.at[:, lanes], sems.at[kt])

    for kt in range(8):
        for c in range(2):
            for v in range(nv):
                cv = c * nv + v
                part = x_ref[pl.ds(kt * 128 * ncv + cv, 128, stride=ncv), :]
                columns[kt, pl.ds(c * 256 + v, 128, stride=2), :] = part.T
        leave(kt).start()
    for kt in range(8):
        leave(kt).wait()


def fetch(jobs, sems):
    copies = []
    for i, (ain, aout, level, start, width, dst, at) in enumerate(jobs):
        cols = pl.ds(pl.multiple_of(start, 128), width)
        copies.append(
            pltpu.make_async_copy(
                ain.at[level, :, cols], dst.at[0:64, at : at + width], sems.at[0, i]
            )
        )
        copies.append(
            pltpu.make_async_copy(
                aout.at[level, :, cols], dst.at[64:96, at : at + width], sems.at[1, i]
            )
        )
    for copy in copies:
        copy.start()
    for copy in copies:
        copy.wait()


def pack_y_kernel(ain, aout, y1, y2, y3, sems):
    y = lax.axis_index("y")
    ry = rev(y, 2)
    jobs = [(ain, aout, 1, ((y >> 1) ^ 1) * 512, 512, y2, 256)]
    for m, dst in ((2, y2), (1, y1), (3, y3)):
        jobs.append((ain, aout, 0, (ry ^ rev(m, 2)) * 256, 256, dst, 0))
    fetch(jobs, sems)


def pack_x_kernel(ain, aout, x1, x2, x3, sems):
    x = lax.axis_index("x")
    rx = rev(x, 2)
    jobs = [(ain, aout, 5, ((x >> 1) ^ 1) * 512, 512, x2, 256)]
    for m, dst in ((2, x2), (1, x1), (3, x3)):
        jobs.append((ain, aout, 4, (rx ^ rev(m, 2)) * 256, 256, dst, 0))
    fetch(jobs, sems)


def core_kernel(ain, aout, y1, y2, y3, kept, sent, sems):
    y = lax.axis_index("y")
    core = lax.axis_index("c")
    ry = rev(y, 2)
    jobs = []
    for dst, side in ((kept, core), (sent, 1 - core)):
        jobs.append((ain, aout, 0, ry * 256 + side * 128, 128, dst, 0))
        jobs.append((ain, aout, 1, (y >> 1) * 512 + side * 256, 256, dst, 512))
        jobs.append((ain, aout, 2, side * 512, 512, dst, 1024))
    fetch(jobs, sems)
    for dst, side in ((kept, core), (sent, 1 - core)):
        for m, src in ((1, y1), (2, y2), (3, y3)):
            cols = pl.ds(pl.multiple_of(side * 128, 128), 128)
            dst[:, m * 128 : m * 128 + 128] = src[:, cols]
        cols = pl.ds(pl.multiple_of(256 + side * 256, 128), 256)
        dst[:, 768:1024] = y2[:, cols]


def turned(read, scratch, width):
    for t in range(width // 128):
        part = read(slice(t * 128, t * 128 + 128))
        full = jnp.concatenate([part, jnp.zeros((32, 128), F32)], axis=0)
        scratch[t * 128 : t * 128 + 128, :] = full.T


def got(ref, at):
    return lambda s: ref[:, at + s.start : at + s.stop]


def weights(interp_ref, w_ref, first, count):
    row = lax.broadcasted_iota(jnp.int32, (256, 64), 0)
    col = lax.broadcasted_iota(jnp.int32, (256, 64), 1)
    left = ((row >> 2) == col).astype(F32).astype(BF16)
    row = lax.broadcasted_iota(jnp.int32, (32, 128), 0)
    col = lax.broadcasted_iota(jnp.int32, (32, 128), 1)
    right = (row == (col >> 2)).astype(F32).astype(BF16)
    row = lax.broadcasted_iota(jnp.int32, (256, 128), 0)
    col = lax.broadcasted_iota(jnp.int32, (256, 128), 1)
    keep = (row & 3) == (col & 3)
    for level in range(count):
        for i, part in enumerate(split(interp_ref[first + level])):
            mid = dot(left, part, ((1,), (1,))).astype(BF16)
            full = jnp.where(keep, dot(mid, right), 0.0)
            w_ref[level, :, i * 128 : i * 128 + 128] = full.astype(BF16)


def tables(count, slabs, raw, tab_ref, tab_v, sems):
    rows = 1024 // slabs
    lane = lax.broadcasted_iota(jnp.int32, (rows, 128), 1)

    def leave(level):
        return pltpu.make_async_copy(tab_v.at[level], tab_ref.at[level], sems.at[level])

    for level in range(count):

        def body(m, _):
            low = pl.ds(pl.multiple_of(m * rows, rows), rows)
            high = pl.ds(pl.multiple_of((m + slabs // 2) * rows, rows), rows)
            if level:
                before = jnp.where(
                    lane < 32,
                    pltpu.roll(raw[level - 1, low, :], 64, 1),
                    pltpu.roll(raw[level - 1, high, :], 96, 1),
                )
                before = jnp.where(lane < 64, before, 0.0)
            for t in range(2):
                at = pl.ds(pl.multiple_of((2 * m + t) * rows, rows), rows)
                angle = raw[level, at, :]
                if level:
                    angle = angle + before
                    turn = jnp.where(angle > PI, TAU, jnp.where(angle < -PI, -TAU, 0.0))
                    angle = angle - turn
                s, c = sincos(angle)
                tab_v[level, at, :] = jnp.where(lane < 64, c, pltpu.roll(s, 64, 1))
                if level == count - 1:
                    out = jnp.where(lane < 32, pltpu.roll(c, 64, 1), pltpu.roll(s, 96, 1))
                    tab_v[count, at, :] = out
            return 0

        lax.fori_loop(0, slabs // 2, body, 0, unroll=2)
        leave(level).start()
    leave(count).start()
    for level in range(count + 1):
        leave(level).wait()


def table_lo_kernel(
    ain, aout, interp, kept, other, tab_ref, w_ref, raw, scratch, mine, sems,
    tab_v, out_sems,
):
    y = lax.axis_index("y")
    core = lax.axis_index("c")
    ry = rev(y, 2)
    fetch([(ain, aout, 3, 0, 1024, mine, 0)], sems)
    weights(interp, w_ref, 0, 4)

    def emit(level, base, ts):
        for t in range(ts):
            at = pl.multiple_of((base + t) * 64, 64)
            raw[level, pl.ds(at, 64), :] = scratch[pl.ds(t, 64, stride=ts), :]

    for src, side in ((kept, core), (other, 1 - core)):
        for m in range(4):
            turned(got(src, m * 128), scratch, 128)
            emit(0, ((ry ^ rev(m, 2)) * 2 + side) * 2, 2)
        for m in range(2):
            turned(got(src, 512 + m * 256), scratch, 256)
            emit(1, (((y >> 1) ^ m) * 2 + side) * 4, 4)
        turned(got(src, 1024), scratch, 512)
        emit(2, side * 8, 8)
    turned(got(mine, 0), scratch, 1024)
    emit(3, 0, 16)
    tables(4, 16, raw, tab_ref, tab_v, out_sems)


def table_hi_kernel(
    ain, aout, interp, x1, x2, x3, tab_ref, w_ref, raw, scratch, mine, sems,
    tab_v, out_sems,
):
    x = lax.axis_index("x")
    rx = rev(x, 2)
    fetch(
        [
            (ain, aout, 4, rx * 256, 256, mine, 0),
            (ain, aout, 5, (x >> 1) * 512, 512, mine, 256),
            (ain, aout, 6, 0, 1024, mine, 768),
        ],
        sems,
    )
    weights(interp, w_ref, 4, 3)

    def emit(level, base, ts):
        for t in range(ts):
            for T in range(16):
                at = pl.multiple_of((base + t) * 128 + T * 8, 8)
                raw[level, pl.ds(at, 8), :] = scratch[pl.ds(T * ts + t, 8, stride=16 * ts), :]

    for m, src in enumerate((None, x1, x2, x3)):
        read = got(mine, 0) if m == 0 else got(src, 0)
        turned(read, scratch, 256)
        emit(0, (rx ^ rev(m, 2)) * 2, 2)
    turned(got(mine, 256), scratch, 512)
    emit(1, (x >> 1) * 4, 4)
    turned(got(x2, 256), scratch, 512)
    emit(1, (1 - (x >> 1)) * 4, 4)
    turned(got(mine, 768), scratch, 1024)
    emit(2, 0, 8)
    tables(3, 8, raw, tab_ref, tab_v, out_sems)


def spread(table, first):
    lane = lax.broadcasted_iota(jnp.int32, table.shape, 1)
    return jnp.take_along_axis(table, first + (lane >> 2), axis=1)


def step(nv, low, high, table, w, after):
    n = table.shape[0]
    sides = []
    for kind, src in enumerate((low, high)):
        c = spread(table, kind * 32)
        s = spread(table, kind * 32 + 64)
        re, im = [], []
        for v in range(nv):
            xr = src(v)
            xi = src(nv + v)
            re.append(xr * c - xi * s)
            im.append(xr * s + xi * c)
        sides.append(jnp.concatenate(re + im, axis=0))
    hi, lo = split(jnp.concatenate(sides, axis=1))
    first = dot(hi, w)
    out = first[:, :128] + first[:, 128:] + dot(lo, w[:, :128])
    out = [out[q * n : q * n + n] for q in range(2 * nv)]
    if after is None:
        return out
    c = spread(after, 0)
    s = spread(after, 32)
    re = [out[v] * c - out[nv + v] * s for v in range(nv)]
    im = [out[v] * s + out[nv + v] * c for v in range(nv)]
    return re + im


def levels_kernel(nv, count, slabs, first, put, x_ref, bufs, tab_ref, w_ref, ready):
    rows = 1024 // slabs
    group = 128 // rows
    lanes = lambda q: slice(q * 128, q * 128 + 128)
    for level in range(count):
        ready(level)
        last = level == count - 1
        src = bufs[(level + 1) % 2] if level else x_ref
        dst = bufs[level % 2]
        w = w_ref[level]
        for i in range(slabs // 2 // group):
            if level == 0:
                lows, highs = first(i)
            else:
                lows = [i * group + g for g in range(group)]
                highs = [m + slabs // 2 for m in lows]
            low = lambda q: jnp.concatenate([src[m, :, lanes(q)] for m in lows], axis=0)
            high = lambda q: jnp.concatenate([src[m, :, lanes(q)] for m in highs], axis=0)
            for t in range(2):
                outs = [2 * (i * group + g) + t for g in range(group)]
                at = [slice(m * rows, m * rows + rows) for m in outs]
                read = lambda k: jnp.concatenate([tab_ref[k, r, :] for r in at], axis=0)
                after = read(count) if last else None
                for q, tile in enumerate(step(nv, low, high, read(level), w, after)):
                    for g, m in enumerate(outs):
                        part = tile[g * rows : g * rows + rows]
                        if last:
                            put(m, q, part)
                        else:
                            dst[m, :, lanes(q)] = part


def levels_lo_kernel(nv, x_ref, tab, w, out_ref, one, two, tab_v, w_v, sems):
    def first(i):
        a = (i & 1) * 8 + (i >> 1) * 4
        return [a, a + 1], [a + 2, a + 3]

    def put(slab, q, tile):
        for kp in range(8):
            rows = slice(slab * 8, slab * 8 + 8)
            out_ref[rev(kp, 3), rows, q * 128 : q * 128 + 128] = tile[kp * 8 : kp * 8 + 8]

    begin = [
        pltpu.make_async_copy(tab.at[0], tab_v.at[0], sems.at[0]),
        pltpu.make_async_copy(w, w_v, sems.at[1]),
        pltpu.make_async_copy(x_ref, two, sems.at[2]),
    ]
    rest = [pltpu.make_async_copy(tab.at[1:5], tab_v.at[1:5], sems.at[3])]

    def ready(level):
        for copy in (begin, rest, [], [])[level]:
            copy.wait()

    for copy in begin + rest:
        copy.start()
    levels_kernel(
        nv, 4, 16, first, put, two, (one, two), tab_v, w_v, ready
    )


def levels_hi_kernel(nv, where_ref, x_ref, tab, w, out_ref, one, two, done):
    ncv = 2 * nv

    def first(i):
        a = rev(i, 2) * 2
        return [a], [a + 1]

    def put(slab, q, tile):
        done[slab * 128 : slab * 128 + 128, q, :] = tile

    levels_kernel(nv, 3, 8, first, put, x_ref, (one, two), tab, w, lambda level: None)

    def gather(e, _):
        for r in range(8):
            out_ref[e, r * ncv : r * ncv + ncv, :] = done[where_ref[e * 8 + r]]
        return 0

    lax.fori_loop(0, 128, gather, 0, unroll=2)


def table_shapes(count, rows):
    shape = jax.ShapeDtypeStruct
    return [shape((rows, 1024, 128), F32), shape((count, 256, 256), BF16)]


def shards(coefficients, angle_in, angle_out, interp, destination):
    nv = 2
    ncv = 2 * nv
    shape = jax.ShapeDtypeStruct
    sends = pl.pallas_call(
        pack_y_kernel,
        out_shape=[shape((96, w), F32) for w in (256, 768, 256)],
        in_specs=[HBM, HBM],
        out_specs=[VMEM] * 3,
        scratch_shapes=[pltpu.SemaphoreType.DMA((2, 4))],
        compiler_params=params(60),
    )(angle_in, angle_out)
    from_y = [
        lax.ppermute(s, "y", [(i, i ^ m) for i in range(4)]) for m, s in zip((1, 2, 3), sends)
    ]

    state = pl.pallas_call(
        functools.partial(send_kernel, nv),
        out_shape=shape((16, 64, ncv * 128), F32),
        in_specs=[VMEM],
        out_specs=VMEM,
        scratch_shapes=[pltpu.VMEM((8, 512, 128), F32)],
        compiler_params=params(6),
    )(coefficients.reshape(512, 1024))
    state, from_y[0] = lax.optimization_barrier((state, from_y[0]))
    state = lax.all_to_all(state, ("y", "zh", "c"), 0, 0, tiled=True)

    sends = pl.pallas_call(
        pack_x_kernel,
        out_shape=[shape((96, w), F32) for w in (256, 768, 256)],
        in_specs=[HBM, HBM],
        out_specs=[VMEM] * 3,
        scratch_shapes=[pltpu.SemaphoreType.DMA((2, 4))],
        compiler_params=params(BIG),
    )(angle_in, angle_out)
    from_x = [
        lax.ppermute(s, "x", [(i, i ^ m) for i in range(4)]) for m, s in zip((1, 2, 3), sends)
    ]
    kept, sent = pl.pallas_call(
        core_kernel,
        out_shape=[shape((96, 1536), F32)] * 2,
        in_specs=[HBM, HBM] + [VMEM] * 3,
        out_specs=[VMEM] * 2,
        scratch_shapes=[pltpu.SemaphoreType.DMA((2, 6))],
        compiler_params=params(BIG),
    )(angle_in, angle_out, *from_y)
    other = lax.ppermute(sent, "c", [(0, 1), (1, 0)])

    tables_lo = pl.pallas_call(
        table_lo_kernel,
        out_shape=table_shapes(4, PAD),
        in_specs=[HBM, HBM] + [VMEM] * 3,
        out_specs=[ANY, VMEM],
        scratch_shapes=[
            pltpu.VMEM((4, 1024, 128), F32),
            pltpu.VMEM((1024, 128), F32),
            pltpu.VMEM((96, 1024), F32),
            pltpu.SemaphoreType.DMA((2, 1)),
        ]
        + [pltpu.VMEM((5, 1024, 128), F32), pltpu.SemaphoreType.DMA((5,))],
        compiler_params=params(BIG),
    )(angle_in, angle_out, interp, kept, other)
    first, *from_x = lax.optimization_barrier((tables_lo[0], *from_x))
    tables_lo = [first, *tables_lo[1:]]
    tables_hi = pl.pallas_call(
        table_hi_kernel,
        out_shape=table_shapes(3, 4),
        in_specs=[HBM, HBM] + [VMEM] * 4,
        out_specs=[ANY, VMEM],
        scratch_shapes=[
            pltpu.VMEM((3, 1024, 128), F32),
            pltpu.VMEM((1024, 128), F32),
            pltpu.VMEM((96, 1792), F32),
            pltpu.SemaphoreType.DMA((2, 3)),
        ]
        + [pltpu.VMEM((4, 1024, 128), F32), pltpu.SemaphoreType.DMA((4,))],
        compiler_params=params(BIG),
    )(angle_in, angle_out, interp, *from_x)

    state = pl.pallas_call(
        functools.partial(levels_lo_kernel, nv),
        out_shape=shape((8, 128, ncv * 128), F32),
        in_specs=[ANY, ANY, ANY],
        out_specs=VMEM,
        scratch_shapes=[pltpu.VMEM((16, 64, ncv * 128), F32)] * 2
        + [
            pltpu.VMEM((5, 1024, 128), F32),
            pltpu.VMEM((4, 256, 256), BF16),
            pltpu.SemaphoreType.DMA((4,)),
        ],
        compiler_params=params(BIG),
    )(state, *tables_lo)
    wanted = destination[0]
    where = (wanted & 7) * 128 + (wanted >> 3 & 15) * 8 + (wanted >> 7)
    state, where, *tables_hi = lax.optimization_barrier((state, where, *tables_hi))
    state = lax.all_to_all(state, ("x", "zl"), 0, 0, tiled=True)

    state = pl.pallas_call(
        functools.partial(levels_hi_kernel, nv),
        out_shape=shape((128, 8 * ncv, 128), F32),
        in_specs=[SMEM] + [VMEM] * 3,
        out_specs=VMEM,
        scratch_shapes=[pltpu.VMEM((8, 128, ncv * 128), F32)] * 2
        + [pltpu.VMEM((1024, ncv, 128), F32)],
        compiler_params=params(BIG),
    )(where, state, *tables_hi)
    state = lax.all_to_all(state, AXES, 0, 0, tiled=True)

    out = pl.pallas_call(
        functools.partial(final_kernel, nv),
        out_shape=shape((512, 1024), F32),
        in_specs=[VMEM],
        out_specs=ANY,
        scratch_shapes=[pltpu.VMEM((8, 512, 128), F32), pltpu.SemaphoreType.DMA((8,))],
        compiler_params=params(6),
    )(state.reshape(1024 * ncv, 128))
    return out.reshape(2, 32, 8, 1024)


def solution(mesh):
    mesh = jax.sharding.Mesh(mesh.devices.reshape(4, 2, 4, 2, 2), AXES)
    placed = (
        P(None, None, None, AXES),
        P(None, None, AXES),
        P(None, None, AXES),
        P(),
        P(AXES, None),
    )
    return jax.shard_map(
        shards,
        mesh=mesh,
        in_specs=placed,
        out_specs=P(None, None, None, AXES),
        check_vma=False,
    )
```

```python
import functools

import jax
import jax.numpy as jnp
from jax import lax
from jax.experimental import pallas as pl
from jax.experimental.pallas import tpu as pltpu
from jax.sharding import PartitionSpec as P

F32 = jnp.float32
BF16 = jnp.bfloat16
VMEM = pl.BlockSpec(memory_space=pltpu.VMEM)
SMEM = pl.BlockSpec(memory_space=pltpu.SMEM)
ANY = pl.BlockSpec(memory_space=pl.ANY)
HBM = pl.BlockSpec(memory_space=pltpu.HBM)
AXES = ("y1", "y0", "zh", "x1", "x0", "zl", "c")
Y = ("y1", "y0")
X = ("x1", "x0")
FIRST = ("y1", "y0", "zh", "c")
SECOND = ("zl", "x0", "x1")
LAST = ("x1", "x0", "zl", "y1", "y0", "zh", "c")
PI = 3.141592653589793
TAU = 6.283185307179586

SIN = (
    0.9999996039252741,
    -0.1666655344642713,
    0.008332407591595805,
    -0.00019808739967677424,
    2.699822692004479e-06,
    -2.036622659870151e-08,
)
COS = (
    0.999999989116818,
    -0.49999989185961996,
    0.04166649020175043,
    -0.0013887807832168462,
    2.476996623505445e-05,
    -2.70797756302502e-07,
    1.724760753325688e-09,
)
MIB = 1024 * 1024
BIG = 30
PAD = 72


def params(mib):
    return pltpu.CompilerParams(vmem_limit_bytes=mib * MIB)


def rev(value, bits):
    out = 0
    for i in range(bits):
        out = out | ((value >> i & 1) << (bits - 1 - i))
    return out


def place(names):
    index = 0
    for name in names:
        index = index * 2 + lax.axis_index(name)
    return index


def horner(coefs, u):
    acc = jnp.full_like(u, coefs[-1])
    for c in reversed(coefs[:-1]):
        acc = acc * u + c
    return acc


def sincos(x):
    u = x * x
    return x * horner(SIN, u), horner(COS, u)


def dot(a, b, dims=((1,), (0,))):
    return lax.dot_general(a, b, (dims, ((), ())), preferred_element_type=F32)


def split(x):
    hi = x.astype(BF16)
    return hi, (x - hi.astype(F32)).astype(BF16)


def send_kernel(nv, x_ref, out_ref, columns):
    for kt in range(8):
        columns[kt] = x_ref[:, kt * 128 : kt * 128 + 128]
        for c in range(2):
            for v in range(nv):
                part = columns[kt, pl.ds(c * 256 + v, 128, stride=2), :].T
                lanes = slice((c * nv + v) * 128, (c * nv + v) * 128 + 128)
                for core in range(2):
                    out_ref[rev(kt, 3) * 2 + core, :, lanes] = part[core * 64 : core * 64 + 64]


def final_kernel(nv, x_ref, out_ref, columns, sems):
    ncv = 2 * nv

    def leave(kt):
        lanes = slice(kt * 128, kt * 128 + 128)
        return pltpu.make_async_copy(columns.at[kt], out_ref.at[:, lanes], sems.at[kt])

    for kt in range(8):
        for c in range(2):
            for v in range(nv):
                cv = c * nv + v
                part = jnp.concatenate(
                    [
                        x_ref[pl.ds((xz * 16 + kt * 2) * 8 * ncv + cv, 16, stride=ncv), :]
                        for xz in range(8)
                    ],
                    axis=0,
                )
                columns[kt, pl.ds(c * 256 + v, 128, stride=2), :] = part.T
        leave(kt).start()
    for kt in range(8):
        leave(kt).wait()


def fetch(jobs, sems):
    copies = []
    for i, (ain, aout, level, start, width, dst, at) in enumerate(jobs):
        cols = pl.ds(pl.multiple_of(start, 128), width)
        copies.append(
            pltpu.make_async_copy(
                ain.at[level, :, cols], dst.at[0:64, at : at + width], sems.at[0, i]
            )
        )
        copies.append(
            pltpu.make_async_copy(
                aout.at[level, :, cols], dst.at[64:96, at : at + width], sems.at[1, i]
            )
        )
    for copy in copies:
        copy.start()
    for copy in copies:
        copy.wait()


def pack_y_kernel(ain, aout, y1, y2, y3, sems):
    y = place(Y)
    ry = rev(y, 2)
    jobs = [(ain, aout, 1, ((y >> 1) ^ 1) * 512, 512, y2, 256)]
    for m, dst in ((2, y2), (1, y1), (3, y3)):
        jobs.append((ain, aout, 0, (ry ^ rev(m, 2)) * 256, 256, dst, 0))
    fetch(jobs, sems)


def pack_x_kernel(ain, aout, x1, x2, x3, sems):
    x = place(X)
    rx = rev(x, 2)
    jobs = [(ain, aout, 5, ((x >> 1) ^ 1) * 512, 512, x2, 256)]
    for m, dst in ((2, x2), (1, x1), (3, x3)):
        jobs.append((ain, aout, 4, (rx ^ rev(m, 2)) * 256, 256, dst, 0))
    fetch(jobs, sems)


def core_kernel(ain, aout, y1, y2, y3, kept, sent, sems):
    y = place(Y)
    core = lax.axis_index("c")
    ry = rev(y, 2)
    jobs = []
    for dst, side in ((kept, core), (sent, 1 - core)):
        jobs.append((ain, aout, 0, ry * 256 + side * 128, 128, dst, 0))
        jobs.append((ain, aout, 1, (y >> 1) * 512 + side * 256, 256, dst, 512))
        jobs.append((ain, aout, 2, side * 512, 512, dst, 1024))
    fetch(jobs, sems)
    for dst, side in ((kept, core), (sent, 1 - core)):
        for m, src in ((1, y1), (2, y2), (3, y3)):
            cols = pl.ds(pl.multiple_of(side * 128, 128), 128)
            dst[:, m * 128 : m * 128 + 128] = src[:, cols]
        cols = pl.ds(pl.multiple_of(256 + side * 256, 128), 256)
        dst[:, 768:1024] = y2[:, cols]


def turned(read, scratch, width):
    for t in range(width // 128):
        part = read(slice(t * 128, t * 128 + 128))
        full = jnp.concatenate([part, jnp.zeros((32, 128), F32)], axis=0)
        scratch[t * 128 : t * 128 + 128, :] = full.T


def got(ref, at):
    return lambda s: ref[:, at + s.start : at + s.stop]


def weights(interp_ref, w_ref, first, count):
    row = lax.broadcasted_iota(jnp.int32, (256, 64), 0)
    col = lax.broadcasted_iota(jnp.int32, (256, 64), 1)
    left = ((row >> 2) == col).astype(F32).astype(BF16)
    row = lax.broadcasted_iota(jnp.int32, (32, 128), 0)
    col = lax.broadcasted_iota(jnp.int32, (32, 128), 1)
    right = (row == (col >> 2)).astype(F32).astype(BF16)
    row = lax.broadcasted_iota(jnp.int32, (256, 128), 0)
    col = lax.broadcasted_iota(jnp.int32, (256, 128), 1)
    keep = (row & 3) == (col & 3)
    for level in range(count):
        for i, part in enumerate(split(interp_ref[first + level])):
            mid = dot(left, part, ((1,), (1,))).astype(BF16)
            full = jnp.where(keep, dot(mid, right), 0.0)
            w_ref[level, :, i * 128 : i * 128 + 128] = full.astype(BF16)


def tables(count, slabs, raw, tab_ref, tab_v, sems):
    rows = 1024 // slabs
    lane = lax.broadcasted_iota(jnp.int32, (rows, 128), 1)

    def leave(level):
        return pltpu.make_async_copy(tab_v.at[level], tab_ref.at[level], sems.at[level])

    for level in range(count):

        def body(m, _):
            low = pl.ds(pl.multiple_of(m * rows, rows), rows)
            high = pl.ds(pl.multiple_of((m + slabs // 2) * rows, rows), rows)
            if level:
                before = jnp.where(
                    lane < 32,
                    pltpu.roll(raw[level - 1, low, :], 64, 1),
                    pltpu.roll(raw[level - 1, high, :], 96, 1),
                )
                before = jnp.where(lane < 64, before, 0.0)
            for t in range(2):
                at = pl.ds(pl.multiple_of((2 * m + t) * rows, rows), rows)
                angle = raw[level, at, :]
                if level:
                    angle = angle + before
                    turn = jnp.where(angle > PI, TAU, jnp.where(angle < -PI, -TAU, 0.0))
                    angle = angle - turn
                s, c = sincos(angle)
                tab_v[level, at, :] = jnp.where(lane < 64, c, pltpu.roll(s, 64, 1))
                if level == count - 1:
                    out = jnp.where(lane < 32, pltpu.roll(c, 64, 1), pltpu.roll(s, 96, 1))
                    tab_v[count, at, :] = out
            return 0

        lax.fori_loop(0, slabs // 2, body, 0, unroll=2)
        leave(level).start()
    leave(count).start()
    for level in range(count + 1):
        leave(level).wait()


def table_lo_kernel(
    ain, aout, interp, kept, other, tab_ref, w_ref, raw, scratch, mine, sems,
    tab_v, out_sems,
):
    y = place(Y)
    core = lax.axis_index("c")
    ry = rev(y, 2)
    fetch([(ain, aout, 3, 0, 1024, mine, 0)], sems)
    weights(interp, w_ref, 0, 4)

    def emit(level, base, ts):
        for t in range(ts):
            at = pl.multiple_of((base + t) * 64, 64)
            raw[level, pl.ds(at, 64), :] = scratch[pl.ds(t, 64, stride=ts), :]

    for src, side in ((kept, core), (other, 1 - core)):
        for m in range(4):
            turned(got(src, m * 128), scratch, 128)
            emit(0, ((ry ^ rev(m, 2)) * 2 + side) * 2, 2)
        for m in range(2):
            turned(got(src, 512 + m * 256), scratch, 256)
            emit(1, (((y >> 1) ^ m) * 2 + side) * 4, 4)
        turned(got(src, 1024), scratch, 512)
        emit(2, side * 8, 8)
    turned(got(mine, 0), scratch, 1024)
    emit(3, 0, 16)
    tables(4, 16, raw, tab_ref, tab_v, out_sems)


def table_hi_kernel(
    ain, aout, interp, x1, x2, x3, tab_ref, w_ref, raw, scratch, mine, sems,
    tab_v, out_sems,
):
    x = place(X)
    rx = rev(x, 2)
    fetch(
        [
            (ain, aout, 4, rx * 256, 256, mine, 0),
            (ain, aout, 5, (x >> 1) * 512, 512, mine, 256),
            (ain, aout, 6, 0, 1024, mine, 768),
        ],
        sems,
    )
    weights(interp, w_ref, 4, 3)

    def emit(level, base, ts):
        for t in range(ts):
            for T in range(16):
                at = pl.multiple_of((base + t) * 128 + T * 8, 8)
                raw[level, pl.ds(at, 8), :] = scratch[pl.ds(T * ts + t, 8, stride=16 * ts), :]

    for m, src in enumerate((None, x1, x2, x3)):
        read = got(mine, 0) if m == 0 else got(src, 0)
        turned(read, scratch, 256)
        emit(0, (rx ^ rev(m, 2)) * 2, 2)
    turned(got(mine, 256), scratch, 512)
    emit(1, (x >> 1) * 4, 4)
    turned(got(x2, 256), scratch, 512)
    emit(1, (1 - (x >> 1)) * 4, 4)
    turned(got(mine, 768), scratch, 1024)
    emit(2, 0, 8)
    tables(3, 8, raw, tab_ref, tab_v, out_sems)


def spread(table, first):
    lane = lax.broadcasted_iota(jnp.int32, table.shape, 1)
    return jnp.take_along_axis(table, first + (lane >> 2), axis=1)


def step(nv, low, high, table, w, after):
    n = table.shape[0]
    sides = []
    for kind, src in enumerate((low, high)):
        c = spread(table, kind * 32)
        s = spread(table, kind * 32 + 64)
        re, im = [], []
        for v in range(nv):
            xr = src(v)
            xi = src(nv + v)
            re.append(xr * c - xi * s)
            im.append(xr * s + xi * c)
        sides.append(jnp.concatenate(re + im, axis=0))
    hi, lo = split(jnp.concatenate(sides, axis=1))
    first = dot(hi, w)
    out = first[:, :128] + first[:, 128:] + dot(lo, w[:, :128])
    out = [out[q * n : q * n + n] for q in range(2 * nv)]
    if after is None:
        return out
    c = spread(after, 0)
    s = spread(after, 32)
    re = [out[v] * c - out[nv + v] * s for v in range(nv)]
    im = [out[v] * s + out[nv + v] * c for v in range(nv)]
    return re + im


def levels_kernel(nv, count, slabs, first, put, x_ref, bufs, tab_ref, w_ref, ready):
    rows = 1024 // slabs
    group = 128 // rows
    lanes = lambda q: slice(q * 128, q * 128 + 128)
    for level in range(count):
        ready(level)
        last = level == count - 1
        src = bufs[(level + 1) % 2] if level else x_ref
        dst = bufs[level % 2]
        w = w_ref[level]
        for i in range(slabs // 2 // group):
            if level == 0:
                lows, highs = first(i)
            else:
                lows = [i * group + g for g in range(group)]
                highs = [m + slabs // 2 for m in lows]
            low = lambda q: jnp.concatenate([src[m, :, lanes(q)] for m in lows], axis=0)
            high = lambda q: jnp.concatenate([src[m, :, lanes(q)] for m in highs], axis=0)
            for t in range(2):
                outs = [2 * (i * group + g) + t for g in range(group)]
                at = [slice(m * rows, m * rows + rows) for m in outs]
                read = lambda k: jnp.concatenate([tab_ref[k, r, :] for r in at], axis=0)
                after = read(count) if last else None
                for q, tile in enumerate(step(nv, low, high, read(level), w, after)):
                    for g, m in enumerate(outs):
                        part = tile[g * rows : g * rows + rows]
                        if last:
                            put(m, q, part)
                        else:
                            dst[m, :, lanes(q)] = part


def levels_lo_kernel(nv, x_ref, tab, w, out_ref, one, two, tab_v, w_v, sems):
    def first(i):
        a = (i & 1) * 8 + (i >> 1) * 4
        return [a, a + 1], [a + 2, a + 3]

    def put(slab, q, tile):
        for kp in range(8):
            rows = slice(slab * 8, slab * 8 + 8)
            out_ref[kp, rows, q * 128 : q * 128 + 128] = tile[kp * 8 : kp * 8 + 8]

    begin = [
        pltpu.make_async_copy(tab.at[0], tab_v.at[0], sems.at[0]),
        pltpu.make_async_copy(w, w_v, sems.at[1]),
        pltpu.make_async_copy(x_ref, two, sems.at[2]),
    ]
    rest = [pltpu.make_async_copy(tab.at[1:5], tab_v.at[1:5], sems.at[3])]

    def ready(level):
        for copy in (begin, rest, [], [])[level]:
            copy.wait()

    for copy in begin + rest:
        copy.start()
    levels_kernel(
        nv, 4, 16, first, put, two, (one, two), tab_v, w_v, ready
    )


def levels_hi_kernel(nv, where_ref, x_ref, tab, w, out_ref, one, two, done):
    ncv = 2 * nv

    def first(i):
        return [i], [i + 4]

    def put(slab, q, tile):
        done[pl.ds(slab * 128 * ncv + q, 128, stride=ncv), :] = tile

    levels_kernel(nv, 3, 8, first, put, x_ref, (one, two), tab, w, lambda level: None)

    def gather(e, _):
        for r in range(8):
            row = pl.multiple_of(where_ref[e * 8 + r], ncv)
            out_ref[e, r * ncv : r * ncv + ncv, :] = done[pl.ds(row, ncv), :]
        return 0

    lax.fori_loop(0, 128, gather, 0, unroll=4)


def table_shapes(count, rows):
    shape = jax.ShapeDtypeStruct
    return [shape((rows, 1024, 128), F32), shape((count, 256, 256), BF16)]


def shards(coefficients, angle_in, angle_out, interp, destination):
    nv = 2
    ncv = 2 * nv
    shape = jax.ShapeDtypeStruct
    sends = pl.pallas_call(
        pack_y_kernel,
        out_shape=[shape((96, w), F32) for w in (256, 768, 256)],
        in_specs=[HBM, HBM],
        out_specs=[VMEM] * 3,
        scratch_shapes=[pltpu.SemaphoreType.DMA((2, 4))],
        compiler_params=params(53),
    )(angle_in, angle_out)
    from_y = [
        lax.ppermute(s, Y, [(i, i ^ m) for i in range(4)]) for m, s in zip((1, 2, 3), sends)
    ]

    state = pl.pallas_call(
        functools.partial(send_kernel, nv),
        out_shape=shape((16, 64, ncv * 128), F32),
        in_specs=[VMEM],
        out_specs=VMEM,
        scratch_shapes=[pltpu.VMEM((8, 512, 128), F32)],
        compiler_params=params(6),
    )(coefficients.reshape(512, 1024))
    state, *from_y = lax.optimization_barrier((state, *from_y))
    state = lax.all_to_all(state, FIRST, 0, 0, tiled=True)

    sends = pl.pallas_call(
        pack_x_kernel,
        out_shape=[shape((96, w), F32) for w in (256, 768, 256)],
        in_specs=[HBM, HBM],
        out_specs=[VMEM] * 3,
        scratch_shapes=[pltpu.SemaphoreType.DMA((2, 4))],
        compiler_params=params(BIG),
    )(angle_in, angle_out)
    from_x = [
        lax.ppermute(s, X, [(i, i ^ m) for i in range(4)]) for m, s in zip((1, 2, 3), sends)
    ]
    kept, sent = pl.pallas_call(
        core_kernel,
        out_shape=[shape((96, 1536), F32)] * 2,
        in_specs=[HBM, HBM] + [VMEM] * 3,
        out_specs=[VMEM] * 2,
        scratch_shapes=[pltpu.SemaphoreType.DMA((2, 6))],
        compiler_params=params(BIG),
    )(angle_in, angle_out, *from_y)
    other = lax.ppermute(sent, "c", [(0, 1), (1, 0)])

    tables_lo = pl.pallas_call(
        table_lo_kernel,
        out_shape=table_shapes(4, PAD),
        in_specs=[HBM, HBM] + [VMEM] * 3,
        out_specs=[ANY, VMEM],
        scratch_shapes=[
            pltpu.VMEM((4, 1024, 128), F32),
            pltpu.VMEM((1024, 128), F32),
            pltpu.VMEM((96, 1024), F32),
            pltpu.SemaphoreType.DMA((2, 1)),
        ]
        + [pltpu.VMEM((5, 1024, 128), F32), pltpu.SemaphoreType.DMA((5,))],
        compiler_params=params(BIG),
    )(angle_in, angle_out, interp, kept, other)
    first, *from_x = lax.optimization_barrier((tables_lo[0], *from_x))
    tables_lo = [first, *tables_lo[1:]]
    tables_hi = pl.pallas_call(
        table_hi_kernel,
        out_shape=table_shapes(3, 4),
        in_specs=[HBM, HBM] + [VMEM] * 4,
        out_specs=[ANY, VMEM],
        scratch_shapes=[
            pltpu.VMEM((3, 1024, 128), F32),
            pltpu.VMEM((1024, 128), F32),
            pltpu.VMEM((96, 1792), F32),
            pltpu.SemaphoreType.DMA((2, 3)),
        ]
        + [pltpu.VMEM((4, 1024, 128), F32), pltpu.SemaphoreType.DMA((4,))],
        compiler_params=params(BIG),
    )(angle_in, angle_out, interp, *from_x)

    state = pl.pallas_call(
        functools.partial(levels_lo_kernel, nv),
        out_shape=shape((8, 128, ncv * 128), F32),
        in_specs=[ANY, ANY, ANY],
        out_specs=VMEM,
        scratch_shapes=[pltpu.VMEM((16, 64, ncv * 128), F32)] * 2
        + [
            pltpu.VMEM((5, 1024, 128), F32),
            pltpu.VMEM((4, 256, 256), BF16),
            pltpu.SemaphoreType.DMA((4,)),
        ],
        compiler_params=params(BIG),
    )(state, *tables_lo)
    wanted = destination[0]
    where = (wanted & 7) * 128 + (wanted >> 3 & 15) * 8 + (wanted >> 7)
    where = (where * ncv).reshape(8, 8, 16).swapaxes(0, 1).reshape(1024)
    state, where, *tables_hi = lax.optimization_barrier((state, where, *tables_hi))
    state = lax.all_to_all(state, SECOND, 0, 0, tiled=True)

    state = pl.pallas_call(
        functools.partial(levels_hi_kernel, nv),
        out_shape=shape((128, 8 * ncv, 128), F32),
        in_specs=[SMEM] + [VMEM] * 3,
        out_specs=VMEM,
        scratch_shapes=[pltpu.VMEM((8, 128, ncv * 128), F32)] * 2
        + [pltpu.VMEM((1024 * ncv, 128), F32)],
        compiler_params=params(BIG),
    )(where, state, *tables_hi)
    state = lax.all_to_all(state, LAST, 0, 0, tiled=True)

    out = pl.pallas_call(
        functools.partial(final_kernel, nv),
        out_shape=shape((512, 1024), F32),
        in_specs=[VMEM],
        out_specs=ANY,
        scratch_shapes=[pltpu.VMEM((8, 512, 128), F32), pltpu.SemaphoreType.DMA((8,))],
        compiler_params=params(6),
    )(state.reshape(1024 * ncv, 128))
    return out.reshape(2, 32, 8, 1024)


def solution(mesh):
    mesh = jax.sharding.Mesh(mesh.devices.reshape((2,) * 7), AXES)
    placed = (
        P(None, None, None, AXES),
        P(None, None, AXES),
        P(None, None, AXES),
        P(),
        P(AXES, None),
    )
    return jax.shard_map(
        shards,
        mesh=mesh,
        in_specs=placed,
        out_specs=P(None, None, None, AXES),
        check_vma=False,
    )
```

```python
import functools

import jax
import jax.numpy as jnp
from jax import lax
from jax.experimental import pallas as pl
from jax.experimental.pallas import tpu as pltpu
from jax.sharding import PartitionSpec as P

F32 = jnp.float32
BF16 = jnp.bfloat16
VMEM = pl.BlockSpec(memory_space=pltpu.VMEM)
SMEM = pl.BlockSpec(memory_space=pltpu.SMEM)
ANY = pl.BlockSpec(memory_space=pl.ANY)
HBM = pl.BlockSpec(memory_space=pltpu.HBM)
AXES = ("y1", "y0", "zh", "x1", "x0", "zl", "c")
Y = ("y1", "y0")
X = ("x1", "x0")
FIRST = ("y1", "y0", "zh", "c")
SECOND = ("zl", "x0", "x1")
LAST = ("x1", "x0", "zl", "y1", "y0", "zh", "c")
PI = 3.141592653589793
TAU = 6.283185307179586

SIN = (
    0.9999996039252741,
    -0.1666655344642713,
    0.008332407591595805,
    -0.00019808739967677424,
    2.699822692004479e-06,
    -2.036622659870151e-08,
)
COS = (
    0.999999989116818,
    -0.49999989185961996,
    0.04166649020175043,
    -0.0013887807832168462,
    2.476996623505445e-05,
    -2.70797756302502e-07,
    1.724760753325688e-09,
)
MIB = 1024 * 1024
BIG = 30
PAD = 72


def params(mib):
    return pltpu.CompilerParams(vmem_limit_bytes=mib * MIB)


def rev(value, bits):
    out = 0
    for i in range(bits):
        out = out | ((value >> i & 1) << (bits - 1 - i))
    return out


def place(names):
    index = 0
    for name in names:
        index = index * 2 + lax.axis_index(name)
    return index


def horner(coefs, u):
    acc = jnp.full_like(u, coefs[-1])
    for c in reversed(coefs[:-1]):
        acc = acc * u + c
    return acc


def sincos(x):
    u = x * x
    return x * horner(SIN, u), horner(COS, u)


def dot(a, b, dims=((1,), (0,))):
    return lax.dot_general(a, b, (dims, ((), ())), preferred_element_type=F32)


def split(x):
    hi = x.astype(BF16)
    return hi, (x - hi.astype(F32)).astype(BF16)


def send_kernel(nv, x_ref, out_ref, columns):
    for kt in range(8):
        columns[kt] = x_ref[:, kt * 128 : kt * 128 + 128]
        for c in range(2):
            for v in range(nv):
                part = columns[kt, pl.ds(c * 256 + v, 128, stride=2), :].T
                lanes = slice((c * nv + v) * 128, (c * nv + v) * 128 + 128)
                for core in range(2):
                    out_ref[rev(kt, 3) * 2 + core, :, lanes] = part[core * 64 : core * 64 + 64]


def final_kernel(nv, x_ref, out_ref, columns, sems):
    ncv = 2 * nv

    def leave(kt):
        lanes = slice(kt * 128, kt * 128 + 128)
        return pltpu.make_async_copy(columns.at[kt], out_ref.at[:, lanes], sems.at[kt])

    for kt in range(8):
        for c in range(2):
            for v in range(nv):
                cv = c * nv + v
                part = jnp.concatenate(
                    [
                        x_ref[pl.ds((xz * 16 + kt * 2) * 8 * ncv + cv, 16, stride=ncv), :]
                        for xz in range(8)
                    ],
                    axis=0,
                )
                columns[kt, pl.ds(c * 256 + v, 128, stride=2), :] = part.T
        leave(kt).start()
    for kt in range(8):
        leave(kt).wait()


def fetch(jobs, sems):
    copies = []
    for i, (ain, aout, level, start, width, dst, at) in enumerate(jobs):
        cols = pl.ds(pl.multiple_of(start, 128), width)
        copies.append(
            pltpu.make_async_copy(
                ain.at[level, :, cols], dst.at[0:64, at : at + width], sems.at[0, i]
            )
        )
        copies.append(
            pltpu.make_async_copy(
                aout.at[level, :, cols], dst.at[64:96, at : at + width], sems.at[1, i]
            )
        )
    for copy in copies:
        copy.start()
    for copy in copies:
        copy.wait()


def pack_y_kernel(ain, aout, y1, y2, y3, sems):
    y = place(Y)
    ry = rev(y, 2)
    jobs = [(ain, aout, 1, ((y >> 1) ^ 1) * 512, 512, y2, 256)]
    for m, dst in ((2, y2), (1, y1), (3, y3)):
        jobs.append((ain, aout, 0, (ry ^ rev(m, 2)) * 256, 256, dst, 0))
    fetch(jobs, sems)


def pack_x_kernel(ain, aout, x1, x2, x3, sems):
    x = place(X)
    rx = rev(x, 2)
    jobs = [(ain, aout, 5, ((x >> 1) ^ 1) * 512, 512, x2, 256)]
    for m, dst in ((2, x2), (1, x1), (3, x3)):
        jobs.append((ain, aout, 4, (rx ^ rev(m, 2)) * 256, 256, dst, 0))
    fetch(jobs, sems)


def core_kernel(ain, aout, y1, y2, y3, kept, sent, sems):
    y = place(Y)
    core = lax.axis_index("c")
    ry = rev(y, 2)
    jobs = []
    for dst, side in ((kept, core), (sent, 1 - core)):
        jobs.append((ain, aout, 0, ry * 256 + side * 128, 128, dst, 0))
        jobs.append((ain, aout, 1, (y >> 1) * 512 + side * 256, 256, dst, 512))
        jobs.append((ain, aout, 2, side * 512, 512, dst, 1024))
    fetch(jobs, sems)
    for dst, side in ((kept, core), (sent, 1 - core)):
        for m, src in ((1, y1), (2, y2), (3, y3)):
            cols = pl.ds(pl.multiple_of(side * 128, 128), 128)
            dst[:, m * 128 : m * 128 + 128] = src[:, cols]
        cols = pl.ds(pl.multiple_of(256 + side * 256, 128), 256)
        dst[:, 768:1024] = y2[:, cols]


def turned(read, scratch, width):
    for t in range(width // 128):
        part = read(slice(t * 128, t * 128 + 128))
        full = jnp.concatenate([part, jnp.zeros((32, 128), F32)], axis=0)
        scratch[t * 128 : t * 128 + 128, :] = full.T


def got(ref, at):
    return lambda s: ref[:, at + s.start : at + s.stop]


def weights(interp_ref, w_ref, first, count):
    row = lax.broadcasted_iota(jnp.int32, (256, 64), 0)
    col = lax.broadcasted_iota(jnp.int32, (256, 64), 1)
    left = ((row >> 2) == col).astype(F32).astype(BF16)
    row = lax.broadcasted_iota(jnp.int32, (32, 128), 0)
    col = lax.broadcasted_iota(jnp.int32, (32, 128), 1)
    right = (row == (col >> 2)).astype(F32).astype(BF16)
    row = lax.broadcasted_iota(jnp.int32, (256, 128), 0)
    col = lax.broadcasted_iota(jnp.int32, (256, 128), 1)
    keep = (row & 3) == (col & 3)
    for level in range(count):
        for i, part in enumerate(split(interp_ref[first + level])):
            mid = dot(left, part, ((1,), (1,))).astype(BF16)
            full = jnp.where(keep, dot(mid, right), 0.0)
            w_ref[level, :, i * 128 : i * 128 + 128] = full.astype(BF16)


def tables(count, slabs, raw, tab_ref, tab_v, sems):
    rows = 1024 // slabs
    lane = lax.broadcasted_iota(jnp.int32, (rows, 128), 1)

    def leave(level):
        return pltpu.make_async_copy(tab_v.at[level], tab_ref.at[level], sems.at[level])

    for level in range(count):

        def body(m, _):
            low = pl.ds(pl.multiple_of(m * rows, rows), rows)
            high = pl.ds(pl.multiple_of((m + slabs // 2) * rows, rows), rows)
            if level:
                before = jnp.where(
                    lane < 32,
                    pltpu.roll(raw[level - 1, low, :], 64, 1),
                    pltpu.roll(raw[level - 1, high, :], 96, 1),
                )
                before = jnp.where(lane < 64, before, 0.0)
            for t in range(2):
                at = pl.ds(pl.multiple_of((2 * m + t) * rows, rows), rows)
                angle = raw[level, at, :]
                if level:
                    angle = angle + before
                    turn = jnp.where(angle > PI, TAU, jnp.where(angle < -PI, -TAU, 0.0))
                    angle = angle - turn
                s, c = sincos(angle)
                tab_v[level, at, :] = jnp.where(lane < 64, c, pltpu.roll(s, 64, 1))
                if level == count - 1:
                    out = jnp.where(lane < 32, pltpu.roll(c, 64, 1), pltpu.roll(s, 96, 1))
                    tab_v[count, at, :] = out
            return 0

        lax.fori_loop(0, slabs // 2, body, 0, unroll=2)
        leave(level).start()
    leave(count).start()
    for level in range(count + 1):
        leave(level).wait()


def table_lo_kernel(
    ain, aout, kept, other, tab_ref, raw, scratch, mine, sems,
    tab_v, out_sems,
):
    y = place(Y)
    core = lax.axis_index("c")
    ry = rev(y, 2)
    fetch([(ain, aout, 3, 0, 1024, mine, 0)], sems)

    def emit(level, base, ts):
        for t in range(ts):
            at = pl.multiple_of((base + t) * 64, 64)
            raw[level, pl.ds(at, 64), :] = scratch[pl.ds(t, 64, stride=ts), :]

    for src, side in ((kept, core), (other, 1 - core)):
        for m in range(4):
            turned(got(src, m * 128), scratch, 128)
            emit(0, ((ry ^ rev(m, 2)) * 2 + side) * 2, 2)
        for m in range(2):
            turned(got(src, 512 + m * 256), scratch, 256)
            emit(1, (((y >> 1) ^ m) * 2 + side) * 4, 4)
        turned(got(src, 1024), scratch, 512)
        emit(2, side * 8, 8)
    turned(got(mine, 0), scratch, 1024)
    emit(3, 0, 16)
    tables(4, 16, raw, tab_ref, tab_v, out_sems)


def table_hi_kernel(
    ain, aout, interp, x1, x2, x3, tab_ref, w_ref, raw, scratch, mine, sems,
    tab_v, out_sems,
):
    x = place(X)
    rx = rev(x, 2)
    fetch(
        [
            (ain, aout, 4, rx * 256, 256, mine, 0),
            (ain, aout, 5, (x >> 1) * 512, 512, mine, 256),
            (ain, aout, 6, 0, 1024, mine, 768),
        ],
        sems,
    )
    weights(interp, w_ref, 4, 3)

    def emit(level, base, ts):
        for t in range(ts):
            for T in range(16):
                at = pl.multiple_of((base + t) * 128 + T * 8, 8)
                raw[level, pl.ds(at, 8), :] = scratch[pl.ds(T * ts + t, 8, stride=16 * ts), :]

    for m, src in enumerate((None, x1, x2, x3)):
        read = got(mine, 0) if m == 0 else got(src, 0)
        turned(read, scratch, 256)
        emit(0, (rx ^ rev(m, 2)) * 2, 2)
    turned(got(mine, 256), scratch, 512)
    emit(1, (x >> 1) * 4, 4)
    turned(got(x2, 256), scratch, 512)
    emit(1, (1 - (x >> 1)) * 4, 4)
    turned(got(mine, 768), scratch, 1024)
    emit(2, 0, 8)
    tables(3, 8, raw, tab_ref, tab_v, out_sems)


def spread(table, first):
    lane = lax.broadcasted_iota(jnp.int32, table.shape, 1)
    return jnp.take_along_axis(table, first + (lane >> 2), axis=1)


def step(nv, low, high, table, w, after):
    n = table.shape[0]
    sides = []
    for kind, src in enumerate((low, high)):
        c = spread(table, kind * 32)
        s = spread(table, kind * 32 + 64)
        re, im = [], []
        for v in range(nv):
            xr = src(v)
            xi = src(nv + v)
            re.append(xr * c - xi * s)
            im.append(xr * s + xi * c)
        sides.append(jnp.concatenate(re + im, axis=0))
    hi, lo = split(jnp.concatenate(sides, axis=1))
    first = dot(hi, w)
    out = first[:, :128] + first[:, 128:] + dot(lo, w[:, :128])
    out = [out[q * n : q * n + n] for q in range(2 * nv)]
    if after is None:
        return out
    c = spread(after, 0)
    s = spread(after, 32)
    re = [out[v] * c - out[nv + v] * s for v in range(nv)]
    im = [out[v] * s + out[nv + v] * c for v in range(nv)]
    return re + im


def levels_kernel(nv, count, slabs, first, put, x_ref, bufs, tab_ref, w_ref, ready):
    rows = 1024 // slabs
    group = 128 // rows
    lanes = lambda q: slice(q * 128, q * 128 + 128)
    for level in range(count):
        ready(level)
        last = level == count - 1
        src = bufs[(level + 1) % 2] if level else x_ref
        dst = bufs[level % 2]
        w = w_ref[level]
        for i in range(slabs // 2 // group):
            if level == 0:
                lows, highs = first(i)
            else:
                lows = [i * group + g for g in range(group)]
                highs = [m + slabs // 2 for m in lows]
            low = lambda q: jnp.concatenate([src[m, :, lanes(q)] for m in lows], axis=0)
            high = lambda q: jnp.concatenate([src[m, :, lanes(q)] for m in highs], axis=0)
            for t in range(2):
                outs = [2 * (i * group + g) + t for g in range(group)]
                at = [slice(m * rows, m * rows + rows) for m in outs]
                read = lambda k: jnp.concatenate([tab_ref[k, r, :] for r in at], axis=0)
                after = read(count) if last else None
                for q, tile in enumerate(step(nv, low, high, read(level), w, after)):
                    for g, m in enumerate(outs):
                        part = tile[g * rows : g * rows + rows]
                        if last:
                            put(m, q, part)
                        else:
                            dst[m, :, lanes(q)] = part


def levels_lo_kernel(nv, x_ref, tab, interp, out_ref, one, two, tab_v, w_v, interp_v, sems):
    def first(i):
        a = (i & 1) * 8 + (i >> 1) * 4
        return [a, a + 1], [a + 2, a + 3]

    def put(slab, q, tile):
        for kp in range(8):
            rows = slice(slab * 8, slab * 8 + 8)
            out_ref[kp, rows, q * 128 : q * 128 + 128] = tile[kp * 8 : kp * 8 + 8]

    begin = [
        pltpu.make_async_copy(tab.at[0], tab_v.at[0], sems.at[0]),
        pltpu.make_async_copy(x_ref, two, sems.at[2]),
    ]
    rest = [pltpu.make_async_copy(tab.at[1:5], tab_v.at[1:5], sems.at[3])]

    def ready(level):
        for copy in (begin, rest, [], [])[level]:
            copy.wait()

    small = pltpu.make_async_copy(interp, interp_v, sems.at[1])
    small.start()
    for copy in begin + rest:
        copy.start()
    small.wait()
    weights(interp_v, w_v, 0, 4)
    levels_kernel(
        nv, 4, 16, first, put, two, (one, two), tab_v, w_v, ready
    )


def levels_hi_kernel(nv, where_ref, x_ref, tab, w, out_ref, one, two, done):
    ncv = 2 * nv

    def first(i):
        return [i], [i + 4]

    def put(slab, q, tile):
        done[pl.ds(slab * 128 * ncv + q, 128, stride=ncv), :] = tile

    levels_kernel(nv, 3, 8, first, put, x_ref, (one, two), tab, w, lambda level: None)

    def gather(e, _):
        slot = (e >> 1 & 7) * 128 + (e >> 4) * 16 + (e & 1) * 8
        for r in range(8):
            row = pl.multiple_of(where_ref[slot + r], ncv)
            out_ref[e, r * ncv : r * ncv + ncv, :] = done[pl.ds(row, ncv), :]
        return 0

    lax.fori_loop(0, 128, gather, 0, unroll=4)


def table_shapes(count, rows):
    shape = jax.ShapeDtypeStruct
    return [shape((rows, 1024, 128), F32), shape((count, 256, 256), BF16)]


def shards(coefficients, angle_in, angle_out, interp, destination):
    nv = 2
    ncv = 2 * nv
    shape = jax.ShapeDtypeStruct
    sends = pl.pallas_call(
        pack_y_kernel,
        out_shape=[shape((96, w), F32) for w in (256, 768, 256)],
        in_specs=[HBM, HBM],
        out_specs=[VMEM] * 3,
        scratch_shapes=[pltpu.SemaphoreType.DMA((2, 4))],
        compiler_params=params(53),
    )(angle_in, angle_out)
    from_y = [
        lax.ppermute(s, Y, [(i, i ^ m) for i in range(4)]) for m, s in zip((1, 2, 3), sends)
    ]

    state = pl.pallas_call(
        functools.partial(send_kernel, nv),
        out_shape=shape((16, 64, ncv * 128), F32),
        in_specs=[VMEM],
        out_specs=VMEM,
        scratch_shapes=[pltpu.VMEM((8, 512, 128), F32)],
        compiler_params=params(6),
    )(coefficients.reshape(512, 1024))
    state, *from_y = lax.optimization_barrier((state, *from_y))
    state = lax.all_to_all(state, FIRST, 0, 0, tiled=True)

    sends = pl.pallas_call(
        pack_x_kernel,
        out_shape=[shape((96, w), F32) for w in (256, 768, 256)],
        in_specs=[HBM, HBM],
        out_specs=[VMEM] * 3,
        scratch_shapes=[pltpu.SemaphoreType.DMA((2, 4))],
        compiler_params=params(BIG),
    )(angle_in, angle_out)
    from_x = [
        lax.ppermute(s, X, [(i, i ^ m) for i in range(4)]) for m, s in zip((1, 2, 3), sends)
    ]
    kept, sent = pl.pallas_call(
        core_kernel,
        out_shape=[shape((96, 1536), F32)] * 2,
        in_specs=[HBM, HBM] + [VMEM] * 3,
        out_specs=[VMEM] * 2,
        scratch_shapes=[pltpu.SemaphoreType.DMA((2, 6))],
        compiler_params=params(BIG),
    )(angle_in, angle_out, *from_y)
    other = lax.ppermute(sent, "c", [(0, 1), (1, 0)])

    tables_lo = pl.pallas_call(
        table_lo_kernel,
        out_shape=shape((PAD, 1024, 128), F32),
        in_specs=[HBM, HBM] + [VMEM] * 2,
        out_specs=ANY,
        scratch_shapes=[
            pltpu.VMEM((4, 1024, 128), F32),
            pltpu.VMEM((1024, 128), F32),
            pltpu.VMEM((96, 1024), F32),
            pltpu.SemaphoreType.DMA((2, 1)),
        ]
        + [pltpu.VMEM((5, 1024, 128), F32), pltpu.SemaphoreType.DMA((5,))],
        compiler_params=params(BIG),
    )(angle_in, angle_out, kept, other)
    tables_lo, *from_x = lax.optimization_barrier((tables_lo, *from_x))
    tables_hi = pl.pallas_call(
        table_hi_kernel,
        out_shape=table_shapes(3, 4),
        in_specs=[HBM, HBM] + [VMEM] * 4,
        out_specs=[ANY, VMEM],
        scratch_shapes=[
            pltpu.VMEM((3, 1024, 128), F32),
            pltpu.VMEM((1024, 128), F32),
            pltpu.VMEM((96, 1792), F32),
            pltpu.SemaphoreType.DMA((2, 3)),
        ]
        + [pltpu.VMEM((4, 1024, 128), F32), pltpu.SemaphoreType.DMA((4,))],
        compiler_params=params(BIG),
    )(angle_in, angle_out, interp, *from_x)

    state = pl.pallas_call(
        functools.partial(levels_lo_kernel, nv),
        out_shape=shape((8, 128, ncv * 128), F32),
        in_specs=[ANY, ANY, ANY],
        out_specs=VMEM,
        scratch_shapes=[pltpu.VMEM((16, 64, ncv * 128), F32)] * 2
        + [
            pltpu.VMEM((5, 1024, 128), F32),
            pltpu.VMEM((4, 256, 256), BF16),
            pltpu.VMEM((7, 32, 64), F32),
            pltpu.SemaphoreType.DMA((4,)),
        ],
        compiler_params=params(BIG),
    )(state, tables_lo, interp)
    wanted = destination[0]
    where = (wanted & 7) * 128 + (wanted >> 3 & 15) * 8 + (wanted >> 7)
    where = where * ncv
    state, where, *tables_hi = lax.optimization_barrier((state, where, *tables_hi))
    state = lax.all_to_all(state, SECOND, 0, 0, tiled=True)

    state = pl.pallas_call(
        functools.partial(levels_hi_kernel, nv),
        out_shape=shape((128, 8 * ncv, 128), F32),
        in_specs=[SMEM] + [VMEM] * 3,
        out_specs=VMEM,
        scratch_shapes=[pltpu.VMEM((8, 128, ncv * 128), F32)] * 2
        + [pltpu.VMEM((1024 * ncv, 128), F32)],
        compiler_params=params(BIG),
    )(where, state, *tables_hi)
    state = lax.all_to_all(state, LAST, 0, 0, tiled=True)

    out = pl.pallas_call(
        functools.partial(final_kernel, nv),
        out_shape=shape((512, 1024), F32),
        in_specs=[VMEM],
        out_specs=ANY,
        scratch_shapes=[pltpu.VMEM((8, 512, 128), F32), pltpu.SemaphoreType.DMA((8,))],
        compiler_params=params(6),
    )(state.reshape(1024 * ncv, 128))
    return out.reshape(2, 32, 8, 1024)


def solution(mesh):
    mesh = jax.sharding.Mesh(mesh.devices.reshape((2,) * 7), AXES)
    placed = (
        P(None, None, None, AXES),
        P(None, None, AXES),
        P(None, None, AXES),
        P(),
        P(AXES, None),
    )
    return jax.shard_map(
        shards,
        mesh=mesh,
        in_specs=placed,
        out_specs=P(None, None, None, AXES),
        check_vma=False,
    )
```

```python
import functools

import jax
import jax.numpy as jnp
from jax import lax
from jax.experimental import pallas as pl
from jax.experimental.pallas import tpu as pltpu
from jax.sharding import PartitionSpec as P

F32 = jnp.float32
BF16 = jnp.bfloat16
VMEM = pl.BlockSpec(memory_space=pltpu.VMEM)
SMEM = pl.BlockSpec(memory_space=pltpu.SMEM)
ANY = pl.BlockSpec(memory_space=pl.ANY)
HBM = pl.BlockSpec(memory_space=pltpu.HBM)
AXES = ("y1", "y0", "zh", "x1", "x0", "zl", "c")
Y = ("y1", "y0")
X = ("x1", "x0")
FIRST = ("zh", "c", "y1", "y0")
SECOND = ("zl", "x0", "x1")
LAST = ("x1", "x0", "zl", "y1", "y0", "zh", "c")
PI = 3.141592653589793
TAU = 6.283185307179586

SIN = (
    0.9999996039252741,
    -0.1666655344642713,
    0.008332407591595805,
    -0.00019808739967677424,
    2.699822692004479e-06,
    -2.036622659870151e-08,
)
COS = (
    0.999999989116818,
    -0.49999989185961996,
    0.04166649020175043,
    -0.0013887807832168462,
    2.476996623505445e-05,
    -2.70797756302502e-07,
    1.724760753325688e-09,
)
MIB = 1024 * 1024
BIG = 30
PAD = 72


def params(mib):
    return pltpu.CompilerParams(vmem_limit_bytes=mib * MIB)


def rev(value, bits):
    out = 0
    for i in range(bits):
        out = out | ((value >> i & 1) << (bits - 1 - i))
    return out


def place(names):
    index = 0
    for name in names:
        index = index * 2 + lax.axis_index(name)
    return index


def horner(coefs, u):
    acc = jnp.full_like(u, coefs[-1])
    for c in reversed(coefs[:-1]):
        acc = acc * u + c
    return acc


def sincos(x):
    u = x * x
    return x * horner(SIN, u), horner(COS, u)


def dot(a, b, dims=((1,), (0,))):
    return lax.dot_general(a, b, (dims, ((), ())), preferred_element_type=F32)


def split(x):
    hi = x.astype(BF16)
    return hi, (x - hi.astype(F32)).astype(BF16)


def send_kernel(nv, x_ref, out_ref, columns):
    for kt in range(8):
        columns[kt] = x_ref[:, kt * 128 : kt * 128 + 128]
        for c in range(2):
            for v in range(nv):
                part = columns[kt, pl.ds(c * 256 + v, 128, stride=2), :].T
                lanes = slice((c * nv + v) * 128, (c * nv + v) * 128 + 128)
                for core in range(2):
                    owner = (kt >> 2) * 8 + core * 4 + rev(kt & 3, 2)
                    out_ref[owner, :, lanes] = part[core * 64 : core * 64 + 64]


def final_kernel(nv, x_ref, out_ref, columns, sems):
    ncv = 2 * nv

    def leave(kt):
        lanes = slice(kt * 128, kt * 128 + 128)
        return pltpu.make_async_copy(columns.at[kt], out_ref.at[:, lanes], sems.at[kt])

    for kt in range(8):
        for c in range(2):
            for v in range(nv):
                cv = c * nv + v
                part = jnp.concatenate(
                    [
                        x_ref[pl.ds((xz * 16 + kt * 2) * 8 * ncv + cv, 16, stride=ncv), :]
                        for xz in range(8)
                    ],
                    axis=0,
                )
                columns[kt, pl.ds(c * 256 + v, 128, stride=2), :] = part.T
        leave(kt).start()
    for kt in range(8):
        leave(kt).wait()


def fetch(jobs, sems):
    copies = []
    for i, (ain, aout, level, start, width, dst, at) in enumerate(jobs):
        cols = pl.ds(pl.multiple_of(start, 128), width)
        copies.append(
            pltpu.make_async_copy(
                ain.at[level, :, cols], dst.at[0:64, at : at + width], sems.at[0, i]
            )
        )
        copies.append(
            pltpu.make_async_copy(
                aout.at[level, :, cols], dst.at[64:96, at : at + width], sems.at[1, i]
            )
        )
    for copy in copies:
        copy.start()
    for copy in copies:
        copy.wait()


def pack_y_kernel(ain, aout, y1, y2, y3, sems):
    y = place(Y)
    ry = rev(y, 2)
    jobs = [(ain, aout, 1, ((y >> 1) ^ 1) * 512, 512, y2, 256)]
    for m, dst in ((2, y2), (1, y1), (3, y3)):
        jobs.append((ain, aout, 0, (ry ^ rev(m, 2)) * 256, 256, dst, 0))
    fetch(jobs, sems)


def pack_x_kernel(ain, aout, x1, x2, x3, sems):
    x = place(X)
    rx = rev(x, 2)
    jobs = [(ain, aout, 5, ((x >> 1) ^ 1) * 512, 512, x2, 256)]
    for m, dst in ((2, x2), (1, x1), (3, x3)):
        jobs.append((ain, aout, 4, (rx ^ rev(m, 2)) * 256, 256, dst, 0))
    fetch(jobs, sems)


def core_kernel(ain, aout, y1, y2, y3, kept, sent, sems):
    y = place(Y)
    core = lax.axis_index("c")
    ry = rev(y, 2)
    jobs = []
    for dst, side in ((kept, core), (sent, 1 - core)):
        jobs.append((ain, aout, 0, ry * 256 + side * 128, 128, dst, 0))
        jobs.append((ain, aout, 1, (y >> 1) * 512 + side * 256, 256, dst, 512))
        jobs.append((ain, aout, 2, side * 512, 512, dst, 1024))
    fetch(jobs, sems)
    for dst, side in ((kept, core), (sent, 1 - core)):
        for m, src in ((1, y1), (2, y2), (3, y3)):
            cols = pl.ds(pl.multiple_of(side * 128, 128), 128)
            dst[:, m * 128 : m * 128 + 128] = src[:, cols]
        cols = pl.ds(pl.multiple_of(256 + side * 256, 128), 256)
        dst[:, 768:1024] = y2[:, cols]


def turned(read, scratch, width):
    for t in range(width // 128):
        part = read(slice(t * 128, t * 128 + 128))
        full = jnp.concatenate([part, jnp.zeros((32, 128), F32)], axis=0)
        scratch[t * 128 : t * 128 + 128, :] = full.T


def got(ref, at):
    return lambda s: ref[:, at + s.start : at + s.stop]


def weights(interp_ref, w_ref, first, count):
    row = lax.broadcasted_iota(jnp.int32, (256, 64), 0)
    col = lax.broadcasted_iota(jnp.int32, (256, 64), 1)
    left = ((row >> 2) == col).astype(F32).astype(BF16)
    row = lax.broadcasted_iota(jnp.int32, (32, 128), 0)
    col = lax.broadcasted_iota(jnp.int32, (32, 128), 1)
    right = (row == (col >> 2)).astype(F32).astype(BF16)
    row = lax.broadcasted_iota(jnp.int32, (256, 128), 0)
    col = lax.broadcasted_iota(jnp.int32, (256, 128), 1)
    keep = (row & 3) == (col & 3)
    for level in range(count):
        for i, part in enumerate(split(interp_ref[first + level])):
            mid = dot(left, part, ((1,), (1,))).astype(BF16)
            full = jnp.where(keep, dot(mid, right), 0.0)
            w_ref[level, :, i * 128 : i * 128 + 128] = full.astype(BF16)


def tables(count, slabs, raw, tab_ref, tab_v, sems):
    rows = 1024 // slabs
    lane = lax.broadcasted_iota(jnp.int32, (rows, 128), 1)

    def leave(level):
        return pltpu.make_async_copy(tab_v.at[level], tab_ref.at[level], sems.at[level])

    for level in range(count):

        def body(m, _):
            low = pl.ds(pl.multiple_of(m * rows, rows), rows)
            high = pl.ds(pl.multiple_of((m + slabs // 2) * rows, rows), rows)
            if level:
                before = jnp.where(
                    lane < 32,
                    pltpu.roll(raw[level - 1, low, :], 64, 1),
                    pltpu.roll(raw[level - 1, high, :], 96, 1),
                )
                before = jnp.where(lane < 64, before, 0.0)
            for t in range(2):
                at = pl.ds(pl.multiple_of((2 * m + t) * rows, rows), rows)
                angle = raw[level, at, :]
                if level:
                    angle = angle + before
                    turn = jnp.where(angle > PI, TAU, jnp.where(angle < -PI, -TAU, 0.0))
                    angle = angle - turn
                s, c = sincos(angle)
                tab_v[level, at, :] = jnp.where(lane < 64, c, pltpu.roll(s, 64, 1))
                if level == count - 1:
                    out = jnp.where(lane < 32, pltpu.roll(c, 64, 1), pltpu.roll(s, 96, 1))
                    tab_v[count, at, :] = out
            return 0

        lax.fori_loop(0, slabs // 2, body, 0, unroll=2)
        leave(level).start()
    leave(count).start()
    for level in range(count + 1):
        leave(level).wait()


def table_lo_kernel(
    ain, aout, kept, other, tab_ref, raw, scratch, mine, sems,
    tab_v, out_sems,
):
    y = place(Y)
    core = lax.axis_index("c")
    ry = rev(y, 2)
    fetch([(ain, aout, 3, 0, 1024, mine, 0)], sems)

    def emit(level, base, ts):
        for t in range(ts):
            at = pl.multiple_of((base + t) * 64, 64)
            raw[level, pl.ds(at, 64), :] = scratch[pl.ds(t, 64, stride=ts), :]

    for src, side in ((kept, core), (other, 1 - core)):
        for m in range(4):
            turned(got(src, m * 128), scratch, 128)
            emit(0, ((ry ^ rev(m, 2)) * 2 + side) * 2, 2)
        for m in range(2):
            turned(got(src, 512 + m * 256), scratch, 256)
            emit(1, (((y >> 1) ^ m) * 2 + side) * 4, 4)
        turned(got(src, 1024), scratch, 512)
        emit(2, side * 8, 8)
    turned(got(mine, 0), scratch, 1024)
    emit(3, 0, 16)
    tables(4, 16, raw, tab_ref, tab_v, out_sems)


def table_hi_kernel(
    ain, aout, interp, x1, x2, x3, tab_ref, w_ref, raw, scratch, mine, sems,
    tab_v, out_sems,
):
    x = place(X)
    rx = rev(x, 2)
    fetch(
        [
            (ain, aout, 4, rx * 256, 256, mine, 0),
            (ain, aout, 5, (x >> 1) * 512, 512, mine, 256),
            (ain, aout, 6, 0, 1024, mine, 768),
        ],
        sems,
    )
    weights(interp, w_ref, 4, 3)

    def emit(level, base, ts):
        for t in range(ts):
            for T in range(16):
                at = pl.multiple_of((base + t) * 128 + T * 8, 8)
                raw[level, pl.ds(at, 8), :] = scratch[pl.ds(T * ts + t, 8, stride=16 * ts), :]

    for m, src in enumerate((None, x1, x2, x3)):
        read = got(mine, 0) if m == 0 else got(src, 0)
        turned(read, scratch, 256)
        emit(0, (rx ^ rev(m, 2)) * 2, 2)
    turned(got(mine, 256), scratch, 512)
    emit(1, (x >> 1) * 4, 4)
    turned(got(x2, 256), scratch, 512)
    emit(1, (1 - (x >> 1)) * 4, 4)
    turned(got(mine, 768), scratch, 1024)
    emit(2, 0, 8)
    tables(3, 8, raw, tab_ref, tab_v, out_sems)


def spread(table, first):
    lane = lax.broadcasted_iota(jnp.int32, table.shape, 1)
    return jnp.take_along_axis(table, first + (lane >> 2), axis=1)


def step(nv, low, high, table, w, after):
    n = table.shape[0]
    sides = []
    for kind, src in enumerate((low, high)):
        c = spread(table, kind * 32)
        s = spread(table, kind * 32 + 64)
        re, im = [], []
        for v in range(nv):
            xr = src(v)
            xi = src(nv + v)
            re.append(xr * c - xi * s)
            im.append(xr * s + xi * c)
        sides.append(jnp.concatenate(re + im, axis=0))
    hi, lo = split(jnp.concatenate(sides, axis=1))
    first = dot(hi, w)
    out = first[:, :128] + first[:, 128:] + dot(lo, w[:, :128])
    out = [out[q * n : q * n + n] for q in range(2 * nv)]
    if after is None:
        return out
    c = spread(after, 0)
    s = spread(after, 32)
    re = [out[v] * c - out[nv + v] * s for v in range(nv)]
    im = [out[v] * s + out[nv + v] * c for v in range(nv)]
    return re + im


def levels_kernel(nv, count, slabs, first, put, x_ref, bufs, tab_ref, w_ref, ready):
    rows = 1024 // slabs
    group = 128 // rows
    lanes = lambda q: slice(q * 128, q * 128 + 128)
    for level in range(count):
        ready(level)
        last = level == count - 1
        src = bufs[(level + 1) % 2] if level else x_ref
        dst = bufs[level % 2]
        w = w_ref[level]
        for i in range(slabs // 2 // group):
            if level == 0:
                lows, highs = first(i)
            else:
                lows = [i * group + g for g in range(group)]
                highs = [m + slabs // 2 for m in lows]
            low = lambda q: jnp.concatenate([src[m, :, lanes(q)] for m in lows], axis=0)
            high = lambda q: jnp.concatenate([src[m, :, lanes(q)] for m in highs], axis=0)
            for t in range(2):
                outs = [2 * (i * group + g) + t for g in range(group)]
                at = [slice(m * rows, m * rows + rows) for m in outs]
                read = lambda k: jnp.concatenate([tab_ref[k, r, :] for r in at], axis=0)
                after = read(count) if last else None
                for q, tile in enumerate(step(nv, low, high, read(level), w, after)):
                    for g, m in enumerate(outs):
                        part = tile[g * rows : g * rows + rows]
                        if last:
                            put(m, q, part)
                        else:
                            dst[m, :, lanes(q)] = part


def levels_lo_kernel(nv, x_ref, tab, interp, out_ref, one, two, tab_v, w_v, interp_v, sems):
    def first(i):
        a = rev(i, 2)
        return [a, a + 4], [a + 8, a + 12]

    def put(slab, q, tile):
        for kp in range(8):
            rows = slice(slab * 8, slab * 8 + 8)
            out_ref[kp, rows, q * 128 : q * 128 + 128] = tile[kp * 8 : kp * 8 + 8]

    begin = [
        pltpu.make_async_copy(tab.at[0], tab_v.at[0], sems.at[0]),
        pltpu.make_async_copy(x_ref, two, sems.at[2]),
    ]
    rest = [pltpu.make_async_copy(tab.at[1:5], tab_v.at[1:5], sems.at[3])]

    def ready(level):
        for copy in (begin, rest, [], [])[level]:
            copy.wait()

    small = pltpu.make_async_copy(interp, interp_v, sems.at[1])
    small.start()
    for copy in begin + rest:
        copy.start()
    small.wait()
    weights(interp_v, w_v, 0, 4)
    levels_kernel(
        nv, 4, 16, first, put, two, (one, two), tab_v, w_v, ready
    )


def levels_hi_kernel(nv, where_ref, x_ref, tab, w, out_ref, one, two, done):
    ncv = 2 * nv

    def first(i):
        return [i], [i + 4]

    def put(slab, q, tile):
        done[pl.ds(slab * 128 * ncv + q, 128, stride=ncv), :] = tile

    levels_kernel(nv, 3, 8, first, put, x_ref, (one, two), tab, w, lambda level: None)

    def gather(e, _):
        slot = (e >> 1 & 7) * 128 + (e >> 4) * 16 + (e & 1) * 8
        for r in range(8):
            row = pl.multiple_of(where_ref[slot + r], ncv)
            out_ref[e, r * ncv : r * ncv + ncv, :] = done[pl.ds(row, ncv), :]
        return 0

    lax.fori_loop(0, 128, gather, 0, unroll=4)


def table_shapes(count, rows):
    shape = jax.ShapeDtypeStruct
    return [shape((rows, 1024, 128), F32), shape((count, 256, 256), BF16)]


def shards(coefficients, angle_in, angle_out, interp, destination):
    nv = 2
    ncv = 2 * nv
    shape = jax.ShapeDtypeStruct
    sends = pl.pallas_call(
        pack_y_kernel,
        out_shape=[shape((96, w), F32) for w in (256, 768, 256)],
        in_specs=[HBM, HBM],
        out_specs=[VMEM] * 3,
        scratch_shapes=[pltpu.SemaphoreType.DMA((2, 4))],
        compiler_params=params(53),
    )(angle_in, angle_out)
    from_y = [
        lax.ppermute(s, Y, [(i, i ^ m) for i in range(4)]) for m, s in zip((1, 2, 3), sends)
    ]

    state = pl.pallas_call(
        functools.partial(send_kernel, nv),
        out_shape=shape((16, 64, ncv * 128), F32),
        in_specs=[VMEM],
        out_specs=VMEM,
        scratch_shapes=[pltpu.VMEM((8, 512, 128), F32)],
        compiler_params=params(6),
    )(coefficients.reshape(512, 1024))
    state, *from_y = lax.optimization_barrier((state, *from_y))
    state = lax.all_to_all(state, FIRST, 0, 0, tiled=True)

    sends = pl.pallas_call(
        pack_x_kernel,
        out_shape=[shape((96, w), F32) for w in (256, 768, 256)],
        in_specs=[HBM, HBM],
        out_specs=[VMEM] * 3,
        scratch_shapes=[pltpu.SemaphoreType.DMA((2, 4))],
        compiler_params=params(BIG),
    )(angle_in, angle_out)
    from_x = [
        lax.ppermute(s, X, [(i, i ^ m) for i in range(4)]) for m, s in zip((1, 2, 3), sends)
    ]
    kept, sent = pl.pallas_call(
        core_kernel,
        out_shape=[shape((96, 1536), F32)] * 2,
        in_specs=[HBM, HBM] + [VMEM] * 3,
        out_specs=[VMEM] * 2,
        scratch_shapes=[pltpu.SemaphoreType.DMA((2, 6))],
        compiler_params=params(BIG),
    )(angle_in, angle_out, *from_y)
    other = lax.ppermute(sent, "c", [(0, 1), (1, 0)])

    tables_lo = pl.pallas_call(
        table_lo_kernel,
        out_shape=shape((PAD, 1024, 128), F32),
        in_specs=[HBM, HBM] + [VMEM] * 2,
        out_specs=ANY,
        scratch_shapes=[
            pltpu.VMEM((4, 1024, 128), F32),
            pltpu.VMEM((1024, 128), F32),
            pltpu.VMEM((96, 1024), F32),
            pltpu.SemaphoreType.DMA((2, 1)),
        ]
        + [pltpu.VMEM((5, 1024, 128), F32), pltpu.SemaphoreType.DMA((5,))],
        compiler_params=params(BIG),
    )(angle_in, angle_out, kept, other)
    tables_lo, *from_x = lax.optimization_barrier((tables_lo, *from_x))
    tables_hi = pl.pallas_call(
        table_hi_kernel,
        out_shape=table_shapes(3, 4),
        in_specs=[HBM, HBM] + [VMEM] * 4,
        out_specs=[ANY, VMEM],
        scratch_shapes=[
            pltpu.VMEM((3, 1024, 128), F32),
            pltpu.VMEM((1024, 128), F32),
            pltpu.VMEM((96, 1792), F32),
            pltpu.SemaphoreType.DMA((2, 3)),
        ]
        + [pltpu.VMEM((4, 1024, 128), F32), pltpu.SemaphoreType.DMA((4,))],
        compiler_params=params(BIG),
    )(angle_in, angle_out, interp, *from_x)

    state = pl.pallas_call(
        functools.partial(levels_lo_kernel, nv),
        out_shape=shape((8, 128, ncv * 128), F32),
        in_specs=[ANY, ANY, ANY],
        out_specs=VMEM,
        scratch_shapes=[pltpu.VMEM((16, 64, ncv * 128), F32)] * 2
        + [
            pltpu.VMEM((5, 1024, 128), F32),
            pltpu.VMEM((4, 256, 256), BF16),
            pltpu.VMEM((7, 32, 64), F32),
            pltpu.SemaphoreType.DMA((4,)),
        ],
        compiler_params=params(BIG),
    )(state, tables_lo, interp)
    wanted = destination[0]
    where = (wanted & 7) * 128 + (wanted >> 3 & 15) * 8 + (wanted >> 7)
    where = where * ncv
    state, where, *tables_hi = lax.optimization_barrier((state, where, *tables_hi))
    state = lax.all_to_all(state, SECOND, 0, 0, tiled=True)

    state = pl.pallas_call(
        functools.partial(levels_hi_kernel, nv),
        out_shape=shape((128, 8 * ncv, 128), F32),
        in_specs=[SMEM] + [VMEM] * 3,
        out_specs=VMEM,
        scratch_shapes=[pltpu.VMEM((8, 128, ncv * 128), F32)] * 2
        + [pltpu.VMEM((1024 * ncv, 128), F32)],
        compiler_params=params(BIG),
    )(where, state, *tables_hi)
    state = lax.all_to_all(state, LAST, 0, 0, tiled=True)

    out = pl.pallas_call(
        functools.partial(final_kernel, nv),
        out_shape=shape((512, 1024), F32),
        in_specs=[VMEM],
        out_specs=ANY,
        scratch_shapes=[pltpu.VMEM((8, 512, 128), F32), pltpu.SemaphoreType.DMA((8,))],
        compiler_params=params(6),
    )(state.reshape(1024 * ncv, 128))
    return out.reshape(2, 32, 8, 1024)


def solution(mesh):
    mesh = jax.sharding.Mesh(mesh.devices.reshape((2,) * 7), AXES)
    placed = (
        P(None, None, None, AXES),
        P(None, None, AXES),
        P(None, None, AXES),
        P(),
        P(AXES, None),
    )
    return jax.shard_map(
        shards,
        mesh=mesh,
        in_specs=placed,
        out_specs=P(None, None, None, AXES),
        check_vma=False,
    )
```

```python
import functools

import jax
import jax.numpy as jnp
from jax import lax
from jax.experimental import pallas as pl
from jax.experimental.pallas import tpu as pltpu
from jax.sharding import PartitionSpec as P

F32 = jnp.float32
BF16 = jnp.bfloat16
VMEM = pl.BlockSpec(memory_space=pltpu.VMEM)
SMEM = pl.BlockSpec(memory_space=pltpu.SMEM)
ANY = pl.BlockSpec(memory_space=pl.ANY)
HBM = pl.BlockSpec(memory_space=pltpu.HBM)
AXES = ("y1", "y0", "zh", "x1", "x0", "zl", "c")
Y = ("y1", "y0")
X = ("x1", "x0")
FIRST = ("zh", "c", "y1", "y0")
SECOND = ("zl", "x0", "x1")
LAST = ("x1", "x0", "zl", "y1", "y0", "zh", "c")
PI = 3.141592653589793
TAU = 6.283185307179586

SIN = (
    0.9999996039252741,
    -0.1666655344642713,
    0.008332407591595805,
    -0.00019808739967677424,
    2.699822692004479e-06,
    -2.036622659870151e-08,
)
COS = (
    0.999999989116818,
    -0.49999989185961996,
    0.04166649020175043,
    -0.0013887807832168462,
    2.476996623505445e-05,
    -2.70797756302502e-07,
    1.724760753325688e-09,
)
MIB = 1024 * 1024
BIG = 30
PAD = 72


def params(mib):
    return pltpu.CompilerParams(vmem_limit_bytes=mib * MIB)


def rev(value, bits):
    out = 0
    for i in range(bits):
        out = out | ((value >> i & 1) << (bits - 1 - i))
    return out


def place(names):
    index = 0
    for name in names:
        index = index * 2 + lax.axis_index(name)
    return index


def horner(coefs, u):
    acc = jnp.full_like(u, coefs[-1])
    for c in reversed(coefs[:-1]):
        acc = acc * u + c
    return acc


def sincos(x):
    u = x * x
    return x * horner(SIN, u), horner(COS, u)


def dot(a, b, dims=((1,), (0,))):
    return lax.dot_general(a, b, (dims, ((), ())), preferred_element_type=F32)


def split(x):
    hi = x.astype(BF16)
    return hi, (x - hi.astype(F32)).astype(BF16)


def send_kernel(nv, x_ref, out_ref, columns):
    for kt in range(8):
        columns[kt] = x_ref[:, kt * 128 : kt * 128 + 128]
        for c in range(2):
            for v in range(nv):
                part = columns[kt, pl.ds(c * 256 + v, 128, stride=2), :].T
                lanes = slice((c * nv + v) * 128, (c * nv + v) * 128 + 128)
                for core in range(2):
                    owner = (kt >> 2) * 8 + core * 4 + rev(kt & 3, 2)
                    out_ref[owner, :, lanes] = part[core * 64 : core * 64 + 64]


def final_kernel(nv, x_ref, out_ref, columns, sems):
    ncv = 2 * nv

    def leave(kt):
        lanes = slice(kt * 128, kt * 128 + 128)
        return pltpu.make_async_copy(columns.at[kt], out_ref.at[:, lanes], sems.at[kt])

    for kt in range(8):
        for c in range(2):
            for v in range(nv):
                cv = c * nv + v
                part = jnp.concatenate(
                    [
                        x_ref[pl.ds((xz * 16 + kt * 2) * 8 * ncv + cv, 16, stride=ncv), :]
                        for xz in range(8)
                    ],
                    axis=0,
                )
                columns[kt, pl.ds(c * 256 + v, 128, stride=2), :] = part.T
        leave(kt).start()
    for kt in range(8):
        leave(kt).wait()


def fetch(jobs, sems):
    copies = []
    for i, (ain, aout, level, start, width, dst, at) in enumerate(jobs):
        cols = pl.ds(pl.multiple_of(start, 128), width)
        copies.append(
            pltpu.make_async_copy(
                ain.at[level, :, cols], dst.at[0:64, at : at + width], sems.at[0, i]
            )
        )
        copies.append(
            pltpu.make_async_copy(
                aout.at[level, :, cols], dst.at[64:96, at : at + width], sems.at[1, i]
            )
        )
    for copy in copies:
        copy.start()
    for copy in copies:
        copy.wait()


def pack_far_kernel(ain, aout, y2, sems):
    y = place(Y)
    jobs = [
        (ain, aout, 1, ((y >> 1) ^ 1) * 512, 512, y2, 256),
        (ain, aout, 0, (rev(y, 2) ^ rev(2, 2)) * 256, 256, y2, 0),
    ]
    fetch(jobs, sems)


def pack_near_kernel(ain, aout, y1, y3, sems):
    ry = rev(place(Y), 2)
    jobs = [
        (ain, aout, 0, (ry ^ rev(m, 2)) * 256, 256, dst, 0) for m, dst in ((1, y1), (3, y3))
    ]
    fetch(jobs, sems)


def pack_x_kernel(ain, aout, x1, x2, x3, sems):
    x = place(X)
    rx = rev(x, 2)
    jobs = [(ain, aout, 5, ((x >> 1) ^ 1) * 512, 512, x2, 256)]
    for m, dst in ((2, x2), (1, x1), (3, x3)):
        jobs.append((ain, aout, 4, (rx ^ rev(m, 2)) * 256, 256, dst, 0))
    fetch(jobs, sems)


def core_kernel(ain, aout, y1, y2, y3, kept, sent, sems):
    y = place(Y)
    core = lax.axis_index("c")
    ry = rev(y, 2)
    jobs = []
    for dst, side in ((kept, core), (sent, 1 - core)):
        jobs.append((ain, aout, 0, ry * 256 + side * 128, 128, dst, 0))
        jobs.append((ain, aout, 1, (y >> 1) * 512 + side * 256, 256, dst, 512))
        jobs.append((ain, aout, 2, side * 512, 512, dst, 1024))
    fetch(jobs, sems)
    for dst, side in ((kept, core), (sent, 1 - core)):
        for m, src in ((1, y1), (2, y2), (3, y3)):
            cols = pl.ds(pl.multiple_of(side * 128, 128), 128)
            dst[:, m * 128 : m * 128 + 128] = src[:, cols]
        cols = pl.ds(pl.multiple_of(256 + side * 256, 128), 256)
        dst[:, 768:1024] = y2[:, cols]


def turned(read, scratch, width):
    for t in range(width // 128):
        part = read(slice(t * 128, t * 128 + 128))
        full = jnp.concatenate([part, jnp.zeros((32, 128), F32)], axis=0)
        scratch[t * 128 : t * 128 + 128, :] = full.T


def got(ref, at):
    return lambda s: ref[:, at + s.start : at + s.stop]


def weights(interp_ref, w_ref, first, count):
    row = lax.broadcasted_iota(jnp.int32, (256, 64), 0)
    col = lax.broadcasted_iota(jnp.int32, (256, 64), 1)
    left = ((row >> 2) == col).astype(F32).astype(BF16)
    row = lax.broadcasted_iota(jnp.int32, (32, 128), 0)
    col = lax.broadcasted_iota(jnp.int32, (32, 128), 1)
    right = (row == (col >> 2)).astype(F32).astype(BF16)
    row = lax.broadcasted_iota(jnp.int32, (256, 128), 0)
    col = lax.broadcasted_iota(jnp.int32, (256, 128), 1)
    keep = (row & 3) == (col & 3)
    for level in range(count):
        for i, part in enumerate(split(interp_ref[first + level])):
            mid = dot(left, part, ((1,), (1,))).astype(BF16)
            full = jnp.where(keep, dot(mid, right), 0.0)
            w_ref[level, :, i * 128 : i * 128 + 128] = full.astype(BF16)


def tables(count, slabs, raw, tab_ref, tab_v, sems):
    rows = 1024 // slabs
    lane = lax.broadcasted_iota(jnp.int32, (rows, 128), 1)

    def leave(level):
        return pltpu.make_async_copy(tab_v.at[level], tab_ref.at[level], sems.at[level])

    for level in range(count):

        def body(m, _):
            low = pl.ds(pl.multiple_of(m * rows, rows), rows)
            high = pl.ds(pl.multiple_of((m + slabs // 2) * rows, rows), rows)
            if level:
                before = jnp.where(
                    lane < 32,
                    pltpu.roll(raw[level - 1, low, :], 64, 1),
                    pltpu.roll(raw[level - 1, high, :], 96, 1),
                )
                before = jnp.where(lane < 64, before, 0.0)
            for t in range(2):
                at = pl.ds(pl.multiple_of((2 * m + t) * rows, rows), rows)
                angle = raw[level, at, :]
                if level:
                    angle = angle + before
                    turn = jnp.where(angle > PI, TAU, jnp.where(angle < -PI, -TAU, 0.0))
                    angle = angle - turn
                s, c = sincos(angle)
                tab_v[level, at, :] = jnp.where(lane < 64, c, pltpu.roll(s, 64, 1))
                if level == count - 1:
                    out = jnp.where(lane < 32, pltpu.roll(c, 64, 1), pltpu.roll(s, 96, 1))
                    tab_v[count, at, :] = out
            return 0

        lax.fori_loop(0, slabs // 2, body, 0, unroll=2)
        leave(level).start()
    leave(count).start()
    for level in range(count + 1):
        leave(level).wait()


def table_lo_kernel(
    ain, aout, kept, other, tab_ref, raw, scratch, mine, sems,
    tab_v, out_sems,
):
    y = place(Y)
    core = lax.axis_index("c")
    ry = rev(y, 2)
    fetch([(ain, aout, 3, 0, 1024, mine, 0)], sems)

    def emit(level, base, ts):
        for t in range(ts):
            at = pl.multiple_of((base + t) * 64, 64)
            raw[level, pl.ds(at, 64), :] = scratch[pl.ds(t, 64, stride=ts), :]

    for src, side in ((kept, core), (other, 1 - core)):
        for m in range(4):
            turned(got(src, m * 128), scratch, 128)
            emit(0, ((ry ^ rev(m, 2)) * 2 + side) * 2, 2)
        for m in range(2):
            turned(got(src, 512 + m * 256), scratch, 256)
            emit(1, (((y >> 1) ^ m) * 2 + side) * 4, 4)
        turned(got(src, 1024), scratch, 512)
        emit(2, side * 8, 8)
    turned(got(mine, 0), scratch, 1024)
    emit(3, 0, 16)
    tables(4, 16, raw, tab_ref, tab_v, out_sems)


def table_hi_kernel(
    ain, aout, interp, x1, x2, x3, tab_ref, w_ref, raw, scratch, mine, sems,
    tab_v, out_sems,
):
    x = place(X)
    rx = rev(x, 2)
    fetch(
        [
            (ain, aout, 4, rx * 256, 256, mine, 0),
            (ain, aout, 5, (x >> 1) * 512, 512, mine, 256),
            (ain, aout, 6, 0, 1024, mine, 768),
        ],
        sems,
    )
    weights(interp, w_ref, 4, 3)

    def emit(level, base, ts):
        for t in range(ts):
            for T in range(16):
                at = pl.multiple_of((base + t) * 128 + T * 8, 8)
                raw[level, pl.ds(at, 8), :] = scratch[pl.ds(T * ts + t, 8, stride=16 * ts), :]

    for m, src in enumerate((None, x1, x2, x3)):
        read = got(mine, 0) if m == 0 else got(src, 0)
        turned(read, scratch, 256)
        emit(0, (rx ^ rev(m, 2)) * 2, 2)
    turned(got(mine, 256), scratch, 512)
    emit(1, (x >> 1) * 4, 4)
    turned(got(x2, 256), scratch, 512)
    emit(1, (1 - (x >> 1)) * 4, 4)
    turned(got(mine, 768), scratch, 1024)
    emit(2, 0, 8)
    tables(3, 8, raw, tab_ref, tab_v, out_sems)


def spread(table, first):
    lane = lax.broadcasted_iota(jnp.int32, table.shape, 1)
    return jnp.take_along_axis(table, first + (lane >> 2), axis=1)


def step(nv, low, high, table, w, after):
    n = table.shape[0]
    sides = []
    for kind, src in enumerate((low, high)):
        c = spread(table, kind * 32)
        s = spread(table, kind * 32 + 64)
        re, im = [], []
        for v in range(nv):
            xr = src(v)
            xi = src(nv + v)
            re.append(xr * c - xi * s)
            im.append(xr * s + xi * c)
        sides.append(jnp.concatenate(re + im, axis=0))
    hi, lo = split(jnp.concatenate(sides, axis=1))
    first = dot(hi, w)
    out = first[:, :128] + first[:, 128:] + dot(lo, w[:, :128])
    out = [out[q * n : q * n + n] for q in range(2 * nv)]
    if after is None:
        return out
    c = spread(after, 0)
    s = spread(after, 32)
    re = [out[v] * c - out[nv + v] * s for v in range(nv)]
    im = [out[v] * s + out[nv + v] * c for v in range(nv)]
    return re + im


def levels_kernel(nv, count, slabs, first, put, x_ref, bufs, tab_ref, w_ref, ready):
    rows = 1024 // slabs
    group = 128 // rows
    lanes = lambda q: slice(q * 128, q * 128 + 128)
    for level in range(count):
        ready(level)
        last = level == count - 1
        src = bufs[(level + 1) % 2] if level else x_ref
        dst = bufs[level % 2]
        w = w_ref[level]
        for i in range(slabs // 2 // group):
            if level == 0:
                lows, highs = first(i)
            else:
                lows = [i * group + g for g in range(group)]
                highs = [m + slabs // 2 for m in lows]
            low = lambda q: jnp.concatenate([src[m, :, lanes(q)] for m in lows], axis=0)
            high = lambda q: jnp.concatenate([src[m, :, lanes(q)] for m in highs], axis=0)
            for t in range(2):
                outs = [2 * (i * group + g) + t for g in range(group)]
                at = [slice(m * rows, m * rows + rows) for m in outs]
                read = lambda k: jnp.concatenate([tab_ref[k, r, :] for r in at], axis=0)
                after = read(count) if last else None
                for q, tile in enumerate(step(nv, low, high, read(level), w, after)):
                    for g, m in enumerate(outs):
                        part = tile[g * rows : g * rows + rows]
                        if last:
                            put(m, q, part)
                        else:
                            dst[m, :, lanes(q)] = part


def levels_lo_kernel(nv, x_ref, tab, interp, out_ref, one, two, tab_v, w_v, interp_v, sems):
    def first(i):
        a = rev(i, 2)
        return [a, a + 4], [a + 8, a + 12]

    def put(slab, q, tile):
        for kp in range(8):
            rows = slice(slab * 8, slab * 8 + 8)
            out_ref[kp, rows, q * 128 : q * 128 + 128] = tile[kp * 8 : kp * 8 + 8]

    begin = [
        pltpu.make_async_copy(tab.at[0], tab_v.at[0], sems.at[0]),
        pltpu.make_async_copy(x_ref, two, sems.at[2]),
    ]
    rest = [pltpu.make_async_copy(tab.at[1:5], tab_v.at[1:5], sems.at[3])]

    def ready(level):
        for copy in (begin, rest, [], [])[level]:
            copy.wait()

    small = pltpu.make_async_copy(interp, interp_v, sems.at[1])
    small.start()
    for copy in begin + rest:
        copy.start()
    small.wait()
    weights(interp_v, w_v, 0, 4)
    levels_kernel(
        nv, 4, 16, first, put, two, (one, two), tab_v, w_v, ready
    )


def levels_hi_kernel(nv, where_ref, x_ref, tab, w, out_ref, one, two, done):
    ncv = 2 * nv

    def first(i):
        return [i], [i + 4]

    def put(slab, q, tile):
        done[pl.ds(slab * 128 * ncv + q, 128, stride=ncv), :] = tile

    levels_kernel(nv, 3, 8, first, put, x_ref, (one, two), tab, w, lambda level: None)

    def gather(e, _):
        slot = (e >> 1 & 7) * 128 + (e >> 4) * 16 + (e & 1) * 8
        for r in range(8):
            row = pl.multiple_of(where_ref[slot + r], ncv)
            out_ref[e, r * ncv : r * ncv + ncv, :] = done[pl.ds(row, ncv), :]
        return 0

    lax.fori_loop(0, 128, gather, 0, unroll=4)


def table_shapes(count, rows):
    shape = jax.ShapeDtypeStruct
    return [shape((rows, 1024, 128), F32), shape((count, 256, 256), BF16)]


def shards(coefficients, angle_in, angle_out, interp, destination):
    nv = 2
    ncv = 2 * nv
    shape = jax.ShapeDtypeStruct
    def pack(kernel, widths):
        return pl.pallas_call(
            kernel,
            out_shape=[shape((96, w), F32) for w in widths],
            in_specs=[HBM, HBM],
            out_specs=[VMEM] * len(widths),
            scratch_shapes=[pltpu.SemaphoreType.DMA((2, 2))],
            compiler_params=params(53),
        )

    far = pack(pack_far_kernel, (768,))(angle_in, angle_out)[0]
    ain, aout, far = lax.optimization_barrier((angle_in, angle_out, far))
    near = pack(pack_near_kernel, (256, 256))(ain, aout)
    from_y = [
        lax.ppermute(s, Y, [(i, i ^ m) for i in range(4)])
        for m, s in zip((1, 2, 3), (near[0], far, near[1]))
    ]

    state = pl.pallas_call(
        functools.partial(send_kernel, nv),
        out_shape=shape((16, 64, ncv * 128), F32),
        in_specs=[VMEM],
        out_specs=VMEM,
        scratch_shapes=[pltpu.VMEM((8, 512, 128), F32)],
        compiler_params=params(6),
    )(coefficients.reshape(512, 1024))
    state, *from_y = lax.optimization_barrier((state, *from_y))
    state = lax.all_to_all(state, FIRST, 0, 0, tiled=True)

    sends = pl.pallas_call(
        pack_x_kernel,
        out_shape=[shape((96, w), F32) for w in (256, 768, 256)],
        in_specs=[HBM, HBM],
        out_specs=[VMEM] * 3,
        scratch_shapes=[pltpu.SemaphoreType.DMA((2, 4))],
        compiler_params=params(BIG),
    )(angle_in, angle_out)
    from_x = [
        lax.ppermute(s, X, [(i, i ^ m) for i in range(4)]) for m, s in zip((1, 2, 3), sends)
    ]
    kept, sent = pl.pallas_call(
        core_kernel,
        out_shape=[shape((96, 1536), F32)] * 2,
        in_specs=[HBM, HBM] + [VMEM] * 3,
        out_specs=[VMEM] * 2,
        scratch_shapes=[pltpu.SemaphoreType.DMA((2, 6))],
        compiler_params=params(BIG),
    )(angle_in, angle_out, *from_y)
    other = lax.ppermute(sent, "c", [(0, 1), (1, 0)])

    tables_lo = pl.pallas_call(
        table_lo_kernel,
        out_shape=shape((PAD, 1024, 128), F32),
        in_specs=[HBM, HBM] + [VMEM] * 2,
        out_specs=ANY,
        scratch_shapes=[
            pltpu.VMEM((4, 1024, 128), F32),
            pltpu.VMEM((1024, 128), F32),
            pltpu.VMEM((96, 1024), F32),
            pltpu.SemaphoreType.DMA((2, 1)),
        ]
        + [pltpu.VMEM((5, 1024, 128), F32), pltpu.SemaphoreType.DMA((5,))],
        compiler_params=params(BIG),
    )(angle_in, angle_out, kept, other)
    tables_lo, *from_x = lax.optimization_barrier((tables_lo, *from_x))
    tables_hi = pl.pallas_call(
        table_hi_kernel,
        out_shape=table_shapes(3, 4),
        in_specs=[HBM, HBM] + [VMEM] * 4,
        out_specs=[ANY, VMEM],
        scratch_shapes=[
            pltpu.VMEM((3, 1024, 128), F32),
            pltpu.VMEM((1024, 128), F32),
            pltpu.VMEM((96, 1792), F32),
            pltpu.SemaphoreType.DMA((2, 3)),
        ]
        + [pltpu.VMEM((4, 1024, 128), F32), pltpu.SemaphoreType.DMA((4,))],
        compiler_params=params(BIG),
    )(angle_in, angle_out, interp, *from_x)

    state = pl.pallas_call(
        functools.partial(levels_lo_kernel, nv),
        out_shape=shape((8, 128, ncv * 128), F32),
        in_specs=[ANY, ANY, ANY],
        out_specs=VMEM,
        scratch_shapes=[pltpu.VMEM((16, 64, ncv * 128), F32)] * 2
        + [
            pltpu.VMEM((5, 1024, 128), F32),
            pltpu.VMEM((4, 256, 256), BF16),
            pltpu.VMEM((7, 32, 64), F32),
            pltpu.SemaphoreType.DMA((4,)),
        ],
        compiler_params=params(BIG),
    )(state, tables_lo, interp)
    wanted = destination[0]
    where = (wanted & 7) * 128 + (wanted >> 3 & 15) * 8 + (wanted >> 7)
    where = where * ncv
    state, where, *tables_hi = lax.optimization_barrier((state, where, *tables_hi))
    state = lax.all_to_all(state, SECOND, 0, 0, tiled=True)

    state = pl.pallas_call(
        functools.partial(levels_hi_kernel, nv),
        out_shape=shape((128, 8 * ncv, 128), F32),
        in_specs=[SMEM] + [VMEM] * 3,
        out_specs=VMEM,
        scratch_shapes=[pltpu.VMEM((8, 128, ncv * 128), F32)] * 2
        + [pltpu.VMEM((1024 * ncv, 128), F32)],
        compiler_params=params(BIG),
    )(where, state, *tables_hi)
    state = lax.all_to_all(state, LAST, 0, 0, tiled=True)

    out = pl.pallas_call(
        functools.partial(final_kernel, nv),
        out_shape=shape((512, 1024), F32),
        in_specs=[VMEM],
        out_specs=ANY,
        scratch_shapes=[pltpu.VMEM((8, 512, 128), F32), pltpu.SemaphoreType.DMA((8,))],
        compiler_params=params(6),
    )(state.reshape(1024 * ncv, 128))
    return out.reshape(2, 32, 8, 1024)


def solution(mesh):
    mesh = jax.sharding.Mesh(mesh.devices.reshape((2,) * 7), AXES)
    placed = (
        P(None, None, None, AXES),
        P(None, None, AXES),
        P(None, None, AXES),
        P(),
        P(AXES, None),
    )
    return jax.shard_map(
        shards,
        mesh=mesh,
        in_specs=placed,
        out_specs=P(None, None, None, AXES),
        check_vma=False,
    )
```

```python
import functools

import jax
import jax.numpy as jnp
from jax import lax
from jax.experimental import pallas as pl
from jax.experimental.pallas import tpu as pltpu
from jax.sharding import PartitionSpec as P

F32 = jnp.float32
BF16 = jnp.bfloat16
VMEM = pl.BlockSpec(memory_space=pltpu.VMEM)
SMEM = pl.BlockSpec(memory_space=pltpu.SMEM)
ANY = pl.BlockSpec(memory_space=pl.ANY)
HBM = pl.BlockSpec(memory_space=pltpu.HBM)
AXES = ("y1", "y0", "zh", "x1", "x0", "zl", "c")
Y = ("y1", "y0")
X = ("x1", "x0")
FIRST = ("zh", "c", "y1", "y0")
SECOND = ("zl", "x0", "x1")
LAST = ("x1", "x0", "zl", "y1", "y0", "zh", "c")
PI = 3.141592653589793
TAU = 6.283185307179586

SIN = (
    0.9999996039252741,
    -0.1666655344642713,
    0.008332407591595805,
    -0.00019808739967677424,
    2.699822692004479e-06,
    -2.036622659870151e-08,
)
COS = (
    0.999999989116818,
    -0.49999989185961996,
    0.04166649020175043,
    -0.0013887807832168462,
    2.476996623505445e-05,
    -2.70797756302502e-07,
    1.724760753325688e-09,
)
MIB = 1024 * 1024
BIG = 30
PAD = 72


def params(mib):
    return pltpu.CompilerParams(vmem_limit_bytes=mib * MIB)


def rev(value, bits):
    out = 0
    for i in range(bits):
        out = out | ((value >> i & 1) << (bits - 1 - i))
    return out


def place(names):
    index = 0
    for name in names:
        index = index * 2 + lax.axis_index(name)
    return index


def horner(coefs, u):
    acc = jnp.full_like(u, coefs[-1])
    for c in reversed(coefs[:-1]):
        acc = acc * u + c
    return acc


def sincos(x):
    u = x * x
    return x * horner(SIN, u), horner(COS, u)


def dot(a, b, dims=((1,), (0,))):
    return lax.dot_general(a, b, (dims, ((), ())), preferred_element_type=F32)


def split(x):
    hi = x.astype(BF16)
    return hi, (x - hi.astype(F32)).astype(BF16)


def send_kernel(nv, x_ref, out_ref, columns):
    for kt in range(8):
        columns[kt] = x_ref[:, kt * 128 : kt * 128 + 128]
        for c in range(2):
            for v in range(nv):
                part = columns[kt, pl.ds(c * 256 + v, 128, stride=2), :].T
                lanes = slice((c * nv + v) * 128, (c * nv + v) * 128 + 128)
                for core in range(2):
                    owner = (kt >> 2) * 8 + core * 4 + rev(kt & 3, 2)
                    out_ref[owner, :, lanes] = part[core * 64 : core * 64 + 64]


def final_kernel(nv, x_ref, out_ref, columns, sems):
    ncv = 2 * nv

    def leave(kt):
        lanes = slice(kt * 128, kt * 128 + 128)
        return pltpu.make_async_copy(columns.at[kt], out_ref.at[:, lanes], sems.at[kt])

    for kt in range(8):
        for c in range(2):
            for v in range(nv):
                cv = c * nv + v
                part = jnp.concatenate(
                    [
                        x_ref[pl.ds((xz * 16 + kt * 2) * 8 * ncv + cv, 16, stride=ncv), :]
                        for xz in range(8)
                    ],
                    axis=0,
                )
                columns[kt, pl.ds(c * 256 + v, 128, stride=2), :] = part.T
        leave(kt).start()
    for kt in range(8):
        leave(kt).wait()


def fetch(jobs, sems):
    copies = []
    for i, (ain, aout, level, start, width, dst, at) in enumerate(jobs):
        cols = pl.ds(pl.multiple_of(start, 128), width)
        copies.append(
            pltpu.make_async_copy(
                ain.at[level, :, cols], dst.at[0:64, at : at + width], sems.at[0, i]
            )
        )
        copies.append(
            pltpu.make_async_copy(
                aout.at[level, :, cols], dst.at[64:96, at : at + width], sems.at[1, i]
            )
        )
    for copy in copies:
        copy.start()
    for copy in copies:
        copy.wait()


def pack_far_kernel(ain, aout, y2, sems):
    y = place(Y)
    jobs = [
        (ain, aout, 1, ((y >> 1) ^ 1) * 512, 512, y2, 256),
        (ain, aout, 0, (rev(y, 2) ^ rev(2, 2)) * 256, 256, y2, 0),
    ]
    fetch(jobs, sems)


def pack_near_kernel(ain, aout, y1, y3, sems):
    ry = rev(place(Y), 2)
    jobs = [
        (ain, aout, 0, (ry ^ rev(m, 2)) * 256, 256, dst, 0) for m, dst in ((1, y1), (3, y3))
    ]
    fetch(jobs, sems)


def pack_x_kernel(ain, aout, x1, x2, x3, sems):
    x = place(X)
    rx = rev(x, 2)
    jobs = [(ain, aout, 5, ((x >> 1) ^ 1) * 512, 512, x2, 256)]
    for m, dst in ((2, x2), (1, x1), (3, x3)):
        jobs.append((ain, aout, 4, (rx ^ rev(m, 2)) * 256, 256, dst, 0))
    fetch(jobs, sems)


def core_kernel(ain, aout, y1, y2, y3, kept, sent, sems):
    y = place(Y)
    core = lax.axis_index("c")
    ry = rev(y, 2)
    jobs = []
    for dst, side in ((kept, core), (sent, 1 - core)):
        jobs.append((ain, aout, 0, ry * 256 + side * 128, 128, dst, 0))
        jobs.append((ain, aout, 1, (y >> 1) * 512 + side * 256, 256, dst, 512))
        jobs.append((ain, aout, 2, side * 512, 512, dst, 1024))
    fetch(jobs, sems)
    for dst, side in ((kept, core), (sent, 1 - core)):
        for m, src in ((1, y1), (2, y2), (3, y3)):
            cols = pl.ds(pl.multiple_of(side * 128, 128), 128)
            dst[:, m * 128 : m * 128 + 128] = src[:, cols]
        cols = pl.ds(pl.multiple_of(256 + side * 256, 128), 256)
        dst[:, 768:1024] = y2[:, cols]


def turned(read, scratch, width):
    for t in range(width // 128):
        part = read(slice(t * 128, t * 128 + 128))
        full = jnp.concatenate([part, jnp.zeros((32, 128), F32)], axis=0)
        scratch[t * 128 : t * 128 + 128, :] = full.T


def got(ref, at):
    return lambda s: ref[:, at + s.start : at + s.stop]


def weights(interp_ref, w_ref, first, count):
    row = lax.broadcasted_iota(jnp.int32, (256, 64), 0)
    col = lax.broadcasted_iota(jnp.int32, (256, 64), 1)
    left = ((row >> 2) == col).astype(F32).astype(BF16)
    row = lax.broadcasted_iota(jnp.int32, (32, 128), 0)
    col = lax.broadcasted_iota(jnp.int32, (32, 128), 1)
    right = (row == (col >> 2)).astype(F32).astype(BF16)
    row = lax.broadcasted_iota(jnp.int32, (256, 128), 0)
    col = lax.broadcasted_iota(jnp.int32, (256, 128), 1)
    keep = (row & 3) == (col & 3)
    for level in range(count):
        for i, part in enumerate(split(interp_ref[first + level])):
            mid = dot(left, part, ((1,), (1,))).astype(BF16)
            full = jnp.where(keep, dot(mid, right), 0.0)
            w_ref[level, :, i * 128 : i * 128 + 128] = full.astype(BF16)


def tables(count, slabs, raw, tab_ref, tab_v, sems):
    rows = 1024 // slabs
    lane = lax.broadcasted_iota(jnp.int32, (rows, 128), 1)

    def leave(level):
        return pltpu.make_async_copy(tab_v.at[level], tab_ref.at[level], sems.at[level])

    for level in range(count):

        def body(m, _):
            low = pl.ds(pl.multiple_of(m * rows, rows), rows)
            high = pl.ds(pl.multiple_of((m + slabs // 2) * rows, rows), rows)
            if level:
                before = jnp.where(
                    lane < 32,
                    pltpu.roll(raw[level - 1, low, :], 64, 1),
                    pltpu.roll(raw[level - 1, high, :], 96, 1),
                )
                before = jnp.where(lane < 64, before, 0.0)
            for t in range(2):
                at = pl.ds(pl.multiple_of((2 * m + t) * rows, rows), rows)
                angle = raw[level, at, :]
                if level:
                    angle = angle + before
                    turn = jnp.where(angle > PI, TAU, jnp.where(angle < -PI, -TAU, 0.0))
                    angle = angle - turn
                s, c = sincos(angle)
                tab_v[level, at, :] = jnp.where(lane < 64, c, pltpu.roll(s, 64, 1))
                if level == count - 1:
                    out = jnp.where(lane < 32, pltpu.roll(c, 64, 1), pltpu.roll(s, 96, 1))
                    tab_v[count, at, :] = out
            return 0

        lax.fori_loop(0, slabs // 2, body, 0, unroll=2)
        leave(level).start()
    leave(count).start()
    for level in range(count + 1):
        leave(level).wait()


def table_lo_kernel(
    ain, aout, kept, other, tab_ref, raw, scratch, mine, sems,
    tab_v, out_sems,
):
    y = place(Y)
    core = lax.axis_index("c")
    ry = rev(y, 2)
    fetch([(ain, aout, 3, 0, 1024, mine, 0)], sems)

    def emit(level, base, ts):
        for t in range(ts):
            at = pl.multiple_of((base + t) * 64, 64)
            raw[level, pl.ds(at, 64), :] = scratch[pl.ds(t, 64, stride=ts), :]

    for src, side in ((kept, core), (other, 1 - core)):
        for m in range(4):
            turned(got(src, m * 128), scratch, 128)
            emit(0, ((ry ^ rev(m, 2)) * 2 + side) * 2, 2)
        for m in range(2):
            turned(got(src, 512 + m * 256), scratch, 256)
            emit(1, (((y >> 1) ^ m) * 2 + side) * 4, 4)
        turned(got(src, 1024), scratch, 512)
        emit(2, side * 8, 8)
    turned(got(mine, 0), scratch, 1024)
    emit(3, 0, 16)
    tables(4, 16, raw, tab_ref, tab_v, out_sems)


def table_hi_kernel(
    ain, aout, interp, x1, x2, x3, tab_ref, w_ref, raw, scratch, mine, sems,
    tab_v, out_sems,
):
    x = place(X)
    rx = rev(x, 2)
    fetch(
        [
            (ain, aout, 4, rx * 256, 256, mine, 0),
            (ain, aout, 5, (x >> 1) * 512, 512, mine, 256),
            (ain, aout, 6, 0, 1024, mine, 768),
        ],
        sems,
    )
    weights(interp, w_ref, 4, 3)

    def emit(level, base, ts):
        for t in range(ts):
            for T in range(16):
                at = pl.multiple_of((base + t) * 128 + T * 8, 8)
                raw[level, pl.ds(at, 8), :] = scratch[pl.ds(T * ts + t, 8, stride=16 * ts), :]

    for m, src in enumerate((None, x1, x2, x3)):
        read = got(mine, 0) if m == 0 else got(src, 0)
        turned(read, scratch, 256)
        emit(0, (rx ^ rev(m, 2)) * 2, 2)
    turned(got(mine, 256), scratch, 512)
    emit(1, (x >> 1) * 4, 4)
    turned(got(x2, 256), scratch, 512)
    emit(1, (1 - (x >> 1)) * 4, 4)
    turned(got(mine, 768), scratch, 1024)
    emit(2, 0, 8)
    tables(3, 8, raw, tab_ref, tab_v, out_sems)


def spread(table, first):
    lane = lax.broadcasted_iota(jnp.int32, table.shape, 1)
    return jnp.take_along_axis(table, first + (lane >> 2), axis=1)


def step(nv, low, high, table, w, after):
    n = table.shape[0]
    sides = []
    for kind, src in enumerate((low, high)):
        c = spread(table, kind * 32)
        s = spread(table, kind * 32 + 64)
        re, im = [], []
        for v in range(nv):
            xr = src(v)
            xi = src(nv + v)
            re.append(xr * c - xi * s)
            im.append(xr * s + xi * c)
        sides.append(jnp.concatenate(re + im, axis=0))
    hi, lo = split(jnp.concatenate(sides, axis=1))
    first = dot(hi, w)
    out = first[:, :128] + first[:, 128:] + dot(lo, w[:, :128])
    out = [out[q * n : q * n + n] for q in range(2 * nv)]
    if after is None:
        return out
    c = spread(after, 0)
    s = spread(after, 32)
    re = [out[v] * c - out[nv + v] * s for v in range(nv)]
    im = [out[v] * s + out[nv + v] * c for v in range(nv)]
    return re + im


def levels_kernel(nv, count, slabs, first, put, x_ref, bufs, tab_ref, w_ref, ready):
    rows = 1024 // slabs
    group = 128 // rows
    lanes = lambda q: slice(q * 128, q * 128 + 128)
    for level in range(count):
        ready(level)
        last = level == count - 1
        src = bufs[(level + 1) % 2] if level else x_ref
        dst = bufs[level % 2]
        w = w_ref[level]
        for i in range(slabs // 2 // group):
            if level == 0:
                lows, highs = first(i)
            else:
                lows = [i * group + g for g in range(group)]
                highs = [m + slabs // 2 for m in lows]
            low = lambda q: jnp.concatenate([src[m, :, lanes(q)] for m in lows], axis=0)
            high = lambda q: jnp.concatenate([src[m, :, lanes(q)] for m in highs], axis=0)
            for t in range(2):
                outs = [2 * (i * group + g) + t for g in range(group)]
                at = [slice(m * rows, m * rows + rows) for m in outs]
                read = lambda k: jnp.concatenate([tab_ref[k, r, :] for r in at], axis=0)
                after = read(count) if last else None
                for q, tile in enumerate(step(nv, low, high, read(level), w, after)):
                    for g, m in enumerate(outs):
                        part = tile[g * rows : g * rows + rows]
                        if last:
                            put(m, q, part)
                        else:
                            dst[m, :, lanes(q)] = part


def levels_lo_kernel(nv, x_ref, tab, interp, out_ref, one, two, tab_v, w_v, interp_v, sems):
    def first(i):
        a = rev(i, 2)
        return [a, a + 4], [a + 8, a + 12]

    def put(slab, q, tile):
        for kp in range(8):
            rows = slice(slab * 8, slab * 8 + 8)
            out_ref[kp, rows, q * 128 : q * 128 + 128] = tile[kp * 8 : kp * 8 + 8]

    begin = [
        pltpu.make_async_copy(tab.at[0], tab_v.at[0], sems.at[0]),
        pltpu.make_async_copy(x_ref, two, sems.at[2]),
    ]
    rest = [pltpu.make_async_copy(tab.at[1:5], tab_v.at[1:5], sems.at[3])]

    def ready(level):
        for copy in (begin, rest, [], [])[level]:
            copy.wait()

    small = pltpu.make_async_copy(interp, interp_v, sems.at[1])
    small.start()
    for copy in begin + rest:
        copy.start()
    small.wait()
    weights(interp_v, w_v, 0, 4)
    levels_kernel(
        nv, 4, 16, first, put, two, (one, two), tab_v, w_v, ready
    )


def levels_hi_kernel(nv, where_ref, x_ref, tab, w, out_ref, one, two, done):
    ncv = 2 * nv

    def first(i):
        return [i], [i + 4]

    def put(slab, q, tile):
        done[pl.ds(slab * 128 * ncv + q, 128, stride=ncv), :] = tile

    levels_kernel(nv, 3, 8, first, put, x_ref, (one, two), tab, w, lambda level: None)

    def gather(e, _):
        slot = (e >> 1 & 7) * 128 + (e >> 4) * 16 + (e & 1) * 8
        for r in range(8):
            row = pl.multiple_of(where_ref[slot + r], ncv)
            out_ref[e, r * ncv : r * ncv + ncv, :] = done[pl.ds(row, ncv), :]
        return 0

    lax.fori_loop(0, 128, gather, 0, unroll=8)


def table_shapes(count, rows):
    shape = jax.ShapeDtypeStruct
    return [shape((rows, 1024, 128), F32), shape((count, 256, 256), BF16)]


def shards(coefficients, angle_in, angle_out, interp, destination):
    nv = 2
    ncv = 2 * nv
    shape = jax.ShapeDtypeStruct
    def pack(kernel, widths):
        return pl.pallas_call(
            kernel,
            out_shape=[shape((96, w), F32) for w in widths],
            in_specs=[HBM, HBM],
            out_specs=[VMEM] * len(widths),
            scratch_shapes=[pltpu.SemaphoreType.DMA((2, 2))],
            compiler_params=params(53),
        )

    far = pack(pack_far_kernel, (768,))(angle_in, angle_out)[0]
    ain, aout, far = lax.optimization_barrier((angle_in, angle_out, far))
    near = pack(pack_near_kernel, (256, 256))(ain, aout)
    from_y = [
        lax.ppermute(s, Y, [(i, i ^ m) for i in range(4)])
        for m, s in zip((1, 2, 3), (near[0], far, near[1]))
    ]

    state = pl.pallas_call(
        functools.partial(send_kernel, nv),
        out_shape=shape((16, 64, ncv * 128), F32),
        in_specs=[VMEM],
        out_specs=VMEM,
        scratch_shapes=[pltpu.VMEM((8, 512, 128), F32)],
        compiler_params=params(6),
    )(coefficients.reshape(512, 1024))
    state, *from_y = lax.optimization_barrier((state, *from_y))
    state = lax.all_to_all(state, FIRST, 0, 0, tiled=True)

    sends = pl.pallas_call(
        pack_x_kernel,
        out_shape=[shape((96, w), F32) for w in (256, 768, 256)],
        in_specs=[HBM, HBM],
        out_specs=[VMEM] * 3,
        scratch_shapes=[pltpu.SemaphoreType.DMA((2, 4))],
        compiler_params=params(BIG),
    )(angle_in, angle_out)
    from_x = [
        lax.ppermute(s, X, [(i, i ^ m) for i in range(4)]) for m, s in zip((1, 2, 3), sends)
    ]
    kept, sent = pl.pallas_call(
        core_kernel,
        out_shape=[shape((96, 1536), F32)] * 2,
        in_specs=[HBM, HBM] + [VMEM] * 3,
        out_specs=[VMEM] * 2,
        scratch_shapes=[pltpu.SemaphoreType.DMA((2, 6))],
        compiler_params=params(BIG),
    )(angle_in, angle_out, *from_y)
    other = lax.ppermute(sent, "c", [(0, 1), (1, 0)])

    tables_lo = pl.pallas_call(
        table_lo_kernel,
        out_shape=shape((PAD, 1024, 128), F32),
        in_specs=[HBM, HBM] + [VMEM] * 2,
        out_specs=ANY,
        scratch_shapes=[
            pltpu.VMEM((4, 1024, 128), F32),
            pltpu.VMEM((1024, 128), F32),
            pltpu.VMEM((96, 1024), F32),
            pltpu.SemaphoreType.DMA((2, 1)),
        ]
        + [pltpu.VMEM((5, 1024, 128), F32), pltpu.SemaphoreType.DMA((5,))],
        compiler_params=params(BIG),
    )(angle_in, angle_out, kept, other)
    tables_lo, *from_x = lax.optimization_barrier((tables_lo, *from_x))
    tables_hi = pl.pallas_call(
        table_hi_kernel,
        out_shape=table_shapes(3, 4),
        in_specs=[HBM, HBM] + [VMEM] * 4,
        out_specs=[ANY, VMEM],
        scratch_shapes=[
            pltpu.VMEM((3, 1024, 128), F32),
            pltpu.VMEM((1024, 128), F32),
            pltpu.VMEM((96, 1792), F32),
            pltpu.SemaphoreType.DMA((2, 3)),
        ]
        + [pltpu.VMEM((4, 1024, 128), F32), pltpu.SemaphoreType.DMA((4,))],
        compiler_params=params(BIG),
    )(angle_in, angle_out, interp, *from_x)

    state = pl.pallas_call(
        functools.partial(levels_lo_kernel, nv),
        out_shape=shape((8, 128, ncv * 128), F32),
        in_specs=[ANY, ANY, ANY],
        out_specs=VMEM,
        scratch_shapes=[pltpu.VMEM((16, 64, ncv * 128), F32)] * 2
        + [
            pltpu.VMEM((5, 1024, 128), F32),
            pltpu.VMEM((4, 256, 256), BF16),
            pltpu.VMEM((7, 32, 64), F32),
            pltpu.SemaphoreType.DMA((4,)),
        ],
        compiler_params=params(BIG),
    )(state, tables_lo, interp)
    wanted = destination[0]
    where = (wanted & 7) * 128 + (wanted >> 3 & 15) * 8 + (wanted >> 7)
    where = where * ncv
    state, where, *tables_hi = lax.optimization_barrier((state, where, *tables_hi))
    state = lax.all_to_all(state, SECOND, 0, 0, tiled=True)

    state = pl.pallas_call(
        functools.partial(levels_hi_kernel, nv),
        out_shape=shape((128, 8 * ncv, 128), F32),
        in_specs=[SMEM] + [VMEM] * 3,
        out_specs=VMEM,
        scratch_shapes=[pltpu.VMEM((8, 128, ncv * 128), F32)] * 2
        + [pltpu.VMEM((1024 * ncv, 128), F32)],
        compiler_params=params(BIG),
    )(where, state, *tables_hi)
    state = lax.all_to_all(state, LAST, 0, 0, tiled=True)

    out = pl.pallas_call(
        functools.partial(final_kernel, nv),
        out_shape=shape((512, 1024), F32),
        in_specs=[VMEM],
        out_specs=ANY,
        scratch_shapes=[pltpu.VMEM((8, 512, 128), F32), pltpu.SemaphoreType.DMA((8,))],
        compiler_params=params(6),
    )(state.reshape(1024 * ncv, 128))
    return out.reshape(2, 32, 8, 1024)


def solution(mesh):
    mesh = jax.sharding.Mesh(mesh.devices.reshape((2,) * 7), AXES)
    placed = (
        P(None, None, None, AXES),
        P(None, None, AXES),
        P(None, None, AXES),
        P(),
        P(AXES, None),
    )
    return jax.shard_map(
        shards,
        mesh=mesh,
        in_specs=placed,
        out_specs=P(None, None, None, AXES),
        check_vma=False,
    )
```
